128 devices in a mesh: dp: 16 (over y_hi, z, core), tensor: 8 (over x, y_lo).
Axes of the slice: x: 4, y: 4 (y_hi: 2, y_lo: 2; y = y_hi * 2 + y_lo), z: 4, core: 2. Of those that a mesh axis runs over, the one named last changes fastest.
Arguments:
- inputs: bfloat16 [16384, 1024], P(('dp', 'tensor')), may hold values from -6 to 6
- first_gain: bfloat16 [1024], P('dp'), may hold values from 0.5 to 1.5
- query_weight: bfloat16 [1024, 1024], P('dp', 'tensor'), may hold values from -0.65625 to 0.65625
- key_matrix: bfloat16 [1024, 512], P('dp', 'tensor'), may hold values from -0.65625 to 0.65625
- value_matrix: bfloat16 [1024, 512], P('dp', 'tensor'), may hold values from -0.1875 to 0.1875
- output_weight: bfloat16 [1024, 1024], P('tensor', 'dp'), may hold values from -3 to 3
- second_gain: bfloat16 [1024], P('dp'), may hold values from 0.5 to 1.5
- gate_weight: bfloat16 [32, 1024, 512], P('tensor', 'dp'), may hold values from -0.1875 to 0.1875
- up_weight: bfloat16 [32, 1024, 512], P('tensor', 'dp'), may hold values from -0.1875 to 0.1875
- down_weight: bfloat16 [32, 512, 1024], P('tensor', None, 'dp'), may hold values from -4.78125 to 4.78125
- expert_ids: int32 [16384, 8], P('dp'), may hold values from 0 to 31, all different within a row; in each aligned block of 1024 rows (0 to 1023, 1024 to 2047, ...) at most 512 rows name the same one
- gate_values: float32 [16384, 8], P('dp'), may hold values from 0.05 to 0.25
- out_grad: bfloat16 [16384, 1024], P(('dp', 'tensor')), may hold values from -6 to 6
Outputs:
- block_output: bfloat16 [16384, 1024], P(('dp', 'tensor'))
- input_grad: bfloat16 [16384, 1024], P(('dp', 'tensor'))
- first_gain_grad: float32 [1024], P('dp')
- query_weight_grad: float32 [1024, 1024], P('dp', 'tensor')
- key_weight_grad: float32 [1024, 512], P('dp', 'tensor')
- value_weight_grad: float32 [1024, 512], P('dp', 'tensor')
- output_weight_grad: float32 [1024, 1024], P('tensor', 'dp')
- second_gain_grad: float32 [1024], P('dp')
- gate_weight_grad: float32 [32, 1024, 512], P('tensor', 'dp')
- up_weight_grad: float32 [32, 1024, 512], P('tensor', 'dp')
- down_weight_grad: float32 [32, 512, 1024], P('tensor', None, 'dp')
The draws below stay inside these ranges and needn't reach their ends.
Inputs may be any that keep to these rules, and one draw needn't show every extreme that they name: `expert_ids`: each row names 8 different experts. Within the rows of one sequence no expert is named more than 512 times, and in some sequence some expert is named exactly 512 times.
All inputs are finite; a program needn't handle non-finite values.
Results may differ from the reference program's by a relative error of at most 0.03.
Values may be sent and summed in bfloat16 or wider, within the bound.
A program may use at most 192 MiB of HBM per device.

```python
import math
import jax
import jax.numpy as jnp
import numpy as np
from jax import lax

MODEL_WIDTH = 1024
QUERY_HEADS = 16
KEY_VALUE_HEADS = 8
HEAD_SIZE = 64
E = 32
F = 512
TOPK = 8
SEQ_LEN = 1024
CAP = 512
TOKENS = 16384
N_DP = 16


def block_scale(stream_key, shape, split, low, top_value):
    level, own = 1.0, jax.random.fold_in(stream_key, 6)
    for dim, shards_of in split:
        steps = jnp.exp(jax.random.uniform(jax.random.fold_in(own, dim), (shards_of,), jnp.float32, low / len(split), top_value / len(split)))
        level = level * jnp.repeat(steps, shape[dim] // shards_of).reshape([-1 if axis == dim else 1 for axis in range(len(shape))])
    return level


def shared_out(rng, own, number, rows, count, top, limit, slope):
    order = jax.random.permutation(rng, count)
    heavy_load, common = load_shares(count, rows * top, limit, slope, True), load_shares(count, rows * top, limit, slope, False)
    places = jnp.arange(count)

    def named(lengths, rotation):
        used = int((lengths > 0).sum())
        fixed = max(1, used // 4)
        moved = fixed + (places - fixed + rotation * (used - fixed)) % max(1, count - fixed)
        return jnp.zeros((count,), jnp.int32).at[order[jnp.where(places < fixed, places, moved)]].set(jnp.asarray(lengths, jnp.int32))

    lengths = jnp.where(number % 4 == 0, named(heavy_load, number // 4), named(common, number - number // 4 - 1))
    mixed = jax.random.permutation(jax.random.fold_in(own, 3), count)
    source_of, taker = mixed[0:count // 2 * 2:2], mixed[1:count // 2 * 2:2]
    margin = jnp.minimum(lengths[source_of] - 1, limit - lengths[taker]) // 2
    margin = jnp.where((source_of == order[0]) | (taker == order[0]) | (lengths[taker] == 0), 0, jnp.maximum(margin, 0))
    moved = jax.random.randint(jax.random.fold_in(own, 4), (count // 2,), 0, 1 << 20) % (margin + 1)
    lengths = lengths.at[source_of].add(-moved).at[taker].add(moved)
    members = jnp.searchsorted(jnp.cumsum(lengths), jnp.arange(rows * top), side="right").astype(jnp.int32)
    grid = members.reshape(top, rows).T
    grid = grid[jax.random.permutation(jax.random.fold_in(own, 1), rows)]
    rotation = jax.random.randint(jax.random.fold_in(own, 2), (rows, 1), 0, top)
    return jnp.take_along_axis(grid, (jnp.arange(top)[None, :] + rotation) % top, axis=1)


def load_shares(amount, total, most, skew, full):
    portions = [(1 << 20) // math.isqrt(rank ** skew) + 1 for rank in range(1, amount + 1)]
    largest = most if full else min(most, max(-(-total // amount), total * portions[0] // sum(portions)))
    least = 1 if total - largest >= amount - 1 else 0
    holding, rest = [largest] + [least] * (amount - 1), total - largest - least * (amount - 1)
    while rest > 0:
        movable = [i for i in range(1, amount) if holding[i] < largest] or [i for i in range(1, amount) if holding[i] < most]
        whole, remaining = sum([portions[i] for i in movable]), rest
        for i in movable:
            addition = min(most - holding[i], max(1, remaining * portions[i] // whole), rest)
            holding[i] = holding[i] + addition
            rest = rest - addition
    return np.array(holding)


def bell_draw(rng, extent, spread, bound, split=(), held_as=jnp.bfloat16):
    loudness = block_scale(rng, extent, split, -0.22, 0.18) if split else 1.0
    drawn = jax.random.normal(rng, extent, jnp.float32) * spread * loudness
    return jnp.minimum(jnp.maximum(drawn, -bound), bound).astype(held_as)


def setup_inputs(seed: int = 0) -> dict:
    streams_of = jax.random.split(jax.random.key(seed), 14)
    inputs = bell_draw(streams_of[0], (TOKENS, MODEL_WIDTH), 1.0, 6.0, ((0, 128),))
    first_gain = jnp.clip(1.0 + 0.1 * jax.random.normal(streams_of[1], (MODEL_WIDTH,), jnp.float32), 0.5, 1.5).astype(jnp.bfloat16)
    query_weight = bell_draw(streams_of[2], (MODEL_WIDTH, QUERY_HEADS * HEAD_SIZE), 0.11, 0.65625, ((0, 16), (1, 8)))
    key_matrix = bell_draw(streams_of[3], (MODEL_WIDTH, KEY_VALUE_HEADS * HEAD_SIZE), 0.11, 0.65625, ((0, 16), (1, 8)))
    value_matrix = bell_draw(streams_of[4], (MODEL_WIDTH, KEY_VALUE_HEADS * HEAD_SIZE), MODEL_WIDTH ** -0.5, 0.1875, ((0, 16), (1, 8)))
    output_weight = bell_draw(streams_of[5], (QUERY_HEADS * HEAD_SIZE, MODEL_WIDTH), 0.5, 3.0, ((0, 8), (1, 16)))
    second_gain = jnp.clip(1.0 + 0.1 * jax.random.normal(streams_of[6], (MODEL_WIDTH,), jnp.float32), 0.5, 1.5).astype(jnp.bfloat16)
    gate_weight = bell_draw(streams_of[7], (E, MODEL_WIDTH, F), MODEL_WIDTH ** -0.5, 0.1875, ((0, 8), (1, 16)))
    up_weight = bell_draw(streams_of[8], (E, MODEL_WIDTH, F), MODEL_WIDTH ** -0.5, 0.1875, ((0, 8), (1, 16)))
    down_weight = bell_draw(streams_of[9], (E, F, MODEL_WIDTH), 0.8, 4.78125, ((0, 8), (2, 16)))
    expert_ids_keys = jax.random.split(jax.random.fold_in(streams_of[10], 1), TOKENS // SEQ_LEN)
    expert_ids_turns = jax.random.permutation(jax.random.fold_in(streams_of[10], 3), TOKENS // SEQ_LEN)
    expert_ids = jax.vmap(lambda own, number: shared_out(jax.random.fold_in(streams_of[10], 2), own, number, SEQ_LEN, E, TOPK, CAP, 2))(expert_ids_keys, expert_ids_turns).reshape((TOKENS, TOPK))
    gate_values = jnp.clip(jnp.exp(math.log(0.25) - 1.609438 * jax.random.uniform(streams_of[11], (TOKENS, TOPK), jnp.float32) ** block_scale(streams_of[11], (TOKENS, TOPK), ((0, 16),), -0.2, 0.2)), 0.05, 0.25)
    out_grad = bell_draw(streams_of[12], (TOKENS, MODEL_WIDTH), 1.0, 6.0, ((0, 128),))
    return dict(inputs=inputs, first_gain=first_gain, query_weight=query_weight, key_matrix=key_matrix, value_matrix=value_matrix, output_weight=output_weight, second_gain=second_gain, gate_weight=gate_weight, up_weight=up_weight, down_weight=down_weight, expert_ids=expert_ids, gate_values=gate_values, out_grad=out_grad)


NORM_EPSILON = 1e-06
ATT_SCALE = 0.015625
RES_SCALE = 0.22
ROPE_BASE = 10000.0
NEG_FILL = -1e+30
HIGHEST_PRECISION = lax.Precision.HIGHEST

@jax.custom_vjp
def reduced_precision(v):
    return lax.optimization_barrier(v.astype(jnp.bfloat16)).astype(jnp.float32)

@jax.custom_vjp
def reduced_backward(v):
    return v

def low_keep(v):
    return (reduced_precision(v), None)

def low_pass(kept, grad):
    return (grad,)

def back_keep(v):
    return (v, None)

def back_low(kept, grad):
    return (reduced_precision(grad),)
reduced_precision.defvjp(low_keep, low_pass)
reduced_backward.defvjp(back_keep, back_low)

def matrix_product(left_side, right_side):
    return jnp.dot(left_side, right_side, precision=HIGHEST_PRECISION, preferred_element_type=jnp.float32)

def rms_normed(activations, gain_vector):
    return activations * lax.rsqrt(lax.optimization_barrier(jnp.mean(activations * activations, axis=-1, keepdims=True)) + NORM_EPSILON) * gain_vector

def rotary_tables(length):
    half_width = HEAD_SIZE // 2
    positions = jnp.arange(length).astype(jnp.float32)
    frequencies = jnp.power(ROPE_BASE, -(jnp.arange(half_width).astype(jnp.float32) * 2.0 / HEAD_SIZE))
    angles = positions[:, None] * frequencies[None, :]
    return (jnp.cos(angles)[:, None, :], jnp.sin(angles)[:, None, :])

def apply_rotary(head_data, cosine_lookup, sine_lookup):
    half_width = head_data.shape[-1] // 2
    first_half = head_data[..., :half_width]
    second_half = head_data[..., half_width:]
    return jnp.concatenate([first_half * cosine_lookup - second_half * sine_lookup, second_half * cosine_lookup + first_half * sine_lookup], axis=-1)

def attention(query_rows, key_head_rows, value_head_rows):
    sequence_rows = query_rows.shape[0]
    group_width = QUERY_HEADS // KEY_VALUE_HEADS
    block_rows = min(512, sequence_rows)
    grouped_query = query_rows.reshape(sequence_rows, KEY_VALUE_HEADS, group_width, HEAD_SIZE)
    key_index = jnp.arange(sequence_rows).astype(jnp.int32)

    def one_block(first_row):
        query_block = lax.dynamic_slice_in_dim(grouped_query, first_row, block_rows, 0)
        scores = jnp.einsum('qhgd,khd->hgqk', query_block, key_head_rows, precision=HIGHEST_PRECISION) * ATT_SCALE
        scores = reduced_backward(scores)
        causal_mask = (first_row + jnp.arange(block_rows).astype(jnp.int32))[:, None] >= key_index[None, :]
        scores = jnp.where(causal_mask, scores, NEG_FILL)
        probs_low = reduced_precision(jax.nn.softmax(scores, axis=-1))
        return jnp.einsum('hgqk,khd->qhgd', probs_low, value_head_rows, precision=HIGHEST_PRECISION)
    starts = jnp.arange(0, sequence_rows, block_rows).astype(jnp.int32)
    blocks = lax.map(jax.checkpoint(one_block), starts)
    return blocks.reshape(sequence_rows, QUERY_HEADS * HEAD_SIZE)

def experts(normed_two, gate_weight, up_weight, down_weight, expert_ids, gate_values):
    sequence_rows = normed_two.shape[0]

    def one_expert(expert_number, gate_slab, up_slab, down_slab):
        matched = expert_ids == expert_number
        is_used = jnp.any(matched, axis=-1)
        combined = lax.optimization_barrier(jnp.sum(jnp.where(matched, gate_values, 0.0), axis=-1))
        slot_index = jnp.cumsum(is_used.astype(jnp.int32)) - 1
        target = jnp.where(is_used, slot_index, CAP).astype(jnp.int32)
        token_of = jnp.zeros((CAP,), jnp.int32).at[target].set(jnp.arange(sequence_rows).astype(jnp.int32), mode='drop')
        filled = jnp.arange(CAP).astype(jnp.int32) < jnp.sum(is_used.astype(jnp.int32))
        expert_rows = normed_two[token_of]
        gate_part = reduced_backward(matrix_product(expert_rows, gate_slab))
        up_part = reduced_backward(matrix_product(expert_rows, up_slab))
        hidden_units = reduced_precision(jax.nn.silu(gate_part) * up_part)
        expert_out = reduced_backward(matrix_product(hidden_units, down_slab))
        row_scale = jnp.where(filled, combined[token_of], 0.0)
        return (token_of, row_scale[:, None] * expert_out)
    token_of, weighted = jax.vmap(one_expert)(jnp.arange(E).astype(jnp.int32), gate_weight, up_weight, down_weight)
    return jnp.zeros_like(normed_two).at[token_of.reshape(-1)].add(weighted.reshape(-1, MODEL_WIDTH))

def layer(inputs, first_gain, query_weight, key_matrix, value_matrix, output_weight, second_gain, gate_weight, up_weight, down_weight, expert_ids, gate_values):
    sequence_rows = inputs.shape[0]
    cosine_lookup, sine_lookup = rotary_tables(sequence_rows)
    normalized_rows = reduced_precision(rms_normed(inputs, first_gain))
    query_rows = reduced_precision(apply_rotary(reduced_backward(matrix_product(normalized_rows, query_weight)).reshape(sequence_rows, QUERY_HEADS, HEAD_SIZE), cosine_lookup, sine_lookup))
    key_head_rows = reduced_precision(apply_rotary(reduced_backward(matrix_product(normalized_rows, key_matrix)).reshape(sequence_rows, KEY_VALUE_HEADS, HEAD_SIZE), cosine_lookup, sine_lookup))
    value_head_rows = reduced_precision(reduced_backward(matrix_product(normalized_rows, value_matrix))).reshape(sequence_rows, KEY_VALUE_HEADS, HEAD_SIZE)
    attended = reduced_precision(reduced_backward(attention(query_rows, key_head_rows, value_head_rows)))
    hidden_state = inputs + RES_SCALE * reduced_backward(matrix_product(attended, output_weight))
    normed_two = reduced_precision(rms_normed(hidden_state, second_gain))
    mixture = experts(normed_two, gate_weight, up_weight, down_weight, expert_ids, gate_values)
    return hidden_state + RES_SCALE * mixture

def reference(inputs, first_gain, query_weight, key_matrix, value_matrix, output_weight, second_gain, gate_weight, up_weight, down_weight, expert_ids, gate_values, out_grad):
    params = tuple((weight_array.astype(jnp.float32) for weight_array in (first_gain, query_weight, key_matrix, value_matrix, output_weight, second_gain, gate_weight, up_weight, down_weight)))
    seq_inputs = inputs.astype(jnp.float32).reshape(N_DP, SEQ_LEN, MODEL_WIDTH)
    seq_grads = out_grad.astype(jnp.float32).reshape(N_DP, SEQ_LEN, MODEL_WIDTH)
    seq_ids = expert_ids.reshape(N_DP, SEQ_LEN, TOPK)
    seq_gates = gate_values.reshape(N_DP, SEQ_LEN, TOPK)

    def per_sequence(running_sums, sequence_item):
        item_inputs, item_grad, item_ids, item_gates = sequence_item

        def forward(item_x, *weights):
            return layer(item_x, *weights, item_ids, item_gates)
        outputs, pullback = jax.vjp(forward, item_inputs, *params)
        gradients = pullback(item_grad)
        running_sums = jax.tree.map(lambda running, latest: running + latest, running_sums, tuple(gradients[1:]))
        return (running_sums, (outputs, gradients[0]))
    initial = tuple((jnp.zeros_like(weight_array) for weight_array in params))
    totals, (outputs, input_grads) = lax.scan(per_sequence, initial, (seq_inputs, seq_grads, seq_ids, seq_gates))
    return (outputs.reshape(-1, MODEL_WIDTH).astype(jnp.bfloat16), input_grads.reshape(-1, MODEL_WIDTH).astype(jnp.bfloat16), totals[0], totals[1], totals[2], totals[3], totals[4], totals[5], totals[6], totals[7], totals[8])
```

```python
import jax
import jax.numpy as jnp
from jax import lax
from jax.sharding import PartitionSpec as P

HEAD_SIZE = 64
NORM_EPSILON = 1e-06
ATT_SCALE = 0.015625
RES_SCALE = 0.22
ROPE_BASE = 10000.0
NEG_FILL = -1e30
F32 = jnp.float32
BF16 = jnp.bfloat16


def rms_normed(activations, gain_vector):
    return (
        activations
        * lax.rsqrt(jnp.mean(activations * activations, axis=-1, keepdims=True) + NORM_EPSILON)
        * gain_vector
    )


def rotary_tables(length):
    half_width = HEAD_SIZE // 2
    positions = jnp.arange(length).astype(F32)
    frequencies = jnp.power(ROPE_BASE, -(jnp.arange(half_width).astype(F32) * 2.0 / HEAD_SIZE))
    angles = positions[:, None] * frequencies[None, :]
    return (jnp.cos(angles)[:, None, :], jnp.sin(angles)[:, None, :])


def apply_rotary(head_data, cosine, sine):
    half_width = head_data.shape[-1] // 2
    first_half = head_data[..., :half_width]
    second_half = head_data[..., half_width:]
    return jnp.concatenate(
        [first_half * cosine - second_half * sine, second_half * cosine + first_half * sine], axis=-1
    )


def mm(a, b, spec):
    return jnp.einsum(spec, a, b, preferred_element_type=F32)


def local(
    inputs, first_gain, query_weight, key_matrix, value_matrix, output_weight, second_gain,
    gate_weight, up_weight, down_weight, expert_ids, gate_values, out_grad,
):
    dp_size = lax.axis_size("dp")
    rank = lax.axis_index("tensor")
    rows = inputs.shape[0] * lax.axis_size("tensor")
    experts, part, units = gate_weight.shape
    width = part * dp_size
    qw = query_weight.shape[1]
    kw = key_matrix.shape[1]
    q_heads, kv_heads = qw // HEAD_SIZE, kw // HEAD_SIZE
    group = q_heads // kv_heads
    cosine, sine = rotary_tables(rows)

    small = jnp.concatenate(
        [query_weight, key_matrix, value_matrix, output_weight.T, first_gain[:, None], second_gain[:, None],
         jnp.zeros((part, 126), BF16)], axis=1)
    small = lax.all_gather(small, "dp", axis=0, tiled=True)
    qkv_full = small[:, : qw + 2 * kw]
    out_t = small[:, qw + 2 * kw : 2 * qw + 2 * kw]
    gain_first = small[:, 2 * qw + 2 * kw].astype(F32)
    gain_second = small[:, 2 * qw + 2 * kw + 1].astype(F32)
    gate_up = lax.all_gather(jnp.concatenate([gate_weight, up_weight], 0), "dp", axis=1, tiled=True)
    down_full = lax.all_gather(down_weight, "dp", axis=2, tiled=True)
    out_grad_full = lax.all_gather(out_grad, "tensor", axis=0, tiled=True)

    x = inputs.astype(F32)
    normed_local = rms_normed(x, gain_first).astype(BF16)
    normed = lax.all_gather(normed_local, "tensor", axis=0, tiled=True)
    qkv = mm(normed, qkv_full, "sd,dq->sq")
    queries = apply_rotary(qkv[:, :qw].reshape(rows, q_heads, HEAD_SIZE), cosine, sine).astype(BF16)
    keys = apply_rotary(qkv[:, qw : qw + kw].reshape(rows, kv_heads, HEAD_SIZE), cosine, sine).astype(BF16)
    values = qkv[:, qw + kw :].astype(BF16).reshape(rows, kv_heads, HEAD_SIZE)
    queries = queries.reshape(rows, kv_heads, group, HEAD_SIZE)
    scores = mm(queries, keys, "qhgd,khd->hgqk") * ATT_SCALE
    mask = jnp.arange(rows)[:, None] >= jnp.arange(rows)[None, :]
    scores = jnp.where(mask, scores, NEG_FILL)
    terms = jnp.exp(scores - jnp.max(scores, axis=-1, keepdims=True))
    probs = terms / jnp.sum(terms, axis=-1, keepdims=True)
    probs_low = probs.astype(BF16)
    attended = mm(probs_low, values, "hgqk,khd->qhgd").astype(BF16).reshape(rows, qw)
    branch = lax.psum_scatter(
        mm(attended, out_t, "sq,dq->sd").astype(BF16), "tensor", scatter_dimension=0, tiled=True
    ).astype(F32)
    hidden = x + RES_SCALE * branch
    normed_two_local = rms_normed(hidden, gain_second).astype(BF16)
    normed_two = lax.all_gather(normed_two_local, "tensor", axis=0, tiled=True)

    expert_index = rank * experts + jnp.arange(experts, dtype=jnp.int32)
    combined = jnp.sum(
        jnp.where(expert_ids[:, :, None] == expert_index, gate_values[:, :, None], 0.0), axis=1)
    gate_full, up_full = gate_up[:experts], gate_up[experts:]
    gate = mm(normed_two, gate_full, "sd,edf->sef")
    up = mm(normed_two, up_full, "sd,edf->sef")
    sig = jax.nn.sigmoid(gate)
    scale = combined[:, :, None]
    hidden_units = (scale * (gate * sig * up)).astype(BF16)
    moe_partial = mm(hidden_units, down_full, "sef,efd->sd")
    down_grad = mm(hidden_units, out_grad_full, "sef,sd->efd") * RES_SCALE
    hidden_grad = mm(out_grad_full, down_full, "sd,efd->sef") * (RES_SCALE * scale)
    gate_pre = (hidden_grad * up * sig * (1.0 + gate * (1.0 - sig))).astype(BF16)
    up_pre = (hidden_grad * gate * sig).astype(BF16)
    gate_grad = mm(normed_two, gate_pre, "sd,sef->edf")
    up_grad = mm(normed_two, up_pre, "sd,sef->edf")
    rows_grad = mm(gate_pre, gate_full, "sef,edf->sd") + mm(up_pre, up_full, "sef,edf->sd")

    moe_local = lax.psum_scatter(
        moe_partial.astype(BF16), "tensor", scatter_dimension=0, tiled=True).astype(F32)
    block_output = (hidden + RES_SCALE * moe_local).astype(BF16)
    normed_two_grad = lax.psum_scatter(
        rows_grad.astype(BF16), "tensor", scatter_dimension=0, tiled=True).astype(F32)
    _, pull_two = jax.vjp(rms_normed, hidden, gain_second)
    state_norm_grad, second_part = pull_two(normed_two_grad)
    state_grad = out_grad.astype(F32) + state_norm_grad
    branch_grad = lax.all_gather(
        (RES_SCALE * state_grad).astype(BF16), "tensor", axis=0, tiled=True)

    output_part = mm(attended, branch_grad, "sq,sd->qd")
    attended_grad = mm(branch_grad, out_t, "sd,dq->sq").astype(BF16)
    attended_grad = attended_grad.reshape(rows, kv_heads, group, HEAD_SIZE)
    value_grad = mm(probs_low, attended_grad, "hgqk,qhgd->khd")
    weight_grad = mm(attended_grad, values, "qhgd,khd->hgqk")
    inner = jnp.sum(weight_grad * probs, axis=-1, keepdims=True)
    score_grad = (probs * (weight_grad - inner)).astype(BF16)
    query_grad = mm(score_grad, keys, "hgqk,khd->qhgd") * ATT_SCALE
    key_grad = mm(score_grad, queries, "hgqk,qhgd->khd") * ATT_SCALE
    query_pre = apply_rotary(query_grad.reshape(rows, q_heads, HEAD_SIZE), cosine, -sine)
    key_pre = apply_rotary(key_grad, cosine, -sine)
    pre = jnp.concatenate(
        [query_pre.reshape(rows, -1), key_pre.reshape(rows, -1), value_grad.reshape(rows, -1)], axis=1
    ).astype(BF16)
    qkv_part = mm(normed, pre, "sd,sq->dq")
    normed_grad = lax.psum_scatter(
        mm(pre, qkv_full, "sq,dq->sd").astype(BF16), "tensor", scatter_dimension=0, tiled=True).astype(F32)
    _, pull_one = jax.vjp(rms_normed, x, gain_first)
    input_norm_grad, first_part = pull_one(normed_grad)
    input_grad = (state_grad + input_norm_grad).astype(BF16)

    gains = lax.psum(jnp.stack([first_part, second_part], 1), "tensor")
    small_grad = jnp.concatenate(
        [qkv_part, output_part.T, gains, jnp.zeros((width, 126), F32)], axis=1).astype(BF16)
    small_grad = lax.psum_scatter(small_grad, "dp", scatter_dimension=0, tiled=True).astype(F32)
    gate_up_grad = lax.psum_scatter(
        jnp.concatenate([gate_grad.astype(BF16), up_grad.astype(BF16)], 0), "dp", scatter_dimension=1, tiled=True
    ).astype(F32)
    down_grad = lax.psum_scatter(
        down_grad.astype(BF16), "dp", scatter_dimension=2, tiled=True).astype(F32)
    return (
        block_output,
        input_grad,
        small_grad[:, 2 * qw + 2 * kw],
        small_grad[:, :qw],
        small_grad[:, qw : qw + kw],
        small_grad[:, qw + kw : qw + 2 * kw],
        small_grad[:, qw + 2 * kw : 2 * qw + 2 * kw].T,
        small_grad[:, 2 * qw + 2 * kw + 1],
        gate_up_grad[:experts],
        gate_up_grad[experts:],
        down_grad,
    )


def solution(mesh):
    in_specs = (
        P(("dp", "tensor"), None),
        P("dp"),
        P("dp", "tensor"),
        P("dp", "tensor"),
        P("dp", "tensor"),
        P("tensor", "dp"),
        P("dp"),
        P("tensor", "dp", None),
        P("tensor", "dp", None),
        P("tensor", None, "dp"),
        P("dp", None),
        P("dp", None),
        P(("dp", "tensor"), None),
    )
    out_specs = (
        P(("dp", "tensor"), None),
        P(("dp", "tensor"), None),
        P("dp"),
        P("dp", "tensor"),
        P("dp", "tensor"),
        P("dp", "tensor"),
        P("tensor", "dp"),
        P("dp"),
        P("tensor", "dp", None),
        P("tensor", "dp", None),
        P("tensor", None, "dp"),
    )
    return jax.shard_map(local, mesh=mesh, in_specs=in_specs, out_specs=out_specs, check_vma=False)
```

```python
import functools

import jax
import jax.numpy as jnp
from jax import lax
from jax.experimental import pallas as pl
from jax.experimental.pallas import tpu as pltpu
from jax.sharding import PartitionSpec as P

HEAD_SIZE = 64
NORM_EPSILON = 1e-06
ATT_SCALE = 0.015625
RES_SCALE = 0.22
ROPE_BASE = 10000.0
NEG_FILL = -1e30
F32 = jnp.float32
BF16 = jnp.bfloat16
MESH = pl.DeviceIdType.MESH
NX, NY, NZ, NCORE = 4, 2, 4, 2
ROWS, WIDTH, PART, UNITS = 128, 1024, 64, 512
ANY = pl.BlockSpec(memory_space=pl.ANY)
VMEM = pl.BlockSpec(memory_space=pltpu.VMEM)
DMA = pltpu.SemaphoreType.DMA


class Place:
    def __init__(self):
        d, t = lax.axis_index("dp"), lax.axis_index("tensor")
        self.d, self.t = d, t
        self.tx, self.ty = t // NY, t % NY
        self.dy, self.dz, self.dc = d // (NZ * NCORE), (d // NCORE) % NZ, d % NCORE
        self.pair = self.tx * NY + (1 - self.ty)
        self.d_pair = self.dp(1 - self.dy, self.dz, self.dc)

    def dp(self, y, z, core):
        return (y * NZ + z) * NCORE + core

    def tensor_pair(self):
        return (self.d, self.pair)

    def x(self, j):
        return (self.tx + j) % NX

    def x_dev(self, j):
        return (self.d, self.x(j) * NY + self.ty)

    def z(self, j):
        return (self.dz + j) % NZ

    def z_dev(self, j):
        return (self.dp(self.dy, self.z(j), self.dc), self.t)

    def y_dev(self):
        return (self.d_pair, self.t)

    def core_dev(self):
        return (self.dp(self.dy, self.dz, 1 - self.dc), self.t)


def meet(p):
    barrier = pltpu.get_barrier_semaphore()
    others = [p.tensor_pair(), p.y_dev(), p.core_dev()]
    others += [p.x_dev(j) for j in range(1, NX)] + [p.z_dev(j) for j in range(1, NZ)]
    for other in others:
        pl.semaphore_signal(barrier, inc=1, device_id=other, device_id_type=MESH)
    pl.semaphore_wait(barrier, len(others))


def push(src, dst, sems, number, device):
    copy = pltpu.make_async_remote_copy(
        src_ref=src, dst_ref=dst, send_sem=sems[0].at[number], recv_sem=sems[1].at[number],
        device_id=device, device_id_type=MESH)
    copy.start()
    return copy


def sems(number):
    return [DMA((number,)), DMA((number,))]


class TensorGather:
    SEMS = 7

    def __init__(self, p, src, out, sem, local_sem):
        self.p, self.out, self.sem = p, out, sem
        self.copies = [push(src, out.at[p.t], sem, 0, p.tensor_pair())]
        self.copies += [push(src, out.at[p.t], sem, j, p.x_dev(j)) for j in range(1, NX)]
        self.own = pltpu.make_async_copy(src, out.at[p.t], local_sem)
        self.own.start()

    def forward(self):
        p = self.p
        self.copies[0].wait_recv()
        self.copies += [
            push(self.out.at[p.pair], self.out.at[p.pair], self.sem, 3 + j, p.x_dev(j)) for j in range(1, NX)]

    def finish(self):
        for copy in self.copies[1:]:
            copy.wait_recv()
        for copy in self.copies:
            copy.wait_send()
        self.own.wait()


class TensorScatter:
    SEMS = 7

    @staticmethod
    def scratch():
        return [pltpu.VMEM((NX, NY, ROWS, WIDTH), BF16), pltpu.VMEM((2, ROWS, WIDTH), BF16)] + sems(7) + [DMA((1,))]

    def __init__(self, p, partial, got, pair_buf, send, recv, local):
        self.p, self.got, self.pair_buf = p, got, pair_buf
        self.sem = (send, recv)
        self.copies = []
        for half, c in enumerate((1 - p.ty, p.ty)):
            self.copies.append([
                push(partial.at[p.x(j) * NY + c], got.at[j, c], self.sem, half * 3 + j - 1, p.x_dev(j))
                for j in range(1, NX)])
        self.own = pltpu.make_async_copy(partial.at[pl.ds(p.tx * NY, NY)], got.at[0], local.at[0])
        self.own.start()

    def total(self, c, rows):
        value = self.got[0, c, rows].astype(F32)
        for j in range(1, NX):
            value = value + self.got[j, c, rows].astype(F32)
        return value

    def exchange(self):
        p = self.p
        self.own.wait()
        for copy in self.copies[0]:
            copy.wait_recv()

        def step(i, carry):
            rows = pl.ds(pl.multiple_of(i * 32, 32), 32)
            self.pair_buf[0, rows] = self.total(1 - p.ty, rows).astype(BF16)
            return carry

        lax.fori_loop(0, ROWS // 32, step, 0)
        self.pair = push(self.pair_buf.at[0], self.pair_buf.at[1], self.sem, 6, p.tensor_pair())

    def arrive(self):
        for copy in self.copies[1]:
            copy.wait_recv()
        self.pair.wait_recv()

    def rows(self, rows):
        return self.total(self.p.ty, rows) + self.pair_buf[1, rows].astype(F32)

    def finish(self):
        for copy in self.copies[0] + self.copies[1] + [self.pair]:
            copy.wait_send()


class PartGather:
    SEMS = 15

    def __init__(self, p, shard, out, sem, local_sem):
        self.p, self.out, self.sem = p, out, sem
        mine = out.at[:, p.d]
        self.pair = push(shard, mine, sem, 0, p.y_dev())
        self.along = [push(shard, mine, sem, j, p.z_dev(j)) for j in range(1, NZ)]
        self.core = [push(shard, mine, sem, 4, p.core_dev())]
        self.own = pltpu.make_async_copy(shard, mine, local_sem)
        self.own.start()

    def resend(self, index, number, device):
        return push(self.out.at[:, index], self.out.at[:, index], self.sem, number, device)

    def forward(self):
        p = self.p
        self.pair.wait_recv()
        self.along_pair = [self.resend(p.d_pair, 4 + j, p.z_dev(j)) for j in range(1, NZ)]
        self.core.append(self.resend(p.d_pair, 8, p.core_dev()))

    def spread(self):
        p = self.p
        for first, copies, y in ((9, self.along, p.dy), (12, self.along_pair, 1 - p.dy)):
            for j in range(1, NZ):
                copies[j - 1].wait_recv()
                index = p.dp(y, (p.dz + NZ - j) % NZ, p.dc)
                self.core.append(self.resend(index, first + j - 1, p.core_dev()))

    def finish(self):
        for copy in self.core:
            copy.wait_recv()
        for copy in [self.pair] + self.along + self.along_pair + self.core:
            copy.wait_send()
        self.own.wait()


class PartScatter:
    SEMS = 5

    @staticmethod
    def scratch(n):
        return [
            pltpu.VMEM((n, 2, NZ, PART, UNITS), BF16),
            pltpu.VMEM((n, 2, NZ, PART, UNITS), BF16),
            pltpu.VMEM((NZ, n, 2, PART, UNITS), BF16),
            pltpu.VMEM((2, n, PART, UNITS), BF16),
        ] + sems(5) + [DMA((1,))]

    def __init__(self, p, grads, own, core_buf, z_buf, y_buf, send, recv, local):
        self.p, self.n = p, grads.shape[0]
        self.own, self.core_buf, self.z_buf, self.y_buf = own, core_buf, z_buf, y_buf
        self.sem = (send, recv)
        self.core = push(grads.at[:, :, :, 1 - p.dc], core_buf, self.sem, 0, p.core_dev())
        self.load = pltpu.make_async_copy(grads.at[:, :, :, p.dc], own, local.at[0])
        self.load.start()

    def along(self):
        p = self.p
        self.load.wait()
        self.core.wait_recv()

        def step(i, carry):
            for y in range(2):
                for z in range(NZ):
                    total = self.own[i, y, z].astype(F32) + self.core_buf[i, y, z].astype(F32)
                    self.own[i, y, z] = total.astype(BF16)
            return carry

        lax.fori_loop(0, self.n, step, 0)
        self.z_copies = [
            push(self.own.at[:, :, p.z(j)], self.z_buf.at[j], self.sem, j, p.z_dev(j)) for j in range(1, NZ)]

    def total(self, i, y):
        value = self.own[i, y, self.p.dz].astype(F32)
        for j in range(1, NZ):
            value = value + self.z_buf[j, i, y].astype(F32)
        return value

    def pair(self):
        p = self.p
        for copy in self.z_copies:
            copy.wait_recv()

        def step(i, carry):
            self.y_buf[0, i] = self.total(i, 1 - p.dy).astype(BF16)
            return carry

        lax.fori_loop(0, self.n, step, 0)
        self.y_copy = push(self.y_buf.at[0], self.y_buf.at[1], self.sem, 4, p.y_dev())

    def finish(self, out):
        p = self.p
        self.y_copy.wait_recv()

        def step(i, carry):
            out[i] = self.total(i, p.dy) + self.y_buf[1, i].astype(F32)
            return carry

        lax.fori_loop(0, self.n, step, 0)
        for copy in [self.core, self.y_copy] + self.z_copies:
            copy.wait_send()


def params(number, megabytes):
    return pltpu.CompilerParams(
        collective_id=number, has_side_effects=True, vmem_limit_bytes=megabytes << 20)


def shape(dims, dtype=BF16):
    return jax.ShapeDtypeStruct(dims, dtype)


def first_kernel(x, small, gate, x_out, small_out, gate_out, ts, tr, ss, sr, gs, gr, local):
    p = Place()
    meet(p)
    small_gather = PartGather(p, small, small_out, (ss, sr), local.at[1])
    rows = TensorGather(p, x, x_out, (ts, tr), local.at[0])
    gates = PartGather(p, gate, gate_out, (gs, gr), local.at[2])
    small_gather.forward()
    rows.forward()
    small_gather.spread()
    gates.forward()
    gates.spread()
    small_gather.finish()
    rows.finish()
    gates.finish()


def second_kernel(partial, x, gain, up, down, hidden, normed_out, up_out, down_out, normed, *scratch):
    p = Place()
    meet(p)
    us, ur, ds, dr, ts, tr, local = scratch[-7:]
    branch = TensorScatter(p, partial, *scratch[:5])
    ups = PartGather(p, up, up_out, (us, ur), local.at[1])
    branch.exchange()
    downs = PartGather(p, down, down_out, (ds, dr), local.at[2])
    ups.forward()
    branch.arrive()

    def step(i, carry):
        rows = pl.ds(pl.multiple_of(i * 32, 32), 32)
        state = x[rows].astype(F32) + RES_SCALE * branch.rows(rows)
        hidden[rows] = state
        scale = lax.rsqrt(jnp.mean(state * state, axis=-1, keepdims=True) + NORM_EPSILON)
        normed[rows] = (state * scale * gain[...]).astype(BF16)
        return carry

    lax.fori_loop(0, ROWS // 32, step, 0)
    gather = TensorGather(p, normed, normed_out, (ts, tr), local.at[0])
    downs.forward()
    gather.forward()
    ups.spread()
    downs.spread()
    branch.finish()
    gather.finish()
    ups.finish()
    downs.finish()


def norm_pull(state, gain, grad):
    r = lax.rsqrt(jnp.mean(state * state, axis=-1, keepdims=True) + NORM_EPSILON)
    u = state * r
    w = gain * grad
    return r * (w - u * jnp.mean(w * u, axis=-1, keepdims=True)), jnp.sum(grad * u, axis=0, keepdims=True)


def third_kernel(
    partial, gate_grads, up_grads, hidden, gain, out_grad,
    branch_out, state_grad, gain_part, gate_out, up_out, branch, *scratch,
):
    p = Place()
    meet(p)
    ts, tr, local = scratch[-3:]
    rows_sum = TensorScatter(p, partial, *scratch[:5])
    gates = PartScatter(p, gate_grads, *scratch[5:12])
    ups = PartScatter(p, up_grads, *scratch[12:19])
    gates.along()
    ups.along()
    rows_sum.exchange()
    rows_sum.arrive()
    gain_part[...] = jnp.zeros_like(gain_part)

    def step(i, carry):
        rows = pl.ds(pl.multiple_of(i * 32, 32), 32)
        pulled, part = norm_pull(hidden[rows], gain[...], rows_sum.rows(rows))
        gain_part[0:1] += part
        state = out_grad[rows].astype(F32) + pulled
        state_grad[rows] = state
        branch[rows] = (RES_SCALE * state).astype(BF16)
        return carry

    lax.fori_loop(0, ROWS // 32, step, 0)
    gather = TensorGather(p, branch, branch_out, (ts, tr), local.at[0])
    gather.forward()
    gates.pair()
    ups.pair()
    rows_sum.finish()
    gates.finish(gate_out)
    ups.finish(up_out)
    gather.finish()


def fourth_kernel(
    partial, down_grads, small_grads, x, gain, state_grad, second_part,
    input_grad, down_out, small_out, gains, gain_buf, *scratch,
):
    p = Place()
    meet(p)
    gs, gr = scratch[-2:]
    rows_sum = TensorScatter(p, partial, *scratch[:5])
    smalls = PartScatter(p, small_grads, *scratch[5:12])
    downs = PartScatter(p, down_grads, *scratch[12:19])
    smalls.along()
    downs.along()
    rows_sum.exchange()
    rows_sum.arrive()
    gains[...] = jnp.zeros_like(gains)
    gains[1:2] = second_part[0:1]

    def step(i, carry):
        rows = pl.ds(pl.multiple_of(i * 32, 32), 32)
        pulled, part = norm_pull(x[rows].astype(F32), gain[...], rows_sum.rows(rows))
        gains[0:1] += part
        input_grad[rows] = (state_grad[rows] + pulled).astype(BF16)
        return carry

    lax.fori_loop(0, ROWS // 32, step, 0)

    number = 0
    copies = []
    stages = (
        [p.x_dev(j) for j in range(1, NX)], [p.tensor_pair()], [p.core_dev()],
        [p.z_dev(j) for j in range(1, NZ)], [p.y_dev()])
    between = (smalls.pair, downs.pair, None, None, None)
    for stage, (devices, work) in enumerate(zip(stages, between)):
        gain_buf[9 + stage] = gains[...]
        now = [push(gain_buf.at[9 + stage], gain_buf.at[number + k], (gs, gr), number + k, device)
               for k, device in enumerate(devices)]
        if work is not None:
            work()
        for k, copy in enumerate(now):
            copy.wait_recv()
            gains[...] += gain_buf[number + k]
        number += len(devices)
        copies += now
    rows_sum.finish()
    smalls.finish(small_out)
    downs.finish(down_out)
    for copy in copies:
        copy.wait_send()


def first(x, small, gate):
    return pl.pallas_call(
        first_kernel,
        out_shape=(shape((8, ROWS, WIDTH)), shape((1, 16, PART, UNITS)), shape((4, 16, PART, UNITS))),
        in_specs=[ANY] * 3, out_specs=(ANY,) * 3,
        scratch_shapes=sems(7) + sems(15) + sems(15) + [DMA((3,))],
        compiler_params=params(1, 32), name="first",
    )(x, small, gate)


def second(partial, x, gain, up, down):
    full = shape((4, 16, PART, UNITS))
    return pl.pallas_call(
        second_kernel,
        out_shape=(shape((ROWS, WIDTH), F32), shape((8, ROWS, WIDTH)), full, full),
        in_specs=[ANY, VMEM, VMEM, ANY, ANY], out_specs=(VMEM, ANY, ANY, ANY),
        scratch_shapes=[pltpu.VMEM((ROWS, WIDTH), BF16)] + TensorScatter.scratch()
        + sems(15) + sems(15) + sems(7) + [DMA((3,))],
        compiler_params=params(2, 32), name="second",
    )(partial, x, gain, up, down)


def third(partial, gate_grads, up_grads, hidden, gain, out_grad):
    return pl.pallas_call(
        third_kernel,
        out_shape=(
            shape((8, ROWS, WIDTH)), shape((ROWS, WIDTH), F32), shape((8, WIDTH), F32),
            shape((4, PART, UNITS), F32), shape((4, PART, UNITS), F32)),
        in_specs=[ANY, ANY, ANY, VMEM, VMEM, VMEM], out_specs=(ANY,) + (VMEM,) * 4,
        scratch_shapes=[pltpu.VMEM((ROWS, WIDTH), BF16)] + TensorScatter.scratch()
        + PartScatter.scratch(4) + PartScatter.scratch(4) + sems(7) + [DMA((1,))],
        compiler_params=params(3, 48), name="third",
    )(partial, gate_grads, up_grads, hidden, gain, out_grad)


def fourth(partial, down_grads, small_grads, x, gain, state_grad, second_part):
    return pl.pallas_call(
        fourth_kernel,
        out_shape=(
            shape((ROWS, WIDTH)), shape((4, PART, UNITS), F32), shape((1, PART, UNITS), F32),
            shape((8, WIDTH), F32)),
        in_specs=[ANY, ANY, ANY, VMEM, VMEM, VMEM, VMEM], out_specs=(VMEM,) * 4,
        scratch_shapes=[pltpu.VMEM((14, 8, WIDTH), F32)] + TensorScatter.scratch()
        + PartScatter.scratch(1) + PartScatter.scratch(4) + sems(9),
        compiler_params=params(4, 48), name="fourth",
    )(partial, down_grads, small_grads, x, gain, state_grad, second_part)


def rms_normed(activations, gain_vector):
    return (
        activations
        * lax.rsqrt(jnp.mean(activations * activations, axis=-1, keepdims=True) + NORM_EPSILON)
        * gain_vector
    )


def rotary_tables(length):
    half_width = HEAD_SIZE // 2
    positions = jnp.arange(length).astype(F32)
    frequencies = jnp.power(ROPE_BASE, -(jnp.arange(half_width).astype(F32) * 2.0 / HEAD_SIZE))
    angles = positions[:, None] * frequencies[None, :]
    return (jnp.cos(angles)[:, None, :], jnp.sin(angles)[:, None, :])


def apply_rotary(head_data, cosine, sine):
    half_width = head_data.shape[-1] // 2
    first_half = head_data[..., :half_width]
    second_half = head_data[..., half_width:]
    return jnp.concatenate(
        [first_half * cosine - second_half * sine, second_half * cosine + first_half * sine], axis=-1
    )


def mm(a, b, spec):
    return jnp.einsum(spec, a, b, preferred_element_type=F32)


def local(
    inputs, first_gain, query_weight, key_matrix, value_matrix, output_weight, second_gain,
    gate_weight, up_weight, down_weight, expert_ids, gate_values, out_grad,
):
    rank = lax.axis_index("tensor")
    rows = inputs.shape[0] * lax.axis_size("tensor")
    experts = gate_weight.shape[0]
    qw = query_weight.shape[1]
    kw = key_matrix.shape[1]
    q_heads, kv_heads = qw // HEAD_SIZE, kw // HEAD_SIZE
    group = q_heads // kv_heads
    cosine, sine = rotary_tables(rows)

    small = jnp.concatenate(
        [query_weight, key_matrix, value_matrix, output_weight.T, first_gain[:, None], second_gain[:, None],
         jnp.zeros((PART, 126), BF16)], axis=1)
    x_full, small, gate_full = first(inputs, small[None], gate_weight)
    out_grad_full = lax.all_gather(out_grad, "tensor", axis=0, tiled=True)
    small = small.reshape(WIDTH, UNITS)
    gate_full = gate_full.reshape(experts, WIDTH, UNITS)
    qkv_full = small[:, : qw + 2 * kw]
    out_t = small[:, qw + 2 * kw : 2 * qw + 2 * kw]
    gain_first = small[:, 2 * qw + 2 * kw].astype(F32)
    gain_second = small[:, 2 * qw + 2 * kw + 1].astype(F32)

    normed = rms_normed(x_full.reshape(rows, WIDTH).astype(F32), gain_first).astype(BF16)
    qkv = mm(normed, qkv_full, "sd,dq->sq")
    queries = apply_rotary(qkv[:, :qw].reshape(rows, q_heads, HEAD_SIZE), cosine, sine).astype(BF16)
    keys = apply_rotary(qkv[:, qw : qw + kw].reshape(rows, kv_heads, HEAD_SIZE), cosine, sine).astype(BF16)
    values = qkv[:, qw + kw :].astype(BF16).reshape(rows, kv_heads, HEAD_SIZE)
    queries = queries.reshape(rows, kv_heads, group, HEAD_SIZE)
    scores = mm(queries, keys, "qhgd,khd->hgqk") * ATT_SCALE
    mask = jnp.arange(rows)[:, None] >= jnp.arange(rows)[None, :]
    scores = jnp.where(mask, scores, NEG_FILL)
    terms = jnp.exp(scores - jnp.max(scores, axis=-1, keepdims=True))
    probs = terms / jnp.sum(terms, axis=-1, keepdims=True)
    probs_low = probs.astype(BF16)
    attended = mm(probs_low, values, "hgqk,khd->qhgd").astype(BF16).reshape(rows, qw)
    partial = mm(attended, out_t, "sq,dq->sd").astype(BF16).reshape(-1, ROWS, WIDTH)
    hidden, normed_two, up_full, down_full = second(
        partial, inputs, gain_second[None], up_weight, jnp.swapaxes(down_weight, 1, 2))
    normed_two = normed_two.reshape(rows, WIDTH)
    up_full = up_full.reshape(experts, WIDTH, UNITS)
    down_full = down_full.reshape(experts, WIDTH, UNITS)

    expert_index = rank * experts + jnp.arange(experts, dtype=jnp.int32)
    combined = jnp.sum(
        jnp.where(expert_ids[:, :, None] == expert_index, gate_values[:, :, None], 0.0), axis=1)
    gate = mm(normed_two, gate_full, "sd,edf->esf")
    up = mm(normed_two, up_full, "sd,edf->esf")
    sig = jax.nn.sigmoid(gate)
    scale = combined.T[:, :, None]
    hidden_units = (scale * (gate * sig * up)).astype(BF16)
    moe_partial = mm(hidden_units, down_full, "esf,edf->sd")
    moe_local = lax.psum_scatter(
        moe_partial.astype(BF16), "tensor", scatter_dimension=0, tiled=True).astype(F32)
    block_output = (hidden + RES_SCALE * moe_local).astype(BF16)
    hidden_grad = mm(out_grad_full, down_full, "sd,edf->esf") * (RES_SCALE * scale)
    gate_pre = (hidden_grad * up * sig * (1.0 + gate * (1.0 - sig))).astype(BF16)
    up_pre = (hidden_grad * gate * sig).astype(BF16)
    rows_grad = mm(gate_pre, gate_full, "esf,edf->sd") + mm(up_pre, up_full, "esf,edf->sd")
    gate_grad = mm(normed_two, gate_pre, "sd,esf->edf").astype(BF16)
    up_grad = mm(normed_two, up_pre, "sd,esf->edf").astype(BF16)
    down_grad = (mm(out_grad_full, hidden_units, "sd,esf->edf") * RES_SCALE).astype(BF16)
    parts = (experts, 2, NZ, 2, PART, UNITS)
    branch_grad, state_grad, second_part, gate_grad, up_grad = third(
        rows_grad.astype(BF16).reshape(-1, ROWS, WIDTH), gate_grad.reshape(parts), up_grad.reshape(parts),
        hidden, gain_second[None], out_grad)
    branch_grad = branch_grad.reshape(rows, WIDTH)

    output_part = mm(branch_grad, attended, "sd,sq->dq")
    attended_grad = mm(branch_grad, out_t, "sd,dq->sq").astype(BF16)
    attended_grad = attended_grad.reshape(rows, kv_heads, group, HEAD_SIZE)
    value_grad = mm(probs_low, attended_grad, "hgqk,qhgd->khd")
    weight_grad = mm(attended_grad, values, "qhgd,khd->hgqk")
    inner = jnp.sum(weight_grad * probs, axis=-1, keepdims=True)
    score_grad = (probs * (weight_grad - inner)).astype(BF16)
    query_grad = mm(score_grad, keys, "hgqk,khd->qhgd") * ATT_SCALE
    key_grad = mm(score_grad, queries, "hgqk,qhgd->khd") * ATT_SCALE
    query_pre = apply_rotary(query_grad.reshape(rows, q_heads, HEAD_SIZE), cosine, -sine)
    key_pre = apply_rotary(key_grad, cosine, -sine)
    pre = jnp.concatenate(
        [query_pre.reshape(rows, -1), key_pre.reshape(rows, -1), value_grad.reshape(rows, -1)], axis=1
    ).astype(BF16)
    qkv_part = mm(normed, pre, "sd,sq->dq")
    normed_grad = mm(pre, qkv_full, "sq,dq->sd").astype(BF16)
    small_grad = jnp.concatenate(
        [qkv_part, output_part, jnp.zeros((WIDTH, 128), F32)], axis=1).astype(BF16)
    input_grad, down_grad, small_grad, gains = fourth(
        normed_grad.reshape(-1, ROWS, WIDTH), down_grad.reshape(parts), small_grad.reshape((1,) + parts[1:]),
        inputs, gain_first[None], state_grad, second_part)
    small_grad = small_grad[0]
    gains = lax.dynamic_slice_in_dim(gains, lax.axis_index("dp") * PART, PART, 1)
    return (
        block_output,
        input_grad,
        gains[0],
        small_grad[:, :qw],
        small_grad[:, qw : qw + kw],
        small_grad[:, qw + kw : qw + 2 * kw],
        small_grad[:, qw + 2 * kw : 2 * qw + 2 * kw].T,
        gains[1],
        gate_grad,
        up_grad,
        jnp.swapaxes(down_grad, 1, 2),
    )


def solution(mesh):
    in_specs = (
        P(("dp", "tensor"), None),
        P("dp"),
        P("dp", "tensor"),
        P("dp", "tensor"),
        P("dp", "tensor"),
        P("tensor", "dp"),
        P("dp"),
        P("tensor", "dp", None),
        P("tensor", "dp", None),
        P("tensor", None, "dp"),
        P("dp", None),
        P("dp", None),
        P(("dp", "tensor"), None),
    )
    out_specs = (
        P(("dp", "tensor"), None),
        P(("dp", "tensor"), None),
        P("dp"),
        P("dp", "tensor"),
        P("dp", "tensor"),
        P("dp", "tensor"),
        P("tensor", "dp"),
        P("dp"),
        P("tensor", "dp", None),
        P("tensor", "dp", None),
        P("tensor", None, "dp"),
    )
    return jax.shard_map(local, mesh=mesh, in_specs=in_specs, out_specs=out_specs, check_vma=False)
```

```python
import functools

import jax
import jax.numpy as jnp
from jax import lax
from jax.experimental import pallas as pl
from jax.experimental.pallas import tpu as pltpu
from jax.sharding import PartitionSpec as P

HEAD_SIZE = 64
NORM_EPSILON = 1e-06
ATT_SCALE = 0.015625
RES_SCALE = 0.22
ROPE_BASE = 10000.0
NEG_FILL = -1e30
F32 = jnp.float32
BF16 = jnp.bfloat16
MESH = pl.DeviceIdType.MESH
NX, NY, NZ, NCORE = 4, 2, 4, 2
ROWS, WIDTH, PART, UNITS = 128, 1024, 64, 512
QBLOCK = 256
ANY = pl.BlockSpec(memory_space=pl.ANY)
VMEM = pl.BlockSpec(memory_space=pltpu.VMEM)
DMA = pltpu.SemaphoreType.DMA


class Place:
    def __init__(self):
        d, t = lax.axis_index("dp"), lax.axis_index("tensor")
        self.d, self.t = d, t
        self.tx, self.ty = t // NY, t % NY
        self.dy, self.dz, self.dc = d // (NZ * NCORE), (d // NCORE) % NZ, d % NCORE
        self.pair = self.tx * NY + (1 - self.ty)
        self.d_pair = self.dp(1 - self.dy, self.dz, self.dc)

    def dp(self, y, z, core):
        return (y * NZ + z) * NCORE + core

    def tensor_pair(self):
        return (self.d, self.pair)

    def x(self, j):
        return (self.tx + j) % NX

    def x_dev(self, j):
        return (self.d, self.x(j) * NY + self.ty)

    def z(self, j):
        return (self.dz + j) % NZ

    def z_dev(self, j):
        return (self.dp(self.dy, self.z(j), self.dc), self.t)

    def y_dev(self):
        return (self.d_pair, self.t)

    def core_dev(self):
        return (self.dp(self.dy, self.dz, 1 - self.dc), self.t)


def meet(p):
    barrier = pltpu.get_barrier_semaphore()
    others = [p.tensor_pair(), p.y_dev(), p.core_dev()]
    others += [p.x_dev(j) for j in range(1, NX)] + [p.z_dev(j) for j in range(1, NZ)]
    for other in others:
        pl.semaphore_signal(barrier, inc=1, device_id=other, device_id_type=MESH)
    pl.semaphore_wait(barrier, len(others))


def push(src, dst, sems, number, device):
    copy = pltpu.make_async_remote_copy(
        src_ref=src, dst_ref=dst, send_sem=sems[0].at[number], recv_sem=sems[1].at[number],
        device_id=device, device_id_type=MESH)
    copy.start()
    return copy


def sems(number):
    return [DMA((number,)), DMA((number,))]


class TensorGather:
    SEMS = 7

    def __init__(self, p, src, out, sem, local_sem):
        self.p, self.out, self.sem = p, out, sem
        self.copies = [push(src, out.at[p.t], sem, 0, p.tensor_pair())]
        self.copies += [push(src, out.at[p.t], sem, j, p.x_dev(j)) for j in range(1, NX)]
        self.own = pltpu.make_async_copy(src, out.at[p.t], local_sem)
        self.own.start()

    def forward(self):
        p = self.p
        self.copies[0].wait_recv()
        self.copies += [
            push(self.out.at[p.pair], self.out.at[p.pair], self.sem, 3 + j, p.x_dev(j)) for j in range(1, NX)]

    def finish(self):
        for copy in self.copies[1:]:
            copy.wait_recv()
        for copy in self.copies:
            copy.wait_send()
        self.own.wait()


class TensorScatter:
    SEMS = 7

    @staticmethod
    def scratch():
        return [pltpu.VMEM((NX, NY, ROWS, WIDTH), BF16), pltpu.VMEM((2, ROWS, WIDTH), BF16)] + sems(7) + [DMA((1,))]

    def __init__(self, p, partial, got, pair_buf, send, recv, local):
        self.p, self.got, self.pair_buf = p, got, pair_buf
        self.sem = (send, recv)
        self.copies = []
        for half, c in enumerate((1 - p.ty, p.ty)):
            self.copies.append([
                push(partial.at[p.x(j) * NY + c], got.at[j, c], self.sem, half * 3 + j - 1, p.x_dev(j))
                for j in range(1, NX)])
        self.own = pltpu.make_async_copy(partial.at[pl.ds(p.tx * NY, NY)], got.at[0], local.at[0])
        self.own.start()

    def total(self, c, rows):
        value = self.got[0, c, rows].astype(F32)
        for j in range(1, NX):
            value = value + self.got[j, c, rows].astype(F32)
        return value

    def exchange(self):
        p = self.p
        self.own.wait()
        for copy in self.copies[0]:
            copy.wait_recv()

        def step(i, carry):
            rows = pl.ds(pl.multiple_of(i * 32, 32), 32)
            self.pair_buf[0, rows] = self.total(1 - p.ty, rows).astype(BF16)
            return carry

        lax.fori_loop(0, ROWS // 32, step, 0)
        self.pair = push(self.pair_buf.at[0], self.pair_buf.at[1], self.sem, 6, p.tensor_pair())

    def arrive(self):
        for copy in self.copies[1]:
            copy.wait_recv()
        self.pair.wait_recv()

    def rows(self, rows):
        return self.total(self.p.ty, rows) + self.pair_buf[1, rows].astype(F32)

    def finish(self):
        for copy in self.copies[0] + self.copies[1] + [self.pair]:
            copy.wait_send()


class PartGather:
    SEMS = 15

    def __init__(self, p, shard, out, sem, local_sem):
        self.p, self.out, self.sem = p, out, sem
        mine = out.at[:, p.d]
        self.pair = push(shard, mine, sem, 0, p.y_dev())
        self.along = [push(shard, mine, sem, j, p.z_dev(j)) for j in range(1, NZ)]
        self.core = [push(shard, mine, sem, 4, p.core_dev())]
        self.own = pltpu.make_async_copy(shard, mine, local_sem)
        self.own.start()

    def resend(self, index, number, device):
        return push(self.out.at[:, index], self.out.at[:, index], self.sem, number, device)

    def forward(self):
        p = self.p
        self.pair.wait_recv()
        self.along_pair = [self.resend(p.d_pair, 4 + j, p.z_dev(j)) for j in range(1, NZ)]
        self.core.append(self.resend(p.d_pair, 8, p.core_dev()))

    def spread(self):
        p = self.p
        for first, copies, y in ((9, self.along, p.dy), (12, self.along_pair, 1 - p.dy)):
            for j in range(1, NZ):
                copies[j - 1].wait_recv()
                index = p.dp(y, (p.dz + NZ - j) % NZ, p.dc)
                self.core.append(self.resend(index, first + j - 1, p.core_dev()))

    def finish(self):
        for copy in self.core:
            copy.wait_recv()
        for copy in [self.pair] + self.along + self.along_pair + self.core:
            copy.wait_send()
        self.own.wait()


class PartScatter:
    SEMS = 5

    @staticmethod
    def scratch(n):
        return [
            pltpu.VMEM((n, 2, NZ, PART, UNITS), BF16),
            pltpu.VMEM((n, 2, NZ, PART, UNITS), BF16),
            pltpu.VMEM((NZ, n, 2, PART, UNITS), BF16),
            pltpu.VMEM((2, n, PART, UNITS), BF16),
        ] + sems(5) + [DMA((1,))]

    def __init__(self, p, grads, own, core_buf, z_buf, y_buf, send, recv, local):
        self.p, self.n = p, grads.shape[0]
        self.own, self.core_buf, self.z_buf, self.y_buf = own, core_buf, z_buf, y_buf
        self.sem = (send, recv)
        self.core = push(grads.at[:, :, :, 1 - p.dc], core_buf, self.sem, 0, p.core_dev())
        self.load = pltpu.make_async_copy(grads.at[:, :, :, p.dc], own, local.at[0])
        self.load.start()

    def along(self):
        p = self.p
        self.load.wait()
        self.core.wait_recv()

        def step(i, carry):
            for y in range(2):
                for z in range(NZ):
                    total = self.own[i, y, z].astype(F32) + self.core_buf[i, y, z].astype(F32)
                    self.own[i, y, z] = total.astype(BF16)
            return carry

        lax.fori_loop(0, self.n, step, 0)
        self.z_copies = [
            push(self.own.at[:, :, p.z(j)], self.z_buf.at[j], self.sem, j, p.z_dev(j)) for j in range(1, NZ)]

    def total(self, i, y):
        value = self.own[i, y, self.p.dz].astype(F32)
        for j in range(1, NZ):
            value = value + self.z_buf[j, i, y].astype(F32)
        return value

    def pair(self):
        p = self.p
        for copy in self.z_copies:
            copy.wait_recv()

        def step(i, carry):
            self.y_buf[0, i] = self.total(i, 1 - p.dy).astype(BF16)
            return carry

        lax.fori_loop(0, self.n, step, 0)
        self.y_copy = push(self.y_buf.at[0], self.y_buf.at[1], self.sem, 4, p.y_dev())

    def finish(self, out):
        p = self.p
        self.y_copy.wait_recv()

        def step(i, carry):
            out[i] = self.total(i, p.dy) + self.y_buf[1, i].astype(F32)
            return carry

        lax.fori_loop(0, self.n, step, 0)
        for copy in [self.core, self.y_copy] + self.z_copies:
            copy.wait_send()


def params(number, megabytes):
    return pltpu.CompilerParams(
        collective_id=number, has_side_effects=True, vmem_limit_bytes=megabytes << 20)


def shape(dims, dtype=BF16):
    return jax.ShapeDtypeStruct(dims, dtype)


def nn(a, b):
    return lax.dot_general(a, b, (((1,), (0,)), ((), ())), preferred_element_type=F32)


def nt(a, b):
    return lax.dot_general(a, b, (((1,), (1,)), ((), ())), preferred_element_type=F32)


def tn(a, b):
    return lax.dot_general(a, b, (((0,), (0,)), ((), ())), preferred_element_type=F32)


def lanes(rows):
    return lax.broadcasted_iota(jnp.int32, (rows, 2 * HEAD_SIZE), 1)


def rotate(pair, cosine, sine):
    first = lanes(pair.shape[0]) % HEAD_SIZE < HEAD_SIZE // 2
    other = jnp.where(first, pltpu.roll(pair, 3 * HEAD_SIZE // 2, 1), pltpu.roll(pair, HEAD_SIZE // 2, 1))
    return pair * cosine + other * sine


def stacked(pair):
    low = lanes(pair.shape[0]) < HEAD_SIZE
    zero = jnp.zeros_like(pair)
    return jnp.concatenate([jnp.where(low, pair, zero), jnp.where(low, zero, pair)], axis=0)


def unstacked(both):
    rows = both.shape[0] // 2
    return jnp.where(lanes(rows) < HEAD_SIZE, both[:rows], both[rows:])


def masked(scores, first_row):
    rows = lax.broadcasted_iota(jnp.int32, scores.shape, 0) % QBLOCK + first_row
    columns = lax.broadcasted_iota(jnp.int32, scores.shape, 1)
    return jnp.where(columns <= rows, scores, NEG_FILL)


def doubled(kv, keys, values):
    low = lanes(kv.shape[0]) < HEAD_SIZE
    kv = kv.astype(F32)
    swapped = pltpu.roll(kv, HEAD_SIZE, 1)
    keys[...] = jnp.where(low, kv, swapped).astype(BF16)
    values[...] = jnp.where(low, swapped, kv).astype(BF16)


def forward_kernel(
    x, small, gate, up, down, out_grad, tables,
    hidden, normed_out, grad_out, gate_out, up_out, down_out, normed, qkv, attended, log_total, small_out, gains,
    x_buf, keys, values, partial, normed_two, *scratch,
):
    p = Place()
    meet(p)
    branch_scratch, scratch = scratch[:5], scratch[5:]
    pairs = [scratch[2 * i : 2 * i + 2] for i in range(7)]
    local = scratch[14]
    smalls = PartGather(p, small, small_out, pairs[0], local.at[0])
    rows_in = TensorGather(p, x, x_buf, pairs[1], local.at[1])
    smalls.forward()
    rows_in.forward()
    gates = PartGather(p, gate, gate_out, pairs[2], local.at[2])
    smalls.spread()
    ups = PartGather(p, up, up_out, pairs[3], local.at[3])
    smalls.finish()
    pick = (lax.broadcasted_iota(jnp.int32, (8, 128), 0) == lax.broadcasted_iota(jnp.int32, (8, 128), 1))
    gains[...] = nt(pick.astype(F32).astype(BF16), small_out[0, :, :, 384:].reshape(WIDTH, 128))
    gates.forward()
    rows_in.finish()
    grads = TensorGather(p, out_grad, grad_out, pairs[4], local.at[4])
    downs = PartGather(p, down, down_out, pairs[5], local.at[5])
    qkv_weight = small_out[0, :, :, :256].reshape(WIDTH, 256)

    def project(i, carry):
        rows = pl.ds(pl.multiple_of(i * ROWS, ROWS), ROWS)
        state = x_buf[i].astype(F32)
        scale = lax.rsqrt(jnp.mean(state * state, axis=-1, keepdims=True) + NORM_EPSILON)
        normed_rows = (state * scale * gains[0:1]).astype(BF16)
        normed[rows] = normed_rows
        pre = nn(normed_rows, qkv_weight)
        qkv[rows, :128] = rotate(pre[:, :128], tables[0, rows], tables[1, rows]).astype(BF16)
        qkv[rows, 128:] = rotate(pre[:, 128:], tables[2, rows], tables[3, rows]).astype(BF16)
        return carry

    lax.fori_loop(0, 8, project, 0)
    ups.forward()
    grads.forward()
    doubled(qkv[:, 128:], keys, values)
    out_weight = small_out[0, :, :, 256:384].reshape(WIDTH, 128)
    for b in range(WIDTH // QBLOCK):
        length = (b + 1) * QBLOCK
        rows = pl.ds(b * QBLOCK, QBLOCK)
        scores = masked(nt(stacked(qkv[rows, :128]), keys[:length]) * ATT_SCALE, b * QBLOCK)
        peak = jnp.max(scores, axis=-1, keepdims=True)
        terms = jnp.exp(scores - peak)
        total = jnp.sum(terms, axis=-1, keepdims=True)
        log_total[b] = peak + jnp.log(total)
        out = unstacked(nn((terms / total).astype(BF16), values[:length])).astype(BF16)
        attended[rows] = out
        partial[2 * b : 2 * b + 2] = nt(out, out_weight).astype(BF16).reshape(2, ROWS, WIDTH)
    branch = TensorScatter(p, partial, *branch_scratch)
    gates.spread()
    downs.forward()
    branch.exchange()
    ups.spread()
    branch.arrive()

    def step(i, carry):
        rows = pl.ds(pl.multiple_of(i * 32, 32), 32)
        state = x[rows].astype(F32) + RES_SCALE * branch.rows(rows)
        hidden[rows] = state
        scale = lax.rsqrt(jnp.mean(state * state, axis=-1, keepdims=True) + NORM_EPSILON)
        normed_two[rows] = (state * scale * gains[1:2]).astype(BF16)
        return carry

    lax.fori_loop(0, ROWS // 32, step, 0)
    gather = TensorGather(p, normed_two, normed_out, pairs[6], local.at[6])
    gather.forward()
    downs.spread()
    branch.finish()
    gather.finish()
    grads.finish()
    gates.finish()
    ups.finish()
    downs.finish()


def forward(x, small, gate, up, down, out_grad, tables):
    full = shape((4, 16, PART, UNITS))
    rows = shape((8, ROWS, WIDTH))
    return pl.pallas_call(
        forward_kernel,
        out_shape=(
            shape((ROWS, WIDTH), F32), rows, rows, full, full, full, shape((WIDTH, WIDTH)), shape((WIDTH, 256)),
            shape((WIDTH, 128)), shape((WIDTH // QBLOCK, 2 * QBLOCK, 1), F32), shape((1, 16, PART, UNITS)),
            shape((8, WIDTH), F32)),
        in_specs=[VMEM, VMEM, ANY, ANY, ANY, ANY, VMEM],
        out_specs=(VMEM,) + (ANY,) * 5 + (VMEM,) * 6,
        scratch_shapes=[
            pltpu.VMEM((8, ROWS, WIDTH), BF16), pltpu.VMEM((WIDTH, 128), BF16), pltpu.VMEM((WIDTH, 128), BF16),
            pltpu.VMEM((8, ROWS, WIDTH), BF16), pltpu.VMEM((ROWS, WIDTH), BF16)]
        + TensorScatter.scratch() + sems(15) + sems(7) + sems(15) + sems(15) + sems(7) + sems(15) + sems(7)
        + [DMA((7,))],
        compiler_params=params(1, 56), name="forward",
    )(x, small, gate, up, down, out_grad, tables)


def norm_pull(state, gain, grad):
    r = lax.rsqrt(jnp.mean(state * state, axis=-1, keepdims=True) + NORM_EPSILON)
    u = state * r
    w = gain * grad
    return r * (w - u * jnp.mean(w * u, axis=-1, keepdims=True)), jnp.sum(grad * u, axis=0, keepdims=True)


def backward_kernel(
    rows_partial, gate_grads, up_grads, down_grads, hidden, gains_in, out_grad, x, normed, qkv, attended, log_total,
    small, tables,
    input_grad, gate_out, up_out, down_out, small_out, gains,
    branch, branch_full, state_grad, keys, values, key_grad, value_grad, pre, partial, small_grads, gain_buf, *scratch,
):
    p = Place()
    meet(p)
    sums, scratch = scratch[:5], scratch[5:]
    more_sums, scratch = scratch[:5], scratch[5:]
    parts = [scratch[7 * i : 7 * i + 7] for i in range(4)]
    ts, tr, gs, gr, local = scratch[28:]
    rows_sum = TensorScatter(p, rows_partial, *sums)
    gates = PartScatter(p, gate_grads, *parts[0])
    ups = PartScatter(p, up_grads, *parts[1])
    downs = PartScatter(p, down_grads, *parts[2])
    doubled(qkv[:, 128:], keys, values)
    key_grad[...] = jnp.zeros_like(key_grad)
    value_grad[...] = jnp.zeros_like(value_grad)
    gains[...] = jnp.zeros_like(gains)
    gates.along()
    rows_sum.exchange()
    rows_sum.arrive()

    def step(i, carry):
        rows = pl.ds(pl.multiple_of(i * 32, 32), 32)
        pulled, part = norm_pull(hidden[rows], gains_in[1:2], rows_sum.rows(rows))
        gains[1:2] += part
        state = out_grad[rows].astype(F32) + pulled
        state_grad[rows] = state
        branch[rows] = (RES_SCALE * state).astype(BF16)
        return carry

    lax.fori_loop(0, ROWS // 32, step, 0)
    gather = TensorGather(p, branch, branch_full, (ts, tr), local.at[0])
    ups.along()
    gather.forward()
    downs.along()
    rows_sum.finish()
    gates.pair()
    gather.finish()

    out_weight = small[0, :, :, 256:384].reshape(WIDTH, 128)
    for b in range(WIDTH // QBLOCK):
        length = (b + 1) * QBLOCK
        rows = pl.ds(b * QBLOCK, QBLOCK)
        grad = stacked(nn(branch_full[2 * b : 2 * b + 2].reshape(QBLOCK, WIDTH), out_weight).astype(BF16))
        query = stacked(qkv[rows, :128])
        scores = masked(nt(query, keys[:length]) * ATT_SCALE, b * QBLOCK)
        probs = jnp.exp(scores - log_total[b])
        value_grad[:length] += tn(probs.astype(BF16), grad)
        weight_grad = nt(grad, values[:length])
        inner = jnp.sum(weight_grad * probs, axis=-1, keepdims=True)
        score_grad = (probs * (weight_grad - inner)).astype(BF16)
        key_grad[:length] += tn(score_grad, query)
        query_grad = unstacked(nn(score_grad, keys[:length])) * ATT_SCALE
        pre[rows, :128] = rotate(query_grad, tables[0, rows], -tables[1, rows]).astype(BF16)
    ups.pair()
    low = lanes(WIDTH) < HEAD_SIZE
    key_sum = key_grad[...] + pltpu.roll(key_grad[...], HEAD_SIZE, 1)
    value_sum = value_grad[...] + pltpu.roll(value_grad[...], HEAD_SIZE, 1)
    kv_grad = jnp.where(low, key_sum * ATT_SCALE, value_sum)
    pre[:, 128:] = rotate(kv_grad, tables[2], -tables[3]).astype(BF16)

    qkv_weight = small[0, :, :, :256].reshape(WIDTH, 256)

    def give(b, carry):
        rows = pl.ds(pl.multiple_of(b * QBLOCK, QBLOCK), QBLOCK)
        partial[pl.ds(2 * b, 2)] = nt(pre[rows], qkv_weight).astype(BF16).reshape(2, ROWS, WIDTH)
        return carry

    lax.fori_loop(0, WIDTH // QBLOCK, give, 0)
    input_sum = TensorScatter(p, partial, *more_sums)

    def weigh(i, carry):
        columns = pl.ds(pl.multiple_of(i * 256, 256), 256)
        of_qkv = tn(normed[:, columns], pre[...]).astype(BF16)
        of_out = tn(branch_full[:, :, columns].reshape(WIDTH, 256), attended[...]).astype(BF16)
        for r in range(4):
            z = (i % 2) * 2 + r // 2
            part = slice(r * PART, r * PART + PART)
            small_grads[0, i // 2, z, r % 2, :, :256] = of_qkv[part]
            small_grads[0, i // 2, z, r % 2, :, 256:384] = of_out[part]
            small_grads[0, i // 2, z, r % 2, :, 384:] = jnp.zeros((PART, 128), BF16)
        return carry

    lax.fori_loop(0, 4, weigh, 0)
    smalls = PartScatter(p, small_grads, *parts[3])
    downs.pair()
    smalls.along()
    gates.finish(gate_out)
    ups.finish(up_out)
    input_sum.exchange()
    input_sum.arrive()

    def last(i, carry):
        rows = pl.ds(pl.multiple_of(i * 32, 32), 32)
        pulled, part = norm_pull(x[rows].astype(F32), gains_in[0:1], input_sum.rows(rows))
        gains[0:1] += part
        input_grad[rows] = (state_grad[rows] + pulled).astype(BF16)
        return carry

    lax.fori_loop(0, ROWS // 32, last, 0)

    number = 0
    copies = []
    stages = (
        [p.x_dev(j) for j in range(1, NX)], [p.tensor_pair()], [p.core_dev()],
        [p.z_dev(j) for j in range(1, NZ)], [p.y_dev()])
    between = (smalls.pair, lambda: downs.finish(down_out), lambda: smalls.finish(small_out), None, None)
    for stage, (devices, work) in enumerate(zip(stages, between)):
        gain_buf[9 + stage] = gains[...]
        now = [push(gain_buf.at[9 + stage], gain_buf.at[number + k], (gs, gr), number + k, device)
               for k, device in enumerate(devices)]
        if work is not None:
            work()
        for k, copy in enumerate(now):
            copy.wait_recv()
            gains[...] += gain_buf[number + k]
        number += len(devices)
        copies += now
    input_sum.finish()
    for copy in copies:
        copy.wait_send()


def backward(rows_partial, gate_grads, up_grads, down_grads, *rest):
    weight = shape((4, PART, UNITS), F32)
    return pl.pallas_call(
        backward_kernel,
        out_shape=(
            shape((ROWS, WIDTH)), weight, weight, weight, shape((1, PART, UNITS), F32), shape((8, WIDTH), F32)),
        in_specs=[ANY] * 4 + [VMEM] * 10, out_specs=(VMEM,) * 6,
        scratch_shapes=[
            pltpu.VMEM((ROWS, WIDTH), BF16), pltpu.VMEM((8, ROWS, WIDTH), BF16), pltpu.VMEM((ROWS, WIDTH), F32),
            pltpu.VMEM((WIDTH, 128), BF16), pltpu.VMEM((WIDTH, 128), BF16),
            pltpu.VMEM((WIDTH, 128), F32), pltpu.VMEM((WIDTH, 128), F32), pltpu.VMEM((WIDTH, 256), BF16),
            pltpu.VMEM((8, ROWS, WIDTH), BF16), pltpu.VMEM((1, 2, NZ, 2, PART, UNITS), BF16),
            pltpu.VMEM((14, 8, WIDTH), F32)]
        + TensorScatter.scratch() * 2 + PartScatter.scratch(4) * 3 + PartScatter.scratch(1)
        + sems(7) + sems(9) + [DMA((1,))],
        compiler_params=params(2, 60), name="backward",
    )(rows_partial, gate_grads, up_grads, down_grads, *rest)


def rotary_tables(length):
    half_width = HEAD_SIZE // 2
    positions = jnp.arange(length).astype(F32)
    frequencies = jnp.power(ROPE_BASE, -(jnp.arange(half_width).astype(F32) * 2.0 / HEAD_SIZE))
    angles = positions[:, None] * frequencies[None, :]
    cosine, sine = jnp.cos(angles), jnp.sin(angles)
    cosine = jnp.concatenate([cosine, cosine], axis=1)
    sine = jnp.concatenate([-sine, sine], axis=1)
    return jnp.stack([
        jnp.concatenate([cosine, cosine], axis=1), jnp.concatenate([sine, sine], axis=1),
        jnp.concatenate([cosine, jnp.ones_like(cosine)], axis=1),
        jnp.concatenate([sine, jnp.zeros_like(sine)], axis=1)])


def mm(a, b, spec):
    return jnp.einsum(spec, a, b, preferred_element_type=F32)


def local(
    inputs, first_gain, query_weight, key_matrix, value_matrix, output_weight, second_gain,
    gate_weight, up_weight, down_weight, expert_ids, gate_values, out_grad,
):
    rank = lax.axis_index("tensor")
    rows = inputs.shape[0] * lax.axis_size("tensor")
    experts = gate_weight.shape[0]
    qw = query_weight.shape[1]
    kw = key_matrix.shape[1]
    tables = rotary_tables(rows)

    small = jnp.concatenate(
        [query_weight, key_matrix, value_matrix, output_weight.T, first_gain[:, None], second_gain[:, None],
         jnp.zeros((PART, 126), BF16)], axis=1)
    (hidden, normed_two, out_grad_full, gate_full, up_full, down_full, normed, qkv, attended, log_total, small,
     gains) = forward(inputs, small[None], gate_weight, up_weight, jnp.swapaxes(down_weight, 1, 2), out_grad, tables)
    normed_two = normed_two.reshape(rows, WIDTH)
    out_grad_full = out_grad_full.reshape(rows, WIDTH)
    gate_full = gate_full.reshape(experts, WIDTH, UNITS)
    up_full = up_full.reshape(experts, WIDTH, UNITS)
    down_full = down_full.reshape(experts, WIDTH, UNITS)

    expert_index = rank * experts + jnp.arange(experts, dtype=jnp.int32)
    combined = jnp.sum(
        jnp.where(expert_ids[:, :, None] == expert_index, gate_values[:, :, None], 0.0), axis=1)
    gate = mm(normed_two, gate_full, "sd,edf->esf")
    up = mm(normed_two, up_full, "sd,edf->esf")
    sig = jax.nn.sigmoid(gate)
    scale = combined.T[:, :, None]
    hidden_units = (scale * (gate * sig * up)).astype(BF16)
    moe_partial = mm(hidden_units, down_full, "esf,edf->sd")
    moe_local = lax.psum_scatter(
        moe_partial.astype(BF16), "tensor", scatter_dimension=0, tiled=True).astype(F32)
    block_output = (hidden + RES_SCALE * moe_local).astype(BF16)
    hidden_grad = mm(out_grad_full, down_full, "sd,edf->esf") * (RES_SCALE * scale)
    gate_pre = (hidden_grad * up * sig * (1.0 + gate * (1.0 - sig))).astype(BF16)
    up_pre = (hidden_grad * gate * sig).astype(BF16)
    rows_grad = mm(gate_pre, gate_full, "esf,edf->sd") + mm(up_pre, up_full, "esf,edf->sd")
    gate_grad = mm(normed_two, gate_pre, "sd,esf->edf").astype(BF16)
    up_grad = mm(normed_two, up_pre, "sd,esf->edf").astype(BF16)
    down_grad = (mm(out_grad_full, hidden_units, "sd,esf->edf") * RES_SCALE).astype(BF16)
    parts = (experts, 2, NZ, 2, PART, UNITS)
    input_grad, gate_grad, up_grad, down_grad, small_grad, gains = backward(
        rows_grad.astype(BF16).reshape(-1, ROWS, WIDTH), gate_grad.reshape(parts), up_grad.reshape(parts),
        down_grad.reshape(parts), hidden, gains, out_grad, inputs, normed, qkv, attended, log_total, small, tables)
    small_grad = small_grad[0]
    gains = lax.dynamic_slice_in_dim(gains, lax.axis_index("dp") * PART, PART, 1)
    return (
        block_output,
        input_grad,
        gains[0],
        small_grad[:, :qw],
        small_grad[:, qw : qw + kw],
        small_grad[:, qw + kw : qw + 2 * kw],
        small_grad[:, qw + 2 * kw : 2 * qw + 2 * kw].T,
        gains[1],
        gate_grad,
        up_grad,
        jnp.swapaxes(down_grad, 1, 2),
    )


def solution(mesh):
    in_specs = (
        P(("dp", "tensor"), None),
        P("dp"),
        P("dp", "tensor"),
        P("dp", "tensor"),
        P("dp", "tensor"),
        P("tensor", "dp"),
        P("dp"),
        P("tensor", "dp", None),
        P("tensor", "dp", None),
        P("tensor", None, "dp"),
        P("dp", None),
        P("dp", None),
        P(("dp", "tensor"), None),
    )
    out_specs = (
        P(("dp", "tensor"), None),
        P(("dp", "tensor"), None),
        P("dp"),
        P("dp", "tensor"),
        P("dp", "tensor"),
        P("dp", "tensor"),
        P("tensor", "dp"),
        P("dp"),
        P("tensor", "dp", None),
        P("tensor", "dp", None),
        P("tensor", None, "dp"),
    )
    return jax.shard_map(local, mesh=mesh, in_specs=in_specs, out_specs=out_specs, check_vma=False)
```

```python
import functools

import jax
import jax.numpy as jnp
from jax import lax
from jax.experimental import pallas as pl
from jax.experimental.pallas import tpu as pltpu
from jax.sharding import PartitionSpec as P

HEAD_SIZE = 64
NORM_EPSILON = 1e-06
ATT_SCALE = 0.015625
RES_SCALE = 0.22
ROPE_BASE = 10000.0
NEG_FILL = -1e30
F32 = jnp.float32
BF16 = jnp.bfloat16
MESH = pl.DeviceIdType.MESH
NX, NY, NZ, NCORE = 4, 2, 4, 2
ROWS, WIDTH, PART, UNITS = 128, 1024, 64, 512
QBLOCK = 256
ANY = pl.BlockSpec(memory_space=pl.ANY)
VMEM = pl.BlockSpec(memory_space=pltpu.VMEM)
DMA = pltpu.SemaphoreType.DMA


class Place:
    def __init__(self):
        d, t = lax.axis_index("dp"), lax.axis_index("tensor")
        self.d, self.t = d, t
        self.tx, self.ty = t // NY, t % NY
        self.dy, self.dz, self.dc = d // (NZ * NCORE), (d // NCORE) % NZ, d % NCORE
        self.pair = self.tx * NY + (1 - self.ty)
        self.d_pair = self.dp(1 - self.dy, self.dz, self.dc)

    def dp(self, y, z, core):
        return (y * NZ + z) * NCORE + core

    def tensor_pair(self):
        return (self.d, self.pair)

    def x(self, j):
        return (self.tx + j) % NX

    def x_dev(self, j):
        return (self.d, self.x(j) * NY + self.ty)

    def z(self, j):
        return (self.dz + j) % NZ

    def z_dev(self, j):
        return (self.dp(self.dy, self.z(j), self.dc), self.t)

    def y_dev(self):
        return (self.d_pair, self.t)

    def core_dev(self):
        return (self.dp(self.dy, self.dz, 1 - self.dc), self.t)


def meet(p):
    barrier = pltpu.get_barrier_semaphore()
    others = [p.tensor_pair(), p.y_dev(), p.core_dev()]
    others += [p.x_dev(j) for j in range(1, NX)] + [p.z_dev(j) for j in range(1, NZ)]
    for other in others:
        pl.semaphore_signal(barrier, inc=1, device_id=other, device_id_type=MESH)
    pl.semaphore_wait(barrier, len(others))


def push(src, dst, sems, number, device):
    copy = pltpu.make_async_remote_copy(
        src_ref=src, dst_ref=dst, send_sem=sems[0].at[number], recv_sem=sems[1].at[number],
        device_id=device, device_id_type=MESH)
    copy.start()
    return copy


def sems(number):
    return [DMA((number,)), DMA((number,))]


class TensorGather:
    SEMS = 7

    def __init__(self, p, src, out, sem, local_sem):
        self.p, self.out, self.sem = p, out, sem
        self.copies = [push(src, out.at[p.t], sem, 0, p.tensor_pair())]
        self.copies += [push(src, out.at[p.t], sem, j, p.x_dev(j)) for j in range(1, NX)]
        self.own = pltpu.make_async_copy(src, out.at[p.t], local_sem)
        self.own.start()

    def forward(self):
        p = self.p
        self.copies[0].wait_recv()
        self.copies += [
            push(self.out.at[p.pair], self.out.at[p.pair], self.sem, 3 + j, p.x_dev(j)) for j in range(1, NX)]

    def finish(self):
        for copy in self.copies[1:]:
            copy.wait_recv()
        for copy in self.copies:
            copy.wait_send()
        self.own.wait()


class TensorScatter:
    SEMS = 7

    @staticmethod
    def scratch():
        return [pltpu.VMEM((NX, NY, ROWS, WIDTH), BF16), pltpu.VMEM((2, ROWS, WIDTH), BF16)] + sems(7) + [DMA((1,))]

    def __init__(self, p, partial, got, pair_buf, send, recv, local):
        self.p, self.got, self.pair_buf = p, got, pair_buf
        self.sem = (send, recv)
        self.copies = []
        for half, c in enumerate((1 - p.ty, p.ty)):
            self.copies.append([
                push(partial.at[p.x(j) * NY + c], got.at[j, c], self.sem, half * 3 + j - 1, p.x_dev(j))
                for j in range(1, NX)])
        self.own = pltpu.make_async_copy(partial.at[pl.ds(p.tx * NY, NY)], got.at[0], local.at[0])
        self.own.start()

    def total(self, c, rows):
        value = self.got[0, c, rows].astype(F32)
        for j in range(1, NX):
            value = value + self.got[j, c, rows].astype(F32)
        return value

    def exchange(self):
        p = self.p
        self.own.wait()
        for copy in self.copies[0]:
            copy.wait_recv()

        def step(i, carry):
            rows = pl.ds(pl.multiple_of(i * 32, 32), 32)
            self.pair_buf[0, rows] = self.total(1 - p.ty, rows).astype(BF16)
            return carry

        lax.fori_loop(0, ROWS // 32, step, 0)
        self.pair = push(self.pair_buf.at[0], self.pair_buf.at[1], self.sem, 6, p.tensor_pair())

    def arrive(self):
        for copy in self.copies[1]:
            copy.wait_recv()
        self.pair.wait_recv()

    def rows(self, rows):
        return self.total(self.p.ty, rows) + self.pair_buf[1, rows].astype(F32)

    def finish(self):
        for copy in self.copies[0] + self.copies[1] + [self.pair]:
            copy.wait_send()


class PartGather:
    SEMS = 15

    def __init__(self, p, shard, out, sem, local_sem):
        self.p, self.out, self.sem = p, out, sem
        mine = out.at[:, p.d]
        self.pair = push(shard, mine, sem, 0, p.y_dev())
        self.along = [push(shard, mine, sem, j, p.z_dev(j)) for j in range(1, NZ)]
        self.core = [push(shard, mine, sem, 4, p.core_dev())]
        self.own = pltpu.make_async_copy(shard, mine, local_sem)
        self.own.start()

    def resend(self, index, number, device):
        return push(self.out.at[:, index], self.out.at[:, index], self.sem, number, device)

    def forward(self):
        p = self.p
        self.pair.wait_recv()
        self.along_pair = [self.resend(p.d_pair, 4 + j, p.z_dev(j)) for j in range(1, NZ)]
        self.core.append(self.resend(p.d_pair, 8, p.core_dev()))

    def spread(self):
        p = self.p
        for first, copies, y in ((9, self.along, p.dy), (12, self.along_pair, 1 - p.dy)):
            for j in range(1, NZ):
                copies[j - 1].wait_recv()
                index = p.dp(y, (p.dz + NZ - j) % NZ, p.dc)
                self.core.append(self.resend(index, first + j - 1, p.core_dev()))

    def finish(self):
        for copy in self.core:
            copy.wait_recv()
        for copy in [self.pair] + self.along + self.along_pair + self.core:
            copy.wait_send()
        self.own.wait()


class PartScatter:
    @staticmethod
    def scratch(n):
        return [
            pltpu.VMEM((n, 2, NZ, 2, PART, UNITS), BF16),
            pltpu.VMEM((n, 2, NZ, PART, UNITS), BF16),
            pltpu.VMEM((NZ - 1, n, 2, PART, UNITS), BF16),
            pltpu.VMEM((2, n, PART, UNITS), BF16),
        ] + sems(5)

    def __init__(self, p, grads, core_buf, z_buf, y_buf, send, recv):
        self.p, self.n = p, grads.shape[0]
        self.grads, self.core_buf, self.z_buf, self.y_buf = grads, core_buf, z_buf, y_buf
        self.sem = (send, recv)
        self.core = push(grads.at[:, :, :, 1 - p.dc], core_buf, self.sem, 0, p.core_dev())

    def along(self):
        p = self.p
        self.core.wait_recv()

        def step(i, carry):
            for y in range(2):
                for z in range(NZ):
                    total = self.grads[i, y, z, p.dc].astype(F32) + self.core_buf[i, y, z].astype(F32)
                    self.grads[i, y, z, p.dc] = total.astype(BF16)
            return carry

        lax.fori_loop(0, self.n, step, 0)
        self.z_copies = [
            push(self.grads.at[:, :, p.z(j), p.dc], self.z_buf.at[j - 1], self.sem, j, p.z_dev(j))
            for j in range(1, NZ)]

    def total(self, i, y):
        value = self.grads[i, y, self.p.dz, self.p.dc].astype(F32)
        for j in range(NZ - 1):
            value = value + self.z_buf[j, i, y].astype(F32)
        return value

    def pair(self):
        p = self.p
        for copy in self.z_copies:
            copy.wait_recv()

        def step(i, carry):
            self.y_buf[0, i] = self.total(i, 1 - p.dy).astype(BF16)
            return carry

        lax.fori_loop(0, self.n, step, 0)
        self.y_copy = push(self.y_buf.at[0], self.y_buf.at[1], self.sem, 4, p.y_dev())

    def finish(self, outs):
        p = self.p
        self.y_copy.wait_recv()
        for i, (out, slot) in enumerate(outs):
            out[slot] = self.total(i, p.dy) + self.y_buf[1, i].astype(F32)
        for copy in [self.core, self.y_copy] + self.z_copies:
            copy.wait_send()


def params(number, megabytes):
    return pltpu.CompilerParams(
        collective_id=number, has_side_effects=True, vmem_limit_bytes=megabytes << 20)


def shape(dims, dtype=BF16):
    return jax.ShapeDtypeStruct(dims, dtype)


def nn(a, b):
    return lax.dot_general(a, b, (((1,), (0,)), ((), ())), preferred_element_type=F32)


def nt(a, b):
    return lax.dot_general(a, b, (((1,), (1,)), ((), ())), preferred_element_type=F32)


def tn(a, b):
    return lax.dot_general(a, b, (((0,), (0,)), ((), ())), preferred_element_type=F32)


def lanes(rows):
    return lax.broadcasted_iota(jnp.int32, (rows, 2 * HEAD_SIZE), 1)


def rotate(pair, cosine, sine):
    first = lanes(pair.shape[0]) % HEAD_SIZE < HEAD_SIZE // 2
    other = jnp.where(first, pltpu.roll(pair, 3 * HEAD_SIZE // 2, 1), pltpu.roll(pair, HEAD_SIZE // 2, 1))
    return pair * cosine + other * sine


def stacked(pair):
    low = lanes(pair.shape[0]) < HEAD_SIZE
    zero = jnp.zeros_like(pair)
    return jnp.concatenate([jnp.where(low, pair, zero), jnp.where(low, zero, pair)], axis=0)


def unstacked(both):
    rows = both.shape[0] // 2
    return jnp.where(lanes(rows) < HEAD_SIZE, both[:rows], both[rows:])


def masked(scores, first_row):
    rows = lax.broadcasted_iota(jnp.int32, scores.shape, 0) % QBLOCK + first_row
    columns = lax.broadcasted_iota(jnp.int32, scores.shape, 1)
    return jnp.where(columns <= rows, scores, NEG_FILL)


def doubled(kv, keys, values):
    low = lanes(kv.shape[0]) < HEAD_SIZE
    kv = kv.astype(F32)
    swapped = pltpu.roll(kv, HEAD_SIZE, 1)
    keys[...] = jnp.where(low, kv, swapped).astype(BF16)
    values[...] = jnp.where(low, swapped, kv).astype(BF16)


def forward_kernel(
    x, small, gate, up, down, out_grad, tables,
    hidden, normed_out, grad_out, gate_out, up_out, down_out, normed, qkv, attended, log_total, small_out, gains,
    x_buf, keys, values, partial, normed_two, *scratch,
):
    p = Place()
    meet(p)
    branch_scratch, scratch = scratch[:5], scratch[5:]
    pairs = [scratch[2 * i : 2 * i + 2] for i in range(7)]
    local = scratch[14]
    smalls = PartGather(p, small, small_out, pairs[0], local.at[0])
    rows_in = TensorGather(p, x, x_buf, pairs[1], local.at[1])
    smalls.forward()
    rows_in.forward()
    gates = PartGather(p, gate, gate_out, pairs[2], local.at[2])
    smalls.spread()
    ups = PartGather(p, up, up_out, pairs[3], local.at[3])
    smalls.finish()
    pick = (lax.broadcasted_iota(jnp.int32, (8, 128), 0) == lax.broadcasted_iota(jnp.int32, (8, 128), 1))
    gains[...] = nt(pick.astype(F32).astype(BF16), small_out[0, :, :, 384:].reshape(WIDTH, 128))
    gates.forward()
    rows_in.finish()
    grads = TensorGather(p, out_grad, grad_out, pairs[4], local.at[4])
    downs = PartGather(p, down, down_out, pairs[5], local.at[5])
    qkv_weight = small_out[0, :, :, :256].reshape(WIDTH, 256)

    def project(i, carry):
        rows = pl.ds(pl.multiple_of(i * ROWS, ROWS), ROWS)
        state = x_buf[i].astype(F32)
        scale = lax.rsqrt(jnp.mean(state * state, axis=-1, keepdims=True) + NORM_EPSILON)
        normed_rows = (state * scale * gains[0:1]).astype(BF16)
        normed[rows] = normed_rows
        pre = nn(normed_rows, qkv_weight)
        qkv[rows, :128] = rotate(pre[:, :128], tables[0, rows], tables[1, rows]).astype(BF16)
        qkv[rows, 128:] = rotate(pre[:, 128:], tables[2, rows], tables[3, rows]).astype(BF16)
        return carry

    lax.fori_loop(0, 8, project, 0)
    ups.forward()
    grads.forward()
    doubled(qkv[:, 128:], keys, values)
    out_weight = small_out[0, :, :, 256:384].reshape(WIDTH, 128)
    for b in range(WIDTH // QBLOCK):
        length = (b + 1) * QBLOCK
        rows = pl.ds(b * QBLOCK, QBLOCK)
        scores = masked(nt(stacked(qkv[rows, :128]), keys[:length]) * ATT_SCALE, b * QBLOCK)
        peak = jnp.max(scores, axis=-1, keepdims=True)
        terms = jnp.exp(scores - peak)
        total = jnp.sum(terms, axis=-1, keepdims=True)
        log_total[b] = peak + jnp.log(total)
        out = unstacked(nn((terms / total).astype(BF16), values[:length])).astype(BF16)
        attended[rows] = out
        partial[2 * b : 2 * b + 2] = nt(out, out_weight).astype(BF16).reshape(2, ROWS, WIDTH)
    branch = TensorScatter(p, partial, *branch_scratch)
    gates.spread()
    downs.forward()
    branch.exchange()
    ups.spread()
    branch.arrive()

    def step(i, carry):
        rows = pl.ds(pl.multiple_of(i * 32, 32), 32)
        state = x[rows].astype(F32) + RES_SCALE * branch.rows(rows)
        hidden[rows] = state
        scale = lax.rsqrt(jnp.mean(state * state, axis=-1, keepdims=True) + NORM_EPSILON)
        normed_two[rows] = (state * scale * gains[1:2]).astype(BF16)
        return carry

    lax.fori_loop(0, ROWS // 32, step, 0)
    gather = TensorGather(p, normed_two, normed_out, pairs[6], local.at[6])
    gather.forward()
    downs.spread()
    branch.finish()
    gather.finish()
    grads.finish()
    gates.finish()
    ups.finish()
    downs.finish()


def forward(x, small, gate, up, down, out_grad, tables):
    full = shape((4, 16, PART, UNITS))
    rows = shape((8, ROWS, WIDTH))
    return pl.pallas_call(
        forward_kernel,
        out_shape=(
            shape((ROWS, WIDTH), F32), rows, rows, full, full, full, shape((WIDTH, WIDTH)), shape((WIDTH, 256)),
            shape((WIDTH, 128)), shape((WIDTH // QBLOCK, 2 * QBLOCK, 1), F32), shape((1, 16, PART, UNITS)),
            shape((8, WIDTH), F32)),
        in_specs=[VMEM, VMEM, ANY, ANY, ANY, ANY, VMEM],
        out_specs=(VMEM,) + (ANY,) * 5 + (VMEM,) * 6,
        scratch_shapes=[
            pltpu.VMEM((8, ROWS, WIDTH), BF16), pltpu.VMEM((WIDTH, 128), BF16), pltpu.VMEM((WIDTH, 128), BF16),
            pltpu.VMEM((8, ROWS, WIDTH), BF16), pltpu.VMEM((ROWS, WIDTH), BF16)]
        + TensorScatter.scratch() + sems(15) + sems(7) + sems(15) + sems(15) + sems(7) + sems(15) + sems(7)
        + [DMA((7,))],
        compiler_params=params(1, 56), name="forward",
    )(x, small, gate, up, down, out_grad, tables)


def norm_pull(state, gain, grad):
    r = lax.rsqrt(jnp.mean(state * state, axis=-1, keepdims=True) + NORM_EPSILON)
    u = state * r
    w = gain * grad
    return r * (w - u * jnp.mean(w * u, axis=-1, keepdims=True)), jnp.sum(grad * u, axis=0, keepdims=True)


def experts_kernel(
    x, out_grad_full, gate, up, down, combined, hidden, gains_in, out_grad,
    moe_out, branch_out, state_grad, gain_part, gate_out, up_out, down_out,
    gate_buf, up_buf, down_buf, moe, rows_acc, units, gate_pre, up_pre, rows_out, branch, *scratch,
):
    p = Place()
    load_sem, scratch = scratch[0], scratch[1:]
    sums, scratch = scratch[:5], scratch[5:]
    parts = [scratch[6 * e : 6 * e + 6] for e in range(4)]
    ts, tr, local = scratch[24:]

    def load(e):
        slot = e % 2
        return [
            pltpu.make_async_copy(ref.at[e], buf.at[slot], load_sem.at[slot, k])
            for k, (ref, buf) in enumerate(((gate, gate_buf), (up, up_buf), (down, down_buf)))]

    loads = load(0)
    for copy in loads:
        copy.start()
    meet(p)
    gain_part[...] = jnp.zeros_like(gain_part)
    scatters = []
    for e in range(4):
        slot = e % 2
        for copy in loads:
            copy.wait()
        if e < 3:
            loads = load(e + 1)
            for copy in loads:
                copy.start()

        def block(i, carry):
            rows = pl.ds(pl.multiple_of(i * QBLOCK, QBLOCK), QBLOCK)
            tokens = x[rows]
            gate_part = nn(tokens, gate_buf[slot])
            up_part = nn(tokens, up_buf[slot])
            sig = 0.5 * jnp.tanh(0.5 * gate_part) + 0.5
            act = gate_part * sig
            scale = combined[rows, e : e + 1]
            unit = (scale * (act * up_part)).astype(BF16)
            grad = nn(out_grad_full[rows], down_buf[slot]) * (RES_SCALE * scale)
            to_gate = (grad * up_part * (sig + act * (1.0 - sig))).astype(BF16)
            to_up = (grad * act).astype(BF16)
            units[rows] = unit
            gate_pre[rows] = to_gate
            up_pre[rows] = to_up
            moe_part = nt(unit, down_buf[slot])
            rows_part = nt(to_gate, gate_buf[slot]) + nt(to_up, up_buf[slot])
            if e == 0:
                moe[rows] = moe_part
                rows_acc[rows] = rows_part
            elif e < 3:
                moe[rows] += moe_part
                rows_acc[rows] += rows_part
            else:
                blocks = pl.ds(2 * i, 2)
                moe_out[blocks] = (moe[rows] + moe_part).astype(BF16).reshape(2, ROWS, WIDTH)
                rows_out[blocks] = (rows_acc[rows] + rows_part).astype(BF16).reshape(2, ROWS, WIDTH)
            return carry

        lax.fori_loop(0, WIDTH // QBLOCK, block, 0)
        if e == 3:
            rows_sum = TensorScatter(p, rows_out, *sums)
        if e >= 1:
            scatters[e - 1].along()
        grads = parts[e][0]

        def weigh(i, carry):
            columns = pl.ds(pl.multiple_of(i * 256, 256), 256)
            tokens = x[:, columns]
            found = (
                tn(tokens, gate_pre[...]), tn(tokens, up_pre[...]),
                tn(out_grad_full[:, columns], units[...]) * RES_SCALE)
            for k in range(3):
                for r in range(4):
                    z = (i % 2) * 2 + r // 2
                    grads[k, i // 2, z, r % 2] = found[k][r * PART : r * PART + PART].astype(BF16)
            return carry

        lax.fori_loop(0, 4, weigh, 0)
        scatters.append(PartScatter(p, *parts[e]))

    rows_sum.exchange()
    scatters[3].along()
    scatters[0].pair()
    rows_sum.arrive()

    def step(i, carry):
        rows = pl.ds(pl.multiple_of(i * 32, 32), 32)
        pulled, part = norm_pull(hidden[rows], gains_in[1:2], rows_sum.rows(rows))
        gain_part[1:2] += part
        state = out_grad[rows].astype(F32) + pulled
        state_grad[rows] = state
        branch[rows] = (RES_SCALE * state).astype(BF16)
        return carry

    lax.fori_loop(0, ROWS // 32, step, 0)
    gather = TensorGather(p, branch, branch_out, (ts, tr), local.at[0])
    scatters[1].pair()
    gather.forward()
    scatters[2].pair()
    scatters[0].finish(((gate_out, 0), (up_out, 0), (down_out, 0)))
    scatters[1].finish(((gate_out, 1), (up_out, 1), (down_out, 1)))
    scatters[3].pair()
    scatters[2].finish(((gate_out, 2), (up_out, 2), (down_out, 2)))
    scatters[3].finish(((gate_out, 3), (up_out, 3), (down_out, 3)))
    rows_sum.finish()
    gather.finish()


def run_experts(*args):
    weight = shape((4, PART, UNITS), F32)
    rows = shape((8, ROWS, WIDTH))
    return pl.pallas_call(
        experts_kernel,
        out_shape=(rows, rows, shape((ROWS, WIDTH), F32), shape((8, WIDTH), F32), weight, weight, weight),
        in_specs=[VMEM, VMEM, ANY, ANY, ANY] + [VMEM] * 4, out_specs=(VMEM, ANY) + (VMEM,) * 5,
        scratch_shapes=[pltpu.VMEM((2, WIDTH, UNITS), BF16)] * 3 + [pltpu.VMEM((WIDTH, WIDTH), F32)] * 2
        + [pltpu.VMEM((WIDTH, UNITS), BF16)] * 3
        + [pltpu.VMEM((8, ROWS, WIDTH), BF16), pltpu.VMEM((ROWS, WIDTH), BF16), DMA((2, 3))]
        + TensorScatter.scratch() + PartScatter.scratch(3) * 4 + sems(7) + [DMA((1,))],
        compiler_params=params(2, 62), name="experts",
    )(*args)


def backward_kernel(
    moe_partial, branch_full, state_grad, gain_part, hidden, gains_in, x, normed, qkv, attended, log_total, small,
    tables,
    block_out, input_grad, small_out, gains,
    keys, values, key_grad, value_grad, pre, partial, gain_buf, *scratch,
):
    p = Place()
    meet(p)
    sums, scratch = scratch[:5], scratch[5:]
    more_sums, scratch = scratch[:5], scratch[5:]
    part = scratch[:6]
    small_grads = part[0]
    gs, gr = scratch[6:]
    moe_sum = TensorScatter(p, moe_partial, *sums)
    doubled(qkv[:, 128:], keys, values)
    key_grad[...] = jnp.zeros_like(key_grad)
    value_grad[...] = jnp.zeros_like(value_grad)
    gains[...] = gain_part[...]

    out_weight = small[0, :, :, 256:384].reshape(WIDTH, 128)
    for b in range(WIDTH // QBLOCK):
        length = (b + 1) * QBLOCK
        rows = pl.ds(b * QBLOCK, QBLOCK)
        grad = stacked(nn(branch_full[2 * b : 2 * b + 2].reshape(QBLOCK, WIDTH), out_weight).astype(BF16))
        query = stacked(qkv[rows, :128])
        scores = masked(nt(query, keys[:length]) * ATT_SCALE, b * QBLOCK)
        probs = jnp.exp(scores - log_total[b])
        value_grad[:length] += tn(probs.astype(BF16), grad)
        weight_grad = nt(grad, values[:length])
        inner = jnp.sum(weight_grad * probs, axis=-1, keepdims=True)
        score_grad = (probs * (weight_grad - inner)).astype(BF16)
        key_grad[:length] += tn(score_grad, query)
        query_grad = unstacked(nn(score_grad, keys[:length])) * ATT_SCALE
        pre[rows, :128] = rotate(query_grad, tables[0, rows], -tables[1, rows]).astype(BF16)
    low = lanes(WIDTH) < HEAD_SIZE
    key_sum = key_grad[...] + pltpu.roll(key_grad[...], HEAD_SIZE, 1)
    value_sum = value_grad[...] + pltpu.roll(value_grad[...], HEAD_SIZE, 1)
    kv_grad = jnp.where(low, key_sum * ATT_SCALE, value_sum)
    pre[:, 128:] = rotate(kv_grad, tables[2], -tables[3]).astype(BF16)

    qkv_weight = small[0, :, :, :256].reshape(WIDTH, 256)

    def give(b, carry):
        rows = pl.ds(pl.multiple_of(b * QBLOCK, QBLOCK), QBLOCK)
        partial[pl.ds(2 * b, 2)] = nt(pre[rows], qkv_weight).astype(BF16).reshape(2, ROWS, WIDTH)
        return carry

    lax.fori_loop(0, WIDTH // QBLOCK, give, 0)
    input_sum = TensorScatter(p, partial, *more_sums)
    moe_sum.exchange()

    def weigh(i, carry):
        columns = pl.ds(pl.multiple_of(i * 256, 256), 256)
        of_qkv = tn(normed[:, columns], pre[...]).astype(BF16)
        of_out = tn(branch_full[:, :, columns].reshape(WIDTH, 256), attended[...]).astype(BF16)
        for r in range(4):
            z = (i % 2) * 2 + r // 2
            piece = slice(r * PART, r * PART + PART)
            small_grads[0, i // 2, z, r % 2, :, :256] = of_qkv[piece]
            small_grads[0, i // 2, z, r % 2, :, 256:384] = of_out[piece]
            small_grads[0, i // 2, z, r % 2, :, 384:] = jnp.zeros((PART, 128), BF16)
        return carry

    lax.fori_loop(0, 4, weigh, 0)
    smalls = PartScatter(p, *part)
    moe_sum.arrive()

    def give_block(i, carry):
        rows = pl.ds(pl.multiple_of(i * 32, 32), 32)
        block_out[rows] = (hidden[rows] + RES_SCALE * moe_sum.rows(rows)).astype(BF16)
        return carry

    lax.fori_loop(0, ROWS // 32, give_block, 0)
    smalls.along()
    input_sum.exchange()
    input_sum.arrive()

    def last(i, carry):
        rows = pl.ds(pl.multiple_of(i * 32, 32), 32)
        pulled, found = norm_pull(x[rows].astype(F32), gains_in[0:1], input_sum.rows(rows))
        gains[0:1] += found
        input_grad[rows] = (state_grad[rows] + pulled).astype(BF16)
        return carry

    lax.fori_loop(0, ROWS // 32, last, 0)

    number = 0
    copies = []
    stages = (
        [p.x_dev(j) for j in range(1, NX)], [p.tensor_pair()], [p.core_dev()],
        [p.z_dev(j) for j in range(1, NZ)], [p.y_dev()])
    between = (smalls.pair, lambda: smalls.finish(((small_out, 0),)), None, None, None)
    for stage, (devices, work) in enumerate(zip(stages, between)):
        gain_buf[9 + stage] = gains[...]
        now = [push(gain_buf.at[9 + stage], gain_buf.at[number + k], (gs, gr), number + k, device)
               for k, device in enumerate(devices)]
        if work is not None:
            work()
        for k, copy in enumerate(now):
            copy.wait_recv()
            gains[...] += gain_buf[number + k]
        number += len(devices)
        copies += now
    moe_sum.finish()
    input_sum.finish()
    for copy in copies:
        copy.wait_send()


def backward(*args):
    rows = shape((ROWS, WIDTH))
    return pl.pallas_call(
        backward_kernel,
        out_shape=(rows, rows, shape((1, PART, UNITS), F32), shape((8, WIDTH), F32)),
        in_specs=[ANY] + [VMEM] * 12, out_specs=(VMEM,) * 4,
        scratch_shapes=[
            pltpu.VMEM((WIDTH, 128), BF16), pltpu.VMEM((WIDTH, 128), BF16),
            pltpu.VMEM((WIDTH, 128), F32), pltpu.VMEM((WIDTH, 128), F32), pltpu.VMEM((WIDTH, 256), BF16),
            pltpu.VMEM((8, ROWS, WIDTH), BF16), pltpu.VMEM((14, 8, WIDTH), F32)]
        + TensorScatter.scratch() * 2 + PartScatter.scratch(1) + sems(9),
        compiler_params=params(3, 56), name="backward",
    )(*args)


def rotary_tables(length):
    half_width = HEAD_SIZE // 2
    positions = jnp.arange(length).astype(F32)
    frequencies = jnp.power(ROPE_BASE, -(jnp.arange(half_width).astype(F32) * 2.0 / HEAD_SIZE))
    angles = positions[:, None] * frequencies[None, :]
    cosine, sine = jnp.cos(angles), jnp.sin(angles)
    cosine = jnp.concatenate([cosine, cosine], axis=1)
    sine = jnp.concatenate([-sine, sine], axis=1)
    return jnp.stack([
        jnp.concatenate([cosine, cosine], axis=1), jnp.concatenate([sine, sine], axis=1),
        jnp.concatenate([cosine, jnp.ones_like(cosine)], axis=1),
        jnp.concatenate([sine, jnp.zeros_like(sine)], axis=1)])


def local(
    inputs, first_gain, query_weight, key_matrix, value_matrix, output_weight, second_gain,
    gate_weight, up_weight, down_weight, expert_ids, gate_values, out_grad,
):
    rank = lax.axis_index("tensor")
    rows = inputs.shape[0] * lax.axis_size("tensor")
    experts = gate_weight.shape[0]
    qw = query_weight.shape[1]
    kw = key_matrix.shape[1]
    tables = rotary_tables(rows)

    small = jnp.concatenate(
        [query_weight, key_matrix, value_matrix, output_weight.T, first_gain[:, None], second_gain[:, None],
         jnp.zeros((PART, 126), BF16)], axis=1)
    (hidden, normed_two, out_grad_full, gate_full, up_full, down_full, normed, qkv, attended, log_total, small,
     gains) = forward(inputs, small[None], gate_weight, up_weight, jnp.swapaxes(down_weight, 1, 2), out_grad, tables)
    normed_two = normed_two.reshape(rows, WIDTH)
    out_grad_full = out_grad_full.reshape(rows, WIDTH)
    gate_full = gate_full.reshape(experts, WIDTH, UNITS)
    up_full = up_full.reshape(experts, WIDTH, UNITS)
    down_full = down_full.reshape(experts, WIDTH, UNITS)

    expert_index = rank * experts + jnp.arange(experts, dtype=jnp.int32)
    combined = jnp.sum(
        jnp.where(expert_ids[:, :, None] == expert_index, gate_values[:, :, None], 0.0), axis=1)
    moe_partial, branch_full, state_grad, gain_part, gate_grad, up_grad, down_grad = run_experts(
        normed_two, out_grad_full, gate_full, up_full, down_full, combined, hidden, gains, out_grad)
    block_output, input_grad, small_grad, gains = backward(
        moe_partial, branch_full, state_grad, gain_part, hidden, gains, inputs, normed, qkv, attended, log_total,
        small, tables)
    small_grad = small_grad[0]
    gains = lax.dynamic_slice_in_dim(gains, lax.axis_index("dp") * PART, PART, 1)
    return (
        block_output,
        input_grad,
        gains[0],
        small_grad[:, :qw],
        small_grad[:, qw : qw + kw],
        small_grad[:, qw + kw : qw + 2 * kw],
        small_grad[:, qw + 2 * kw : 2 * qw + 2 * kw].T,
        gains[1],
        gate_grad,
        up_grad,
        jnp.swapaxes(down_grad, 1, 2),
    )


def solution(mesh):
    in_specs = (
        P(("dp", "tensor"), None),
        P("dp"),
        P("dp", "tensor"),
        P("dp", "tensor"),
        P("dp", "tensor"),
        P("tensor", "dp"),
        P("dp"),
        P("tensor", "dp", None),
        P("tensor", "dp", None),
        P("tensor", None, "dp"),
        P("dp", None),
        P("dp", None),
        P(("dp", "tensor"), None),
    )
    out_specs = (
        P(("dp", "tensor"), None),
        P(("dp", "tensor"), None),
        P("dp"),
        P("dp", "tensor"),
        P("dp", "tensor"),
        P("dp", "tensor"),
        P("tensor", "dp"),
        P("dp"),
        P("tensor", "dp", None),
        P("tensor", "dp", None),
        P("tensor", None, "dp"),
    )
    return jax.shard_map(local, mesh=mesh, in_specs=in_specs, out_specs=out_specs, check_vma=False)
```

```python
import functools

import jax
import jax.numpy as jnp
import numpy as np
from jax import lax
from jax.experimental import pallas as pl
from jax.experimental.pallas import tpu as pltpu
from jax.sharding import PartitionSpec as P

HEAD_SIZE = 64
NORM_EPSILON = 1e-06
ATT_SCALE = 0.015625
RES_SCALE = 0.22
ROPE_BASE = 10000.0
NEG_FILL = -1e30
F32 = jnp.float32
BF16 = jnp.bfloat16
MESH = pl.DeviceIdType.MESH
NX, NY, NZ, NCORE = 4, 2, 4, 2
ROWS, WIDTH, PART, UNITS = 128, 1024, 64, 512
QBLOCK = 256
ANY = pl.BlockSpec(memory_space=pl.ANY)
VMEM = pl.BlockSpec(memory_space=pltpu.VMEM)
DMA = pltpu.SemaphoreType.DMA


class Place:
    def __init__(self):
        d, t = lax.axis_index("dp"), lax.axis_index("tensor")
        self.d, self.t = d, t
        self.tx, self.ty = t // NY, t % NY
        self.dy, self.dz, self.dc = d // (NZ * NCORE), (d // NCORE) % NZ, d % NCORE
        self.pair = self.tx * NY + (1 - self.ty)
        self.d_pair = self.dp(1 - self.dy, self.dz, self.dc)

    def dp(self, y, z, core):
        return (y * NZ + z) * NCORE + core

    def tensor_pair(self):
        return (self.d, self.pair)

    def x(self, j):
        return (self.tx + j) % NX

    def x_dev(self, j):
        return (self.d, self.x(j) * NY + self.ty)

    def z(self, j):
        return (self.dz + j) % NZ

    def z_dev(self, j):
        return (self.dp(self.dy, self.z(j), self.dc), self.t)

    def y_dev(self):
        return (self.d_pair, self.t)

    def core_dev(self):
        return (self.dp(self.dy, self.dz, 1 - self.dc), self.t)


def meet(p):
    barrier = pltpu.get_barrier_semaphore()
    others = [p.tensor_pair(), p.y_dev(), p.core_dev()]
    others += [p.x_dev(j) for j in range(1, NX)] + [p.z_dev(j) for j in range(1, NZ)]
    for other in others:
        pl.semaphore_signal(barrier, inc=1, device_id=other, device_id_type=MESH)
    pl.semaphore_wait(barrier, len(others))


def push(src, dst, sems, number, device):
    copy = pltpu.make_async_remote_copy(
        src_ref=src, dst_ref=dst, send_sem=sems[0].at[number], recv_sem=sems[1].at[number],
        device_id=device, device_id_type=MESH)
    copy.start()
    return copy


def sems(number):
    return [DMA((number,)), DMA((number,))]


class TensorGather:
    SEMS = 9

    def __init__(self, p, src, out, sem, local_sem):
        self.p, self.out, self.sem = p, out, sem
        self.copies = [push(src, out.at[p.t], sem, 0, p.tensor_pair())]
        self.copies += [push(src, out.at[p.t], sem, 1 + k, p.x_dev(j)) for k, j in enumerate((1, 3))]
        self.own = pltpu.make_async_copy(src, out.at[p.t], local_sem)
        self.own.start()

    def resend(self, block, number, j):
        self.copies.append(push(block, block, self.sem, number, self.p.x_dev(j)))

    def forward(self):
        self.copies[0].wait_recv()
        for k, j in enumerate((1, 3)):
            self.resend(self.out.at[self.p.pair], 3 + k, j)

    def relay(self):
        p = self.p
        for k, (back, on) in enumerate(((3, 1), (1, 3))):
            for c, first in ((p.ty, 1), (1 - p.ty, 3)):
                self.copies[first + k].wait_recv()
                half = self.out.at[p.x(back) * NY + c, pl.ds(k * (ROWS // 2), ROWS // 2)]
                self.resend(half, 4 + first + k, on)

    def arrive(self):
        for copy in self.copies[5:]:
            copy.wait_recv()

    def sent(self):
        for copy in self.copies:
            copy.wait_send()

    def finish(self):
        self.arrive()
        self.sent()
        self.own.wait()


class TensorScatter:
    STEPS = (2, 1, 3)

    @staticmethod
    def scratch():
        half = pltpu.VMEM((2, NY, ROWS // 2, WIDTH), BF16)
        return [pltpu.VMEM((3, NY, ROWS, WIDTH), BF16), half, half, pltpu.VMEM((2, ROWS, WIDTH), BF16)] + sems(13) + [
            DMA((1,))]

    def __init__(self, p, partial, got, via, merged, pair_buf, send, recv, local):
        self.p, self.partial, self.got, self.pair_buf = p, partial, got, pair_buf
        self.via, self.merged = via, merged
        self.sem = (send, recv)
        self.own = pltpu.make_async_copy(partial.at[pl.ds(p.tx * NY, NY)], got.at[2], local.at[0])

    def half(self, k):
        return pl.ds(k * (ROWS // 2), ROWS // 2)

    def copy(self, kind, k, order):
        p = self.p
        c = p.ty if order else 1 - p.ty
        number = kind * 4 + order * 2 + k
        j = (1, 3)[k]
        if kind == 0:
            src, dst = self.partial.at[p.x(2) * NY + c, self.half(k)], self.via.at[k, c]
        elif kind == 1:
            src, dst = self.partial.at[p.x(j) * NY + c, self.half(1 - k)], self.got.at[k, c, self.half(1 - k)]
        else:
            src, dst = self.merged.at[k, c], self.got.at[k, c, self.half(k)]
        return pltpu.make_async_remote_copy(
            src_ref=src, dst_ref=dst, send_sem=self.sem[0].at[number], recv_sem=self.sem[1].at[number],
            device_id=p.x_dev(j), device_id_type=MESH)

    def send(self, j):
        for order in range(2):
            if j == 2:
                self.copy(0, 0, order).start()
                self.copy(0, 1, order).start()
            else:
                self.copy(1, (1, 3).index(j), order).start()

    def row(self, step):
        return self.p.x((2 + 3 * step + 3 * (step // 2) + 2 * (step // 3)) % NX)

    def send_after(self, step):
        for number, j in enumerate(self.STEPS):
            pl.when(step == number)(functools.partial(self.send, j))

    def send_all(self):
        for j in self.STEPS:
            self.send(j)
        self.own.start()

    def relay(self):
        p = self.p
        for order in range(2):
            c = p.ty if order else 1 - p.ty
            for k in range(2):
                self.copy(0, k, order).wait_recv()
                block = p.x((1, 3)[k]) * NY + c

                def step(i, carry):
                    rows = pl.ds(pl.multiple_of(i * 32, 32), 32)
                    mine = self.partial[block, pl.ds(pl.multiple_of(k * (ROWS // 2) + i * 32, 32), 32)]
                    self.merged[k, c, rows] = (mine.astype(F32) + self.via[k, c, rows].astype(F32)).astype(BF16)
                    return carry

                lax.fori_loop(0, ROWS // 64, step, 0)
                self.copy(2, k, order).start()

    def total(self, c, rows):
        value = self.got[0, c, rows].astype(F32)
        for k in range(1, 3):
            value = value + self.got[k, c, rows].astype(F32)
        return value

    def wait_near(self, order):
        for k in range(2):
            self.copy(1, k, order).wait_recv()
            self.copy(2, k, order).wait_recv()

    def exchange(self):
        p = self.p
        self.own.wait()
        self.wait_near(0)

        def step(i, carry):
            rows = pl.ds(pl.multiple_of(i * 32, 32), 32)
            self.pair_buf[0, rows] = self.total(1 - p.ty, rows).astype(BF16)
            return carry

        lax.fori_loop(0, ROWS // 32, step, 0)
        self.pair = push(self.pair_buf.at[0], self.pair_buf.at[1], self.sem, 12, p.tensor_pair())

    def arrive(self):
        self.wait_near(1)
        self.pair.wait_recv()

    def rows(self, rows):
        return self.total(self.p.ty, rows) + self.pair_buf[1, rows].astype(F32)

    def finish(self):
        for kind in range(3):
            for order in range(2):
                for k in range(2):
                    self.copy(kind, k, order).wait_send()
        self.pair.wait_send()


class PartGather:
    SEMS = 17

    def __init__(self, p, shard, out, sem, local_sem):
        self.p, self.out, self.sem = p, out, sem
        mine = out.at[:, p.d]
        self.copies = [push(shard, mine, sem, 0, p.y_dev())]
        self.copies += [push(shard, mine, sem, 1 + k, p.z_dev(j)) for k, j in enumerate((1, 3))]
        self.core = [push(shard, mine, sem, 3, p.core_dev())]
        self.halves = []
        self.own = pltpu.make_async_copy(shard, mine, local_sem)
        self.own.start()

    def resend(self, block, number, device):
        return push(block, block, self.sem, number, device)

    def forward(self):
        p = self.p
        self.copies[0].wait_recv()
        block = self.out.at[:, p.d_pair]
        self.copies += [self.resend(block, 4 + k, p.z_dev(j)) for k, j in enumerate((1, 3))]
        self.core.append(self.resend(block, 6, p.core_dev()))

    def index(self, j, pair):
        p = self.p
        return p.dp(1 - p.dy if pair else p.dy, p.z(j), p.dc)

    def spread(self):
        p = self.p
        for pair in range(2):
            for k, (back, on) in enumerate(((3, 1), (1, 3))):
                self.copies[1 + 2 * pair + k].wait_recv()
                index = self.index(back, pair)
                half = self.out.at[:, index, pl.ds(k * (PART // 2), PART // 2)]
                self.halves.append(self.resend(half, 7 + 2 * pair + k, p.z_dev(on)))
                self.core.append(self.resend(self.out.at[:, index], 11 + 2 * pair + k, p.core_dev()))

    def far(self):
        p = self.p
        for copy in self.halves:
            copy.wait_recv()
        self.core += [
            self.resend(self.out.at[:, self.index(2, pair)], 15 + pair, p.core_dev()) for pair in range(2)]

    def finish(self):
        for copy in self.core:
            copy.wait_recv()
        for copy in self.copies + self.halves + self.core:
            copy.wait_send()
        self.own.wait()


class PartScatter:
    @staticmethod
    def scratch(n):
        return [
            pltpu.VMEM((n, 2, NZ, 2, PART, UNITS), BF16),
            pltpu.VMEM((n, 2, NZ, PART, UNITS), BF16),
            pltpu.VMEM((2, n, 2, PART, UNITS), BF16),
            pltpu.VMEM((2, n, 2, PART // 2, UNITS), BF16),
            pltpu.VMEM((2, n, PART, UNITS), BF16),
        ] + sems(8)

    def __init__(self, p, grads, core_buf, z_buf, via, y_buf, send, recv):
        self.p, self.n = p, grads.shape[0]
        self.grads, self.core_buf, self.z_buf, self.via, self.y_buf = grads, core_buf, z_buf, via, y_buf
        self.sem = (send, recv)
        self.core = push(grads.at[:, :, :, 1 - p.dc], core_buf, self.sem, 0, p.core_dev())

    def half(self, k):
        return pl.ds(k * (PART // 2), PART // 2)

    def copy(self, kind, k):
        p = self.p
        j = (1, 3)[k]
        if kind == 0:
            src, dst = self.grads.at[:, :, p.z(2), p.dc, self.half(k)], self.via.at[k]
        else:
            half = self.half(1 - k if kind == 1 else k)
            src, dst = self.grads.at[:, :, p.z(j), p.dc, half], self.z_buf.at[k, :, :, half]
        number = 1 + kind * 2 + k
        return pltpu.make_async_remote_copy(
            src_ref=src, dst_ref=dst, send_sem=self.sem[0].at[number], recv_sem=self.sem[1].at[number],
            device_id=p.z_dev(j), device_id_type=MESH)

    def along(self):
        p = self.p
        self.core.wait_recv()

        def step(i, carry):
            for y in range(2):
                for z in range(NZ):
                    total = self.grads[i, y, z, p.dc].astype(F32) + self.core_buf[i, y, z].astype(F32)
                    self.grads[i, y, z, p.dc] = total.astype(BF16)
            return carry

        lax.fori_loop(0, self.n, step, 0)
        for kind in range(2):
            for k in range(2):
                self.copy(kind, k).start()

    def relay(self):
        p = self.p
        for k, j in enumerate((1, 3)):
            self.copy(0, k).wait_recv()
            z = p.z(j)

            def step(i, carry):
                for y in range(2):
                    total = self.grads[i, y, z, p.dc, self.half(k)].astype(F32) + self.via[k, i, y].astype(F32)
                    self.grads[i, y, z, p.dc, self.half(k)] = total.astype(BF16)
                return carry

            lax.fori_loop(0, self.n, step, 0)
            self.copy(2, k).start()

    def total(self, i, y):
        value = self.grads[i, y, self.p.dz, self.p.dc].astype(F32)
        for k in range(2):
            value = value + self.z_buf[k, i, y].astype(F32)
        return value

    def pair(self):
        p = self.p
        for kind in (1, 2):
            for k in range(2):
                self.copy(kind, k).wait_recv()

        def step(i, carry):
            self.y_buf[0, i] = self.total(i, 1 - p.dy).astype(BF16)
            return carry

        lax.fori_loop(0, self.n, step, 0)
        self.y_copy = push(self.y_buf.at[0], self.y_buf.at[1], self.sem, 7, p.y_dev())

    def finish(self, outs):
        p = self.p
        self.y_copy.wait_recv()
        for i, (out, slot) in enumerate(outs):
            out[slot] = self.total(i, p.dy) + self.y_buf[1, i].astype(F32)
        for copy in [self.core, self.y_copy] + [self.copy(kind, k) for kind in range(3) for k in range(2)]:
            copy.wait_send()


def params(number, megabytes):
    return pltpu.CompilerParams(
        collective_id=number, has_side_effects=True, vmem_limit_bytes=megabytes << 20)


def shape(dims, dtype=BF16):
    return jax.ShapeDtypeStruct(dims, dtype)


def nn(a, b):
    return lax.dot_general(a, b, (((1,), (0,)), ((), ())), preferred_element_type=F32)


def nt(a, b):
    return lax.dot_general(a, b, (((1,), (1,)), ((), ())), preferred_element_type=F32)


def tn(a, b):
    return lax.dot_general(a, b, (((0,), (0,)), ((), ())), preferred_element_type=F32)


def lanes(rows):
    return lax.broadcasted_iota(jnp.int32, (rows, 2 * HEAD_SIZE), 1)


def rotate(pair, cosine, sine):
    first = lanes(pair.shape[0]) % HEAD_SIZE < HEAD_SIZE // 2
    other = jnp.where(first, pltpu.roll(pair, 3 * HEAD_SIZE // 2, 1), pltpu.roll(pair, HEAD_SIZE // 2, 1))
    return pair * cosine + other * sine


def stacked(pair):
    low = lanes(pair.shape[0]) < HEAD_SIZE
    zero = jnp.zeros_like(pair)
    return jnp.concatenate([jnp.where(low, pair, zero), jnp.where(low, zero, pair)], axis=0)


def unstacked(both):
    rows = both.shape[0] // 2
    return jnp.where(lanes(rows) < HEAD_SIZE, both[:rows], both[rows:])


def masked(scores, first_row):
    rows = lax.broadcasted_iota(jnp.int32, scores.shape, 0) % QBLOCK + first_row
    columns = lax.broadcasted_iota(jnp.int32, scores.shape, 1)
    return jnp.where(columns <= rows, scores, NEG_FILL)


def doubled(kv, keys, values):
    low = lanes(kv.shape[0]) < HEAD_SIZE
    kv = kv.astype(F32)
    swapped = pltpu.roll(kv, HEAD_SIZE, 1)
    keys[...] = jnp.where(low, kv, swapped).astype(BF16)
    values[...] = jnp.where(low, swapped, kv).astype(BF16)


def forward_kernel(
    x, small, gate, up, down, out_grad, tables,
    hidden, normed_out, grad_out, gate_out, up_out, down_out, normed, qkv, attended, log_total, small_out, gains,
    x_buf, keys, values, partial, normed_two, *scratch,
):
    p = Place()
    meet(p)
    branch_scratch, scratch = scratch[:7], scratch[7:]
    pairs = [scratch[2 * i : 2 * i + 2] for i in range(7)]
    local = scratch[14]
    smalls = PartGather(p, small, small_out, pairs[0], local.at[0])
    rows_in = TensorGather(p, x, x_buf, pairs[1], local.at[1])
    smalls.forward()
    rows_in.forward()
    gates = PartGather(p, gate, gate_out, pairs[2], local.at[2])
    smalls.spread()
    smalls.far()
    ups = PartGather(p, up, up_out, pairs[3], local.at[3])
    downs = PartGather(p, down, down_out, pairs[5], local.at[5])
    smalls.finish()
    pick = (lax.broadcasted_iota(jnp.int32, (8, 128), 0) == lax.broadcasted_iota(jnp.int32, (8, 128), 1))
    gains[...] = nt(pick.astype(F32).astype(BF16), small_out[0, :, :, 384:].reshape(WIDTH, 128))
    gates.forward()
    qkv_weight = small_out[0, :, :, :256].reshape(WIDTH, 256)

    def project(i, carry):
        rows = pl.ds(pl.multiple_of(i * ROWS, ROWS), ROWS)
        state = x_buf[i].astype(F32)
        scale = lax.rsqrt(jnp.mean(state * state, axis=-1, keepdims=True) + NORM_EPSILON)
        normed_rows = (state * scale * gains[0:1]).astype(BF16)
        normed[rows] = normed_rows
        pre = nn(normed_rows, qkv_weight)
        qkv[rows, :128] = rotate(pre[:, :128], tables[0, rows], tables[1, rows]).astype(BF16)
        qkv[rows, 128:] = rotate(pre[:, 128:], tables[2, rows], tables[3, rows]).astype(BF16)
        return carry

    rows_in.own.wait()
    lax.fori_loop(p.tx * NY, p.tx * NY + NY, project, 0)
    ups.forward()
    rows_in.relay()
    grads = TensorGather(p, out_grad, grad_out, pairs[4], local.at[4])
    for j in (1, 3, 2):
        if j == 2:
            rows_in.arrive()
            downs.forward()
            grads.forward()
        start = p.x(j) * NY
        lax.fori_loop(start, start + NY, project, 0)
    doubled(qkv[:, 128:], keys, values)
    out_weight = small_out[0, :, :, 256:384].reshape(WIDTH, 128)
    branch = TensorScatter(p, partial, *branch_scratch)
    for b in range(WIDTH // QBLOCK):
        length = (b + 1) * QBLOCK
        rows = pl.ds(b * QBLOCK, QBLOCK)
        scores = masked(nt(stacked(qkv[rows, :128]), keys[:length]) * ATT_SCALE, b * QBLOCK)
        peak = jnp.max(scores, axis=-1, keepdims=True)
        terms = jnp.exp(scores - peak)
        total = jnp.sum(terms, axis=-1, keepdims=True)
        log_total[b] = peak + jnp.log(total)
        out = unstacked(nn((terms / total).astype(BF16), values[:length])).astype(BF16)
        attended[rows] = out
        partial[2 * b : 2 * b + 2] = nt(out, out_weight).astype(BF16).reshape(2, ROWS, WIDTH)
        for j in range(1, NX):
            pl.when(p.x(j) == b)(functools.partial(branch.send, j))
        if b == 1:
            grads.relay()
            gates.spread()
    branch.own.start()
    branch.relay()
    ups.spread()
    gates.far()
    branch.exchange()
    downs.spread()
    branch.arrive()

    def step(i, carry):
        rows = pl.ds(pl.multiple_of(i * 32, 32), 32)
        state = x[rows].astype(F32) + RES_SCALE * branch.rows(rows)
        hidden[rows] = state
        scale = lax.rsqrt(jnp.mean(state * state, axis=-1, keepdims=True) + NORM_EPSILON)
        normed_two[rows] = (state * scale * gains[1:2]).astype(BF16)
        return carry

    lax.fori_loop(0, ROWS // 32, step, 0)
    gather = TensorGather(p, normed_two, normed_out, pairs[6], local.at[6])
    gather.forward()
    ups.far()
    gather.relay()
    downs.far()
    branch.finish()
    gather.finish()
    rows_in.sent()
    grads.finish()
    gates.finish()
    ups.finish()
    downs.finish()


def forward(x, small, gate, up, down, out_grad, tables):
    full = shape((4, 16, PART, UNITS))
    rows = shape((8, ROWS, WIDTH))
    return pl.pallas_call(
        forward_kernel,
        out_shape=(
            shape((ROWS, WIDTH), F32), rows, rows, full, full, full, shape((WIDTH, WIDTH)), shape((WIDTH, 256)),
            shape((WIDTH, 128)), shape((WIDTH // QBLOCK, 2 * QBLOCK, 1), F32), shape((1, 16, PART, UNITS)),
            shape((8, WIDTH), F32)),
        in_specs=[VMEM, VMEM, ANY, ANY, ANY, ANY, VMEM],
        out_specs=(VMEM,) + (ANY,) * 5 + (VMEM,) * 6,
        scratch_shapes=[
            pltpu.VMEM((8, ROWS, WIDTH), BF16), pltpu.VMEM((WIDTH, 128), BF16), pltpu.VMEM((WIDTH, 128), BF16),
            pltpu.VMEM((8, ROWS, WIDTH), BF16), pltpu.VMEM((ROWS, WIDTH), BF16)]
        + TensorScatter.scratch() + sems(17) + sems(9) + sems(17) + sems(17) + sems(9) + sems(17) + sems(9)
        + [DMA((7,))],
        compiler_params=params(1, 56), name="forward",
    )(x, small, gate, up, down, out_grad, tables)


def norm_pull(state, gain, grad):
    r = lax.rsqrt(jnp.mean(state * state, axis=-1, keepdims=True) + NORM_EPSILON)
    u = state * r
    w = gain * grad
    return r * (w - u * jnp.mean(w * u, axis=-1, keepdims=True)), jnp.sum(grad * u, axis=0, keepdims=True)


def experts_kernel(
    x, out_grad_full, gate, up, down, combined, hidden, gains_in, out_grad,
    moe_out, branch_out, state_grad, gain_part, gate_out, up_out, down_out,
    gate_buf, up_buf, down_buf, moe, rows_acc, units, gate_pre, up_pre, rows_out, branch, *scratch,
):
    p = Place()
    load_sem, scratch = scratch[0], scratch[1:]
    sums, scratch = scratch[:7], scratch[7:]
    parts = [scratch[7 * e : 7 * e + 7] for e in range(4)]
    ts, tr, local = scratch[28:]

    def load(e):
        slot = e % 2
        return [
            pltpu.make_async_copy(ref.at[e], buf.at[slot], load_sem.at[slot, k])
            for k, (ref, buf) in enumerate(((gate, gate_buf), (up, up_buf), (down, down_buf)))]

    loads = load(0)
    for copy in loads:
        copy.start()
    meet(p)
    gain_part[...] = jnp.zeros_like(gain_part)
    scatters = []
    rows_sum = TensorScatter(p, rows_out, *sums)

    def weigh_expert(e):
        grads = parts[e][0]

        def weigh(i, carry):
            columns = pl.ds(pl.multiple_of(i * 256, 256), 256)
            tokens = x[:, columns]
            found = (
                tn(tokens, gate_pre[e % 2]), tn(tokens, up_pre[e % 2]),
                tn(out_grad_full[:, columns], units[e % 2]) * RES_SCALE)
            for k in range(3):
                for r in range(4):
                    z = (i % 2) * 2 + r // 2
                    grads[k, i // 2, z, r % 2] = found[k][r * PART : r * PART + PART].astype(BF16)
            return carry

        lax.fori_loop(0, 4, weigh, 0)
        scatters.append(PartScatter(p, *parts[e]))
        if e == 1:
            scatters[0].relay()
        if e == 3:
            scatters[2].along()

    for e in range(4):
        slot = e % 2
        for copy in loads:
            copy.wait()
        if e < 3:
            loads = load(e + 1)
            for copy in loads:
                copy.start()

        def block(step, carry):
            i = rows_sum.row(step)
            rows = pl.ds(pl.multiple_of(i * QBLOCK, QBLOCK), QBLOCK)
            tokens = x[rows]
            gate_part = nn(tokens, gate_buf[slot])
            up_part = nn(tokens, up_buf[slot])
            sig = 0.5 * jnp.tanh(0.5 * gate_part) + 0.5
            act = gate_part * sig
            scale = combined[rows, e : e + 1]
            unit = (scale * (act * up_part)).astype(BF16)
            grad = nn(out_grad_full[rows], down_buf[slot]) * (RES_SCALE * scale)
            to_gate = (grad * up_part * (sig + act * (1.0 - sig))).astype(BF16)
            to_up = (grad * act).astype(BF16)
            units[slot, rows] = unit
            gate_pre[slot, rows] = to_gate
            up_pre[slot, rows] = to_up
            moe_part = nt(unit, down_buf[slot])
            rows_part = nt(to_gate, gate_buf[slot]) + nt(to_up, up_buf[slot])
            if e == 0:
                moe[rows] = moe_part
                rows_acc[rows] = rows_part
            elif e < 3:
                moe[rows] += moe_part
                rows_acc[rows] += rows_part
            else:
                blocks = pl.ds(2 * i, 2)
                moe_out[blocks] = (moe[rows] + moe_part).astype(BF16).reshape(2, ROWS, WIDTH)
                rows_out[blocks] = (rows_acc[rows] + rows_part).astype(BF16).reshape(2, ROWS, WIDTH)
                rows_sum.send_after(step)
            return carry

        lax.fori_loop(0, WIDTH // QBLOCK, block, 0)
        if e == 1 or e == 2:
            scatters[e - 1].along()
        if e == 3:
            rows_sum.own.start()
            rows_sum.relay()
            scatters[1].relay()
        for done in ((0,), (1,), (), (2, 3))[e]:
            weigh_expert(done)

    scatters[0].pair()
    scatters[3].along()
    scatters[2].relay()
    rows_sum.exchange()
    scatters[1].pair()
    rows_sum.arrive()

    def step(i, carry):
        rows = pl.ds(pl.multiple_of(i * 32, 32), 32)
        pulled, part = norm_pull(hidden[rows], gains_in[1:2], rows_sum.rows(rows))
        gain_part[1:2] += part
        state = out_grad[rows].astype(F32) + pulled
        state_grad[rows] = state
        branch[rows] = (RES_SCALE * state).astype(BF16)
        return carry

    lax.fori_loop(0, ROWS // 32, step, 0)
    gather = TensorGather(p, branch, branch_out, (ts, tr), local.at[0])
    scatters[3].relay()
    gather.forward()
    scatters[2].pair()
    gather.relay()
    scatters[0].finish(((gate_out, 0), (up_out, 0), (down_out, 0)))
    scatters[1].finish(((gate_out, 1), (up_out, 1), (down_out, 1)))
    scatters[3].pair()
    scatters[2].finish(((gate_out, 2), (up_out, 2), (down_out, 2)))
    scatters[3].finish(((gate_out, 3), (up_out, 3), (down_out, 3)))
    rows_sum.finish()
    gather.finish()


def run_experts(*args):
    weight = shape((4, PART, UNITS), F32)
    rows = shape((8, ROWS, WIDTH))
    return pl.pallas_call(
        experts_kernel,
        out_shape=(rows, rows, shape((ROWS, WIDTH), F32), shape((8, WIDTH), F32), weight, weight, weight),
        in_specs=[VMEM, VMEM, ANY, ANY, ANY] + [VMEM] * 4, out_specs=(VMEM, ANY) + (VMEM,) * 5,
        scratch_shapes=[pltpu.VMEM((2, WIDTH, UNITS), BF16)] * 3 + [pltpu.VMEM((WIDTH, WIDTH), F32)] * 2
        + [pltpu.VMEM((2, WIDTH, UNITS), BF16)] * 3
        + [pltpu.VMEM((8, ROWS, WIDTH), BF16), pltpu.VMEM((ROWS, WIDTH), BF16), DMA((2, 3))]
        + TensorScatter.scratch() + PartScatter.scratch(3) * 4 + sems(9) + [DMA((1,))],
        compiler_params=params(2, 63), name="experts",
    )(*args)


def backward_kernel(
    moe_partial, branch_full, state_grad, gain_part, hidden, gains_in, x, normed, qkv, attended, log_total, small,
    tables,
    block_out, input_grad, small_out, gains,
    keys, values, key_grad, value_grad, pre, partial, gain_buf, *scratch,
):
    p = Place()
    meet(p)
    sums, scratch = scratch[:7], scratch[7:]
    more_sums, scratch = scratch[:7], scratch[7:]
    part = scratch[:7]
    small_grads = part[0]
    gs, gr = scratch[7:]
    moe_sum = TensorScatter(p, moe_partial, *sums)
    moe_sum.send_all()
    doubled(qkv[:, 128:], keys, values)
    key_grad[...] = jnp.zeros_like(key_grad)
    value_grad[...] = jnp.zeros_like(value_grad)
    gains[...] = gain_part[...]

    out_weight = small[0, :, :, 256:384].reshape(WIDTH, 128)
    for b in range(WIDTH // QBLOCK):
        if b == 2:
            moe_sum.relay()
        length = (b + 1) * QBLOCK
        rows = pl.ds(b * QBLOCK, QBLOCK)
        grad = stacked(nn(branch_full[2 * b : 2 * b + 2].reshape(QBLOCK, WIDTH), out_weight).astype(BF16))
        query = stacked(qkv[rows, :128])
        scores = masked(nt(query, keys[:length]) * ATT_SCALE, b * QBLOCK)
        probs = jnp.exp(scores - log_total[b])
        value_grad[:length] += tn(probs.astype(BF16), grad)
        weight_grad = nt(grad, values[:length])
        inner = jnp.sum(weight_grad * probs, axis=-1, keepdims=True)
        score_grad = (probs * (weight_grad - inner)).astype(BF16)
        key_grad[:length] += tn(score_grad, query)
        query_grad = unstacked(nn(score_grad, keys[:length])) * ATT_SCALE
        pre[rows, :128] = rotate(query_grad, tables[0, rows], -tables[1, rows]).astype(BF16)
    low = lanes(WIDTH) < HEAD_SIZE
    key_sum = key_grad[...] + pltpu.roll(key_grad[...], HEAD_SIZE, 1)
    value_sum = value_grad[...] + pltpu.roll(value_grad[...], HEAD_SIZE, 1)
    kv_grad = jnp.where(low, key_sum * ATT_SCALE, value_sum)
    pre[:, 128:] = rotate(kv_grad, tables[2], -tables[3]).astype(BF16)

    qkv_weight = small[0, :, :, :256].reshape(WIDTH, 256)

    input_sum = TensorScatter(p, partial, *more_sums)

    def give(step, carry):
        b = input_sum.row(step)
        rows = pl.ds(pl.multiple_of(b * QBLOCK, QBLOCK), QBLOCK)
        found = nt(pre[rows], qkv_weight)
        partial[pl.ds(2 * b, 2)] = found.astype(BF16).reshape(2, ROWS, WIDTH)
        input_sum.send_after(step)
        gains[0:1] += jnp.sum(found * normed[rows].astype(F32), axis=0, keepdims=True)
        return carry

    lax.fori_loop(0, WIDTH // QBLOCK, give, 0)
    input_sum.own.start()
    gains[0:1] = gains[0:1] / gains_in[0:1]

    copies = []
    stages = iter((
        [p.x_dev(j) for j in range(1, NX)], [p.tensor_pair()], [p.core_dev()],
        [p.z_dev(j) for j in range(1, NZ)], [p.y_dev()]))

    def gains_send():
        stage = len(copies)
        first = sum(len(group) for group in copies)
        gain_buf[9 + stage] = gains[...]
        copies.append([
            push(gain_buf.at[9 + stage], gain_buf.at[first + k], (gs, gr), first + k, device)
            for k, device in enumerate(next(stages))])

    def gains_add():
        first = sum(len(group) for group in copies[:-1])
        for k, copy in enumerate(copies[-1]):
            copy.wait_recv()
            gains[...] += gain_buf[first + k]

    gains_send()
    moe_sum.exchange()
    input_sum.relay()

    def weigh(i, carry):
        columns = pl.ds(pl.multiple_of(i * 256, 256), 256)
        of_qkv = tn(normed[:, columns], pre[...]).astype(BF16)
        of_out = tn(branch_full[:, :, columns].reshape(WIDTH, 256), attended[...]).astype(BF16)
        for r in range(4):
            z = (i % 2) * 2 + r // 2
            piece = slice(r * PART, r * PART + PART)
            small_grads[0, i // 2, z, r % 2, :, :256] = of_qkv[piece]
            small_grads[0, i // 2, z, r % 2, :, 256:384] = of_out[piece]
            small_grads[0, i // 2, z, r % 2, :, 384:] = jnp.zeros((PART, 128), BF16)
        return carry

    lax.fori_loop(0, 4, weigh, 0)
    smalls = PartScatter(p, *part)
    gains_add()
    gains_send()
    moe_sum.arrive()

    def give_block(i, carry):
        rows = pl.ds(pl.multiple_of(i * 32, 32), 32)
        block_out[rows] = (hidden[rows] + RES_SCALE * moe_sum.rows(rows)).astype(BF16)
        return carry

    lax.fori_loop(0, ROWS // 32, give_block, 0)
    smalls.along()
    gains_add()
    gains_send()
    smalls.relay()
    input_sum.exchange()
    gains_add()
    gains_send()
    smalls.pair()
    gains_add()
    gains_send()
    input_sum.arrive()

    def last(i, carry):
        rows = pl.ds(pl.multiple_of(i * 32, 32), 32)
        pulled, _ = norm_pull(x[rows].astype(F32), gains_in[0:1], input_sum.rows(rows))
        input_grad[rows] = (state_grad[rows] + pulled).astype(BF16)
        return carry

    lax.fori_loop(0, ROWS // 32, last, 0)
    gains_add()
    smalls.finish(((small_out, 0),))
    moe_sum.finish()
    input_sum.finish()
    for group in copies:
        for copy in group:
            copy.wait_send()


def backward(*args):
    rows = shape((ROWS, WIDTH))
    return pl.pallas_call(
        backward_kernel,
        out_shape=(rows, rows, shape((1, PART, UNITS), F32), shape((8, WIDTH), F32)),
        in_specs=[VMEM] * 13, out_specs=(VMEM,) * 4,
        scratch_shapes=[
            pltpu.VMEM((WIDTH, 128), BF16), pltpu.VMEM((WIDTH, 128), BF16),
            pltpu.VMEM((WIDTH, 128), F32), pltpu.VMEM((WIDTH, 128), F32), pltpu.VMEM((WIDTH, 256), BF16),
            pltpu.VMEM((8, ROWS, WIDTH), BF16), pltpu.VMEM((14, 8, WIDTH), F32)]
        + TensorScatter.scratch() * 2 + PartScatter.scratch(1) + sems(9),
        compiler_params=params(3, 56), name="backward",
    )(*args)


def rotary_tables(length):
    half_width = HEAD_SIZE // 2
    positions = np.arange(length).astype(np.float32)
    frequencies = np.power(
        np.float32(ROPE_BASE), -(np.arange(half_width).astype(np.float32) * np.float32(2.0 / HEAD_SIZE)))
    angles = positions[:, None] * frequencies[None, :]
    cosine, sine = np.cos(angles), np.sin(angles)
    cosine = np.concatenate([cosine, cosine], axis=1)
    sine = np.concatenate([-sine, sine], axis=1)
    return np.stack([
        np.concatenate([cosine, cosine], axis=1), np.concatenate([sine, sine], axis=1),
        np.concatenate([cosine, np.ones_like(cosine)], axis=1),
        np.concatenate([sine, np.zeros_like(sine)], axis=1)]).astype(np.float32)


def local(
    inputs, first_gain, query_weight, key_matrix, value_matrix, output_weight, second_gain,
    gate_weight, up_weight, down_weight, expert_ids, gate_values, out_grad,
):
    rank = lax.axis_index("tensor")
    rows = inputs.shape[0] * lax.axis_size("tensor")
    experts = gate_weight.shape[0]
    qw = query_weight.shape[1]
    kw = key_matrix.shape[1]
    tables = jnp.asarray(rotary_tables(rows))

    small = jnp.concatenate(
        [query_weight, key_matrix, value_matrix, output_weight.T, first_gain[:, None], second_gain[:, None],
         jnp.zeros((PART, 126), BF16)], axis=1)
    (hidden, normed_two, out_grad_full, gate_full, up_full, down_full, normed, qkv, attended, log_total, small,
     gains) = forward(inputs, small[None], gate_weight, up_weight, jnp.swapaxes(down_weight, 1, 2), out_grad, tables)
    normed_two = normed_two.reshape(rows, WIDTH)
    out_grad_full = out_grad_full.reshape(rows, WIDTH)
    gate_full = gate_full.reshape(experts, WIDTH, UNITS)
    up_full = up_full.reshape(experts, WIDTH, UNITS)
    down_full = down_full.reshape(experts, WIDTH, UNITS)

    expert_index = rank * experts + jnp.arange(experts, dtype=jnp.int32)
    combined = jnp.sum(
        jnp.where(expert_ids[:, :, None] == expert_index, gate_values[:, :, None], 0.0), axis=1)
    moe_partial, branch_full, state_grad, gain_part, gate_grad, up_grad, down_grad = run_experts(
        normed_two, out_grad_full, gate_full, up_full, down_full, combined, hidden, gains, out_grad)
    block_output, input_grad, small_grad, gains = backward(
        moe_partial, branch_full, state_grad, gain_part, hidden, gains, inputs, normed, qkv, attended, log_total,
        small, tables)
    small_grad = small_grad[0]
    gains = lax.dynamic_slice_in_dim(gains, lax.axis_index("dp") * PART, PART, 1)
    return (
        block_output,
        input_grad,
        gains[0],
        small_grad[:, :qw],
        small_grad[:, qw : qw + kw],
        small_grad[:, qw + kw : qw + 2 * kw],
        small_grad[:, qw + 2 * kw : 2 * qw + 2 * kw].T,
        gains[1],
        gate_grad,
        up_grad,
        jnp.swapaxes(down_grad, 1, 2),
    )


def solution(mesh):
    in_specs = (
        P(("dp", "tensor"), None),
        P("dp"),
        P("dp", "tensor"),
        P("dp", "tensor"),
        P("dp", "tensor"),
        P("tensor", "dp"),
        P("dp"),
        P("tensor", "dp", None),
        P("tensor", "dp", None),
        P("tensor", None, "dp"),
        P("dp", None),
        P("dp", None),
        P(("dp", "tensor"), None),
    )
    out_specs = (
        P(("dp", "tensor"), None),
        P(("dp", "tensor"), None),
        P("dp"),
        P("dp", "tensor"),
        P("dp", "tensor"),
        P("dp", "tensor"),
        P("tensor", "dp"),
        P("dp"),
        P("tensor", "dp", None),
        P("tensor", "dp", None),
        P("tensor", None, "dp"),
    )
    return jax.shard_map(local, mesh=mesh, in_specs=in_specs, out_specs=out_specs, check_vma=False)
```

```python
import functools

import jax
import jax.numpy as jnp
import numpy as np
from jax import lax
from jax.experimental import pallas as pl
from jax.experimental.pallas import tpu as pltpu
from jax.sharding import PartitionSpec as P

HEAD_SIZE = 64
NORM_EPSILON = 1e-06
ATT_SCALE = 0.015625
RES_SCALE = 0.22
ROPE_BASE = 10000.0
NEG_FILL = -1e30
F32 = jnp.float32
BF16 = jnp.bfloat16
MESH = pl.DeviceIdType.MESH
NX, NY, NZ, NCORE = 4, 2, 4, 2
ROWS, WIDTH, PART, UNITS = 128, 1024, 64, 512
QBLOCK = 256
ANY = pl.BlockSpec(memory_space=pl.ANY)
VMEM = pl.BlockSpec(memory_space=pltpu.VMEM)
DMA = pltpu.SemaphoreType.DMA


class Place:
    def __init__(self):
        d, t = lax.axis_index("dp"), lax.axis_index("tensor")
        self.d, self.t = d, t
        self.tx, self.ty = t // NY, t % NY
        self.dy, self.dz, self.dc = d // (NZ * NCORE), (d // NCORE) % NZ, d % NCORE
        self.pair = self.tx * NY + (1 - self.ty)
        self.d_pair = self.dp(1 - self.dy, self.dz, self.dc)

    def dp(self, y, z, core):
        return (y * NZ + z) * NCORE + core

    def tensor_pair(self):
        return (self.d, self.pair)

    def x(self, j):
        return (self.tx + j) % NX

    def x_dev(self, j):
        return (self.d, self.x(j) * NY + self.ty)

    def z(self, j):
        return (self.dz + j) % NZ

    def z_dev(self, j):
        return (self.dp(self.dy, self.z(j), self.dc), self.t)

    def y_dev(self):
        return (self.d_pair, self.t)

    def core_dev(self):
        return (self.dp(self.dy, self.dz, 1 - self.dc), self.t)


def meet(p):
    barrier = pltpu.get_barrier_semaphore()
    others = [p.tensor_pair(), p.y_dev(), p.core_dev()]
    others += [p.x_dev(j) for j in range(1, NX)] + [p.z_dev(j) for j in range(1, NZ)]
    for other in others:
        pl.semaphore_signal(barrier, inc=1, device_id=other, device_id_type=MESH)
    pl.semaphore_wait(barrier, len(others))


def push(src, dst, sems, number, device):
    copy = pltpu.make_async_remote_copy(
        src_ref=src, dst_ref=dst, send_sem=sems[0].at[number], recv_sem=sems[1].at[number],
        device_id=device, device_id_type=MESH)
    copy.start()
    return copy


def sems(number):
    return [DMA((number,)), DMA((number,))]


class TensorGather:
    SEMS = 9

    def __init__(self, p, src, out, sem, local_sem):
        self.p, self.out, self.sem = p, out, sem
        self.copies = [push(src, out.at[p.t], sem, 0, p.tensor_pair())]
        self.copies += [push(src, out.at[p.t], sem, 1 + k, p.x_dev(j)) for k, j in enumerate((1, 3))]
        self.own = pltpu.make_async_copy(src, out.at[p.t], local_sem)
        self.own.start()

    def resend(self, block, number, j):
        self.copies.append(push(block, block, self.sem, number, self.p.x_dev(j)))

    def forward(self):
        self.copies[0].wait_recv()
        for k, j in enumerate((1, 3)):
            self.resend(self.out.at[self.p.pair], 3 + k, j)

    def relay(self):
        p = self.p
        for k, (back, on) in enumerate(((3, 1), (1, 3))):
            for c, first in ((p.ty, 1), (1 - p.ty, 3)):
                self.copies[first + k].wait_recv()
                half = self.out.at[p.x(back) * NY + c, pl.ds(k * (ROWS // 2), ROWS // 2)]
                self.resend(half, 4 + first + k, on)

    def arrive(self):
        for copy in self.copies[5:]:
            copy.wait_recv()

    def sent(self):
        for copy in self.copies:
            copy.wait_send()

    def finish(self):
        self.arrive()
        self.sent()
        self.own.wait()


class TensorScatter:
    STEPS = (2, 1, 3)

    @staticmethod
    def scratch():
        half = pltpu.VMEM((2, NY, ROWS // 2, WIDTH), BF16)
        return [pltpu.VMEM((3, NY, ROWS, WIDTH), BF16), half, half, pltpu.VMEM((2, ROWS, WIDTH), BF16)] + sems(13) + [
            DMA((1,))]

    def __init__(self, p, partial, got, via, merged, pair_buf, send, recv, local):
        self.p, self.partial, self.got, self.pair_buf = p, partial, got, pair_buf
        self.via, self.merged = via, merged
        self.sem = (send, recv)
        self.own = pltpu.make_async_copy(partial.at[pl.ds(p.tx * NY, NY)], got.at[2], local.at[0])

    def half(self, k):
        return pl.ds(k * (ROWS // 2), ROWS // 2)

    def copy(self, kind, k, order):
        p = self.p
        c = p.ty if order else 1 - p.ty
        number = kind * 4 + order * 2 + k
        j = (1, 3)[k]
        if kind == 0:
            src, dst = self.partial.at[p.x(2) * NY + c, self.half(k)], self.via.at[k, c]
        elif kind == 1:
            src, dst = self.partial.at[p.x(j) * NY + c, self.half(1 - k)], self.got.at[k, c, self.half(1 - k)]
        else:
            src, dst = self.merged.at[k, c], self.got.at[k, c, self.half(k)]
        return pltpu.make_async_remote_copy(
            src_ref=src, dst_ref=dst, send_sem=self.sem[0].at[number], recv_sem=self.sem[1].at[number],
            device_id=p.x_dev(j), device_id_type=MESH)

    def send(self, j):
        for order in range(2):
            if j == 2:
                self.copy(0, 0, order).start()
                self.copy(0, 1, order).start()
            else:
                self.copy(1, (1, 3).index(j), order).start()

    def row(self, step):
        return self.p.x((2 + 3 * step + 3 * (step // 2) + 2 * (step // 3)) % NX)

    def send_after(self, step):
        for number, j in enumerate(self.STEPS):
            pl.when(step == number)(functools.partial(self.send, j))

    def send_all(self):
        for j in self.STEPS:
            self.send(j)
        self.own.start()

    def relay(self):
        p = self.p
        for order in range(2):
            c = p.ty if order else 1 - p.ty
            for k in range(2):
                self.copy(0, k, order).wait_recv()
                block = p.x((1, 3)[k]) * NY + c

                def step(i, carry):
                    rows = pl.ds(pl.multiple_of(i * 32, 32), 32)
                    mine = self.partial[block, pl.ds(pl.multiple_of(k * (ROWS // 2) + i * 32, 32), 32)]
                    self.merged[k, c, rows] = (mine.astype(F32) + self.via[k, c, rows].astype(F32)).astype(BF16)
                    return carry

                lax.fori_loop(0, ROWS // 64, step, 0)
                self.copy(2, k, order).start()

    def total(self, c, rows):
        value = self.got[0, c, rows].astype(F32)
        for k in range(1, 3):
            value = value + self.got[k, c, rows].astype(F32)
        return value

    def wait_near(self, order):
        for k in range(2):
            self.copy(1, k, order).wait_recv()
            self.copy(2, k, order).wait_recv()

    def exchange(self):
        p = self.p
        self.own.wait()
        self.wait_near(0)

        def step(i, carry):
            rows = pl.ds(pl.multiple_of(i * 32, 32), 32)
            self.pair_buf[0, rows] = self.total(1 - p.ty, rows).astype(BF16)
            return carry

        lax.fori_loop(0, ROWS // 32, step, 0)
        self.pair = push(self.pair_buf.at[0], self.pair_buf.at[1], self.sem, 12, p.tensor_pair())

    def arrive(self):
        self.wait_near(1)
        self.pair.wait_recv()

    def rows(self, rows):
        return self.total(self.p.ty, rows) + self.pair_buf[1, rows].astype(F32)

    def finish(self):
        for kind in range(3):
            for order in range(2):
                for k in range(2):
                    self.copy(kind, k, order).wait_send()
        self.pair.wait_send()


class PartGather:
    SEMS = 17

    def __init__(self, p, shard, out, sem, local_sem):
        self.p, self.out, self.sem = p, out, sem
        mine = out.at[:, p.d]
        self.copies = [push(shard, mine, sem, 0, p.y_dev())]
        self.copies += [push(shard, mine, sem, 1 + k, p.z_dev(j)) for k, j in enumerate((1, 3))]
        self.core = [push(shard, mine, sem, 3, p.core_dev())]
        self.halves = []
        self.own = pltpu.make_async_copy(shard, mine, local_sem)
        self.own.start()

    def resend(self, block, number, device):
        return push(block, block, self.sem, number, device)

    def forward(self):
        p = self.p
        self.copies[0].wait_recv()
        block = self.out.at[:, p.d_pair]
        self.copies += [self.resend(block, 4 + k, p.z_dev(j)) for k, j in enumerate((1, 3))]
        self.core.append(self.resend(block, 6, p.core_dev()))

    def index(self, j, pair):
        p = self.p
        return p.dp(1 - p.dy if pair else p.dy, p.z(j), p.dc)

    def spread(self):
        p = self.p
        for pair in range(2):
            for k, (back, on) in enumerate(((3, 1), (1, 3))):
                self.copies[1 + 2 * pair + k].wait_recv()
                index = self.index(back, pair)
                half = self.out.at[:, index, pl.ds(k * (PART // 2), PART // 2)]
                self.halves.append(self.resend(half, 7 + 2 * pair + k, p.z_dev(on)))
                self.core.append(self.resend(self.out.at[:, index], 11 + 2 * pair + k, p.core_dev()))

    def far(self):
        p = self.p
        for copy in self.halves:
            copy.wait_recv()
        self.core += [
            self.resend(self.out.at[:, self.index(2, pair)], 15 + pair, p.core_dev()) for pair in range(2)]

    def finish(self):
        for copy in self.core:
            copy.wait_recv()
        for copy in self.copies + self.halves + self.core:
            copy.wait_send()
        self.own.wait()


class PartScatter:
    @staticmethod
    def scratch(n):
        return [
            pltpu.VMEM((n, 2, NZ, 2, PART, UNITS), BF16),
            pltpu.VMEM((n, 2, NZ, PART, UNITS), BF16),
            pltpu.VMEM((2, n, 2, PART, UNITS), BF16),
            pltpu.VMEM((2, n, 2, PART // 2, UNITS), BF16),
            pltpu.VMEM((2, n, PART, UNITS), BF16),
        ] + sems(8)

    def __init__(self, p, grads, core_buf, z_buf, via, y_buf, send, recv):
        self.p, self.n = p, grads.shape[0]
        self.grads, self.core_buf, self.z_buf, self.via, self.y_buf = grads, core_buf, z_buf, via, y_buf
        self.sem = (send, recv)
        self.core = push(grads.at[:, :, :, 1 - p.dc], core_buf, self.sem, 0, p.core_dev())

    def half(self, k):
        return pl.ds(k * (PART // 2), PART // 2)

    def copy(self, kind, k):
        p = self.p
        j = (1, 3)[k]
        if kind == 0:
            src, dst = self.grads.at[:, :, p.z(2), p.dc, self.half(k)], self.via.at[k]
        else:
            half = self.half(1 - k if kind == 1 else k)
            src, dst = self.grads.at[:, :, p.z(j), p.dc, half], self.z_buf.at[k, :, :, half]
        number = 1 + kind * 2 + k
        return pltpu.make_async_remote_copy(
            src_ref=src, dst_ref=dst, send_sem=self.sem[0].at[number], recv_sem=self.sem[1].at[number],
            device_id=p.z_dev(j), device_id_type=MESH)

    def along(self):
        p = self.p
        self.core.wait_recv()

        def step(i, carry):
            for y in range(2):
                for z in range(NZ):
                    total = self.grads[i, y, z, p.dc].astype(F32) + self.core_buf[i, y, z].astype(F32)
                    self.grads[i, y, z, p.dc] = total.astype(BF16)
            return carry

        lax.fori_loop(0, self.n, step, 0)
        for kind in range(2):
            for k in range(2):
                self.copy(kind, k).start()

    def relay(self):
        p = self.p
        for k, j in enumerate((1, 3)):
            self.copy(0, k).wait_recv()
            z = p.z(j)

            def step(i, carry):
                for y in range(2):
                    total = self.grads[i, y, z, p.dc, self.half(k)].astype(F32) + self.via[k, i, y].astype(F32)
                    self.grads[i, y, z, p.dc, self.half(k)] = total.astype(BF16)
                return carry

            lax.fori_loop(0, self.n, step, 0)
            self.copy(2, k).start()

    def total(self, i, y):
        value = self.grads[i, y, self.p.dz, self.p.dc].astype(F32)
        for k in range(2):
            value = value + self.z_buf[k, i, y].astype(F32)
        return value

    def pair(self):
        p = self.p
        for kind in (1, 2):
            for k in range(2):
                self.copy(kind, k).wait_recv()

        def step(i, carry):
            self.y_buf[0, i] = self.total(i, 1 - p.dy).astype(BF16)
            return carry

        lax.fori_loop(0, self.n, step, 0)
        self.y_copy = push(self.y_buf.at[0], self.y_buf.at[1], self.sem, 7, p.y_dev())

    def finish(self, outs):
        p = self.p
        self.y_copy.wait_recv()
        for i, (out, slot) in enumerate(outs):
            out[slot] = self.total(i, p.dy) + self.y_buf[1, i].astype(F32)
        for copy in [self.core, self.y_copy] + [self.copy(kind, k) for kind in range(3) for k in range(2)]:
            copy.wait_send()


def params(number, megabytes):
    return pltpu.CompilerParams(
        collective_id=number, has_side_effects=True, vmem_limit_bytes=megabytes << 20)


def shape(dims, dtype=BF16):
    return jax.ShapeDtypeStruct(dims, dtype)


def nn(a, b):
    return lax.dot_general(a, b, (((1,), (0,)), ((), ())), preferred_element_type=F32)


def nt(a, b):
    return lax.dot_general(a, b, (((1,), (1,)), ((), ())), preferred_element_type=F32)


def tn(a, b):
    return lax.dot_general(a, b, (((0,), (0,)), ((), ())), preferred_element_type=F32)


def lanes(rows):
    return lax.broadcasted_iota(jnp.int32, (rows, 2 * HEAD_SIZE), 1)


def rotate(pair, cosine, sine):
    first = lanes(pair.shape[0]) % HEAD_SIZE < HEAD_SIZE // 2
    other = jnp.where(first, pltpu.roll(pair, 3 * HEAD_SIZE // 2, 1), pltpu.roll(pair, HEAD_SIZE // 2, 1))
    return pair * cosine + other * sine


def stacked(pair):
    low = lanes(pair.shape[0]) < HEAD_SIZE
    zero = jnp.zeros_like(pair)
    return jnp.concatenate([jnp.where(low, pair, zero), jnp.where(low, zero, pair)], axis=0)


def unstacked(both):
    rows = both.shape[0] // 2
    return jnp.where(lanes(rows) < HEAD_SIZE, both[:rows], both[rows:])


def masked(scores, first_row):
    rows = lax.broadcasted_iota(jnp.int32, scores.shape, 0) % QBLOCK + first_row
    columns = lax.broadcasted_iota(jnp.int32, scores.shape, 1)
    return jnp.where(columns <= rows, scores, NEG_FILL)


def doubled(kv, keys, values):
    low = lanes(kv.shape[0]) < HEAD_SIZE
    kv = kv.astype(F32)
    swapped = pltpu.roll(kv, HEAD_SIZE, 1)
    keys[...] = jnp.where(low, kv, swapped).astype(BF16)
    values[...] = jnp.where(low, swapped, kv).astype(BF16)


def forward_kernel(
    x, small, gate, up, down, out_grad, tables,
    hidden, normed_out, grad_out, gate_out, up_out, down_out, normed, qkv, attended, log_total, small_out, gains,
    x_buf, keys, values, partial, normed_two, *scratch,
):
    p = Place()
    meet(p)
    branch_scratch, scratch = scratch[:7], scratch[7:]
    pairs = [scratch[2 * i : 2 * i + 2] for i in range(7)]
    local = scratch[14]
    smalls = PartGather(p, small, small_out, pairs[0], local.at[0])
    rows_in = TensorGather(p, x, x_buf, pairs[1], local.at[1])
    smalls.forward()
    rows_in.forward()
    gates = PartGather(p, gate, gate_out, pairs[2], local.at[2])
    smalls.spread()
    smalls.far()
    ups = PartGather(p, up, up_out, pairs[3], local.at[3])
    downs = PartGather(p, down, down_out, pairs[5], local.at[5])
    smalls.finish()
    pick = (lax.broadcasted_iota(jnp.int32, (8, 128), 0) == lax.broadcasted_iota(jnp.int32, (8, 128), 1))
    gains[...] = nt(pick.astype(F32).astype(BF16), small_out[0, :, :, 384:].reshape(WIDTH, 128))
    qkv_weight = small_out[0, :, :, :256].reshape(WIDTH, 256)

    def project(i, carry):
        rows = pl.ds(pl.multiple_of(i * ROWS, ROWS), ROWS)
        state = x_buf[i].astype(F32)
        scale = lax.rsqrt(jnp.mean(state * state, axis=-1, keepdims=True) + NORM_EPSILON)
        normed_rows = (state * scale * gains[0:1]).astype(BF16)
        normed[rows] = normed_rows
        pre = nn(normed_rows, qkv_weight)
        qkv[rows, :128] = rotate(pre[:, :128], tables[0, rows], tables[1, rows]).astype(BF16)
        qkv[rows, 128:] = rotate(pre[:, 128:], tables[2, rows], tables[3, rows]).astype(BF16)
        return carry

    rows_in.own.wait()
    lax.fori_loop(p.tx * NY, p.tx * NY + NY, project, 0)
    rows_in.relay()
    grads = TensorGather(p, out_grad, grad_out, pairs[4], local.at[4])
    for j in (1, 3, 2):
        if j == 2:
            gates.forward()
            rows_in.arrive()
        start = p.x(j) * NY
        lax.fori_loop(start, start + NY, project, 0)
    grads.forward()
    ups.forward()
    doubled(qkv[:, 128:], keys, values)
    out_weight = small_out[0, :, :, 256:384].reshape(WIDTH, 128)
    branch = TensorScatter(p, partial, *branch_scratch)
    for b in range(WIDTH // QBLOCK):
        length = (b + 1) * QBLOCK
        rows = pl.ds(b * QBLOCK, QBLOCK)
        scores = masked(nt(stacked(qkv[rows, :128]), keys[:length]) * ATT_SCALE, b * QBLOCK)
        peak = jnp.max(scores, axis=-1, keepdims=True)
        terms = jnp.exp(scores - peak)
        total = jnp.sum(terms, axis=-1, keepdims=True)
        log_total[b] = peak + jnp.log(total)
        out = unstacked(nn((terms / total).astype(BF16), values[:length])).astype(BF16)
        attended[rows] = out
        partial[2 * b : 2 * b + 2] = nt(out, out_weight).astype(BF16).reshape(2, ROWS, WIDTH)
        for j in range(1, NX):
            pl.when(p.x(j) == b)(functools.partial(branch.send, j))
        if b == 0:
            downs.forward()
        if b == 2:
            grads.relay()
    branch.own.start()
    branch.relay()
    gates.spread()
    ups.spread()
    branch.exchange()
    downs.spread()
    branch.arrive()

    def step(i, carry):
        rows = pl.ds(pl.multiple_of(i * 32, 32), 32)
        state = x[rows].astype(F32) + RES_SCALE * branch.rows(rows)
        hidden[rows] = state
        scale = lax.rsqrt(jnp.mean(state * state, axis=-1, keepdims=True) + NORM_EPSILON)
        normed_two[rows] = (state * scale * gains[1:2]).astype(BF16)
        return carry

    lax.fori_loop(0, ROWS // 32, step, 0)
    gather = TensorGather(p, normed_two, normed_out, pairs[6], local.at[6])
    gates.far()
    gather.forward()
    ups.far()
    downs.far()
    gather.relay()
    branch.finish()
    gather.finish()
    rows_in.sent()
    grads.finish()
    gates.finish()
    ups.finish()
    downs.finish()


def forward(x, small, gate, up, down, out_grad, tables):
    full = shape((4, 16, PART, UNITS))
    rows = shape((8, ROWS, WIDTH))
    return pl.pallas_call(
        forward_kernel,
        out_shape=(
            shape((ROWS, WIDTH), F32), rows, rows, full, full, full, shape((WIDTH, WIDTH)), shape((WIDTH, 256)),
            shape((WIDTH, 128)), shape((WIDTH // QBLOCK, 2 * QBLOCK, 1), F32), shape((1, 16, PART, UNITS)),
            shape((8, WIDTH), F32)),
        in_specs=[VMEM, VMEM, ANY, ANY, ANY, ANY, VMEM],
        out_specs=(VMEM,) + (ANY,) * 5 + (VMEM,) * 6,
        scratch_shapes=[
            pltpu.VMEM((8, ROWS, WIDTH), BF16), pltpu.VMEM((WIDTH, 128), BF16), pltpu.VMEM((WIDTH, 128), BF16),
            pltpu.VMEM((8, ROWS, WIDTH), BF16), pltpu.VMEM((ROWS, WIDTH), BF16)]
        + TensorScatter.scratch() + sems(17) + sems(9) + sems(17) + sems(17) + sems(9) + sems(17) + sems(9)
        + [DMA((7,))],
        compiler_params=params(1, 56), name="forward",
    )(x, small, gate, up, down, out_grad, tables)


def norm_pull(state, gain, grad):
    r = lax.rsqrt(jnp.mean(state * state, axis=-1, keepdims=True) + NORM_EPSILON)
    u = state * r
    w = gain * grad
    return r * (w - u * jnp.mean(w * u, axis=-1, keepdims=True)), jnp.sum(grad * u, axis=0, keepdims=True)


def experts_kernel(
    x_in, out_grad_in, gate, up, down, combined, hidden, gains_in, out_grad,
    moe_out, branch_out, state_grad, gain_part, gate_out, up_out, down_out,
    x, out_grad_full, gate_buf, up_buf, down_buf, moe, rows_acc, units, gate_pre, up_pre, rows_out, branch, *scratch,
):
    p = Place()
    load_sem, scratch = scratch[0], scratch[1:]
    sums, scratch = scratch[:7], scratch[7:]
    parts = [scratch[7 * e : 7 * e + 7] for e in range(4)]
    ts, tr, local = scratch[28:]

    def load(e):
        slot = e % 2
        return [
            pltpu.make_async_copy(ref.at[e], buf.at[slot], load_sem.at[slot, k])
            for k, (ref, buf) in enumerate(((gate, gate_buf), (up, up_buf), (down, down_buf)))]

    loads = load(0) + [
        pltpu.make_async_copy(x_in, x, load_sem.at[2, 0]), pltpu.make_async_copy(out_grad_in, out_grad_full, load_sem.at[2, 1])]
    for copy in loads:
        copy.start()
    meet(p)
    gain_part[...] = jnp.zeros_like(gain_part)
    scatters = []
    rows_sum = TensorScatter(p, rows_out, *sums)

    def weigh_expert(e):
        grads = parts[e][0]

        def weigh(i, carry):
            columns = pl.ds(pl.multiple_of(i * 256, 256), 256)
            tokens = x[:, columns]
            found = (
                tn(tokens, gate_pre[...]), tn(tokens, up_pre[...]),
                tn(out_grad_full[:, columns], units[...]) * RES_SCALE)
            for k in range(3):
                for r in range(4):
                    z = (i % 2) * 2 + r // 2
                    grads[k, i // 2, z, r % 2] = found[k][r * PART : r * PART + PART].astype(BF16)
            return carry

        lax.fori_loop(0, 4, weigh, 0)
        scatters.append(PartScatter(p, *parts[e]))

    for e in range(4):
        slot = e % 2
        for copy in loads:
            copy.wait()
        if e < 3:
            loads = load(e + 1)
            for copy in loads:
                copy.start()

        def block(step, carry):
            i = rows_sum.row(step)
            rows = pl.ds(pl.multiple_of(i * QBLOCK, QBLOCK), QBLOCK)
            tokens = x[rows]
            gate_part = nn(tokens, gate_buf[slot])
            up_part = nn(tokens, up_buf[slot])
            sig = 0.5 * jnp.tanh(0.5 * gate_part) + 0.5
            act = gate_part * sig
            scale = combined[rows, e : e + 1]
            unit = (scale * (act * up_part)).astype(BF16)
            grad = nn(out_grad_full[rows], down_buf[slot]) * (RES_SCALE * scale)
            to_gate = (grad * up_part * (sig + act * (1.0 - sig))).astype(BF16)
            to_up = (grad * act).astype(BF16)
            units[rows] = unit
            gate_pre[rows] = to_gate
            up_pre[rows] = to_up
            moe_part = nt(unit, down_buf[slot])
            rows_part = nt(to_gate, gate_buf[slot]) + nt(to_up, up_buf[slot])
            if e == 0:
                moe[rows] = moe_part
                rows_acc[rows] = rows_part
            elif e < 3:
                moe[rows] += moe_part
                rows_acc[rows] += rows_part
            else:
                blocks = pl.ds(2 * i, 2)
                moe_out[blocks] = (moe[rows] + moe_part).astype(BF16).reshape(2, ROWS, WIDTH)
                rows_out[blocks] = (rows_acc[rows] + rows_part).astype(BF16).reshape(2, ROWS, WIDTH)
                rows_sum.send_after(step)
            return carry

        lax.fori_loop(0, WIDTH // QBLOCK, block, 0)
        if e == 3:
            rows_sum.own.start()
            rows_sum.relay()
        if e >= 1:
            scatters[e - 1].along()
        if e == 3:
            scatters[1].pair()
        weigh_expert(e)
        if e == 1 or e == 2:
            scatters[e - 1].relay()
        if e == 2:
            scatters[0].pair()

    scatters[2].relay()
    scatters[3].along()
    rows_sum.exchange()
    scatters[0].finish(((gate_out, 0), (up_out, 0), (down_out, 0)))
    rows_sum.arrive()

    def step(i, carry):
        rows = pl.ds(pl.multiple_of(i * 32, 32), 32)
        pulled, part = norm_pull(hidden[rows], gains_in[1:2], rows_sum.rows(rows))
        gain_part[1:2] += part
        state = out_grad[rows].astype(F32) + pulled
        state_grad[rows] = state
        branch[rows] = (RES_SCALE * state).astype(BF16)
        return carry

    lax.fori_loop(0, ROWS // 32, step, 0)
    gather = TensorGather(p, branch, branch_out, (ts, tr), local.at[0])
    scatters[3].relay()
    gather.forward()
    scatters[2].pair()
    gather.relay()
    scatters[1].finish(((gate_out, 1), (up_out, 1), (down_out, 1)))
    scatters[3].pair()
    scatters[2].finish(((gate_out, 2), (up_out, 2), (down_out, 2)))
    scatters[3].finish(((gate_out, 3), (up_out, 3), (down_out, 3)))
    rows_sum.finish()
    gather.finish()


def run_experts(*args):
    weight = shape((4, PART, UNITS), F32)
    rows = shape((8, ROWS, WIDTH))
    return pl.pallas_call(
        experts_kernel,
        out_shape=(rows, rows, shape((ROWS, WIDTH), F32), shape((8, WIDTH), F32), weight, weight, weight),
        in_specs=[ANY] * 5 + [VMEM] * 4, out_specs=(VMEM, ANY) + (VMEM,) * 5,
        scratch_shapes=[pltpu.VMEM((WIDTH, WIDTH), BF16)] * 2 + [pltpu.VMEM((2, WIDTH, UNITS), BF16)] * 3 + [pltpu.VMEM((WIDTH, WIDTH), F32)] * 2
        + [pltpu.VMEM((WIDTH, UNITS), BF16)] * 3
        + [pltpu.VMEM((8, ROWS, WIDTH), BF16), pltpu.VMEM((ROWS, WIDTH), BF16), DMA((3, 3))]
        + TensorScatter.scratch() + PartScatter.scratch(3) * 4 + sems(9) + [DMA((1,))],
        compiler_params=params(2, 63), name="experts",
    )(*args)


def backward_kernel(
    moe_partial, branch_full, state_grad, gain_part, hidden, gains_in, x, normed_in, qkv, attended, log_total, small,
    tables_in,
    block_out, input_grad, small_out, gains, normed, tables, load_sem,
    keys, values, key_grad, value_grad, pre, partial, gain_buf, *scratch,
):
    p = Place()
    loads = [
        pltpu.make_async_copy(tables_in, tables, load_sem.at[0]), pltpu.make_async_copy(normed_in, normed, load_sem.at[1])]
    for copy in loads:
        copy.start()
    meet(p)
    sums, scratch = scratch[:7], scratch[7:]
    more_sums, scratch = scratch[:7], scratch[7:]
    part = scratch[:7]
    small_grads = part[0]
    gs, gr = scratch[7:]
    moe_sum = TensorScatter(p, moe_partial, *sums)
    moe_sum.send_all()
    doubled(qkv[:, 128:], keys, values)
    key_grad[...] = jnp.zeros_like(key_grad)
    value_grad[...] = jnp.zeros_like(value_grad)
    gains[...] = gain_part[...]

    out_weight = small[0, :, :, 256:384].reshape(WIDTH, 128)
    for copy in loads:
        copy.wait()
    for b in range(WIDTH // QBLOCK):
        if b == 2:
            moe_sum.relay()
        length = (b + 1) * QBLOCK
        rows = pl.ds(b * QBLOCK, QBLOCK)
        grad = stacked(nn(branch_full[2 * b : 2 * b + 2].reshape(QBLOCK, WIDTH), out_weight).astype(BF16))
        query = stacked(qkv[rows, :128])
        scores = masked(nt(query, keys[:length]) * ATT_SCALE, b * QBLOCK)
        probs = jnp.exp(scores - log_total[b])
        value_grad[:length] += tn(probs.astype(BF16), grad)
        weight_grad = nt(grad, values[:length])
        inner = jnp.sum(weight_grad * probs, axis=-1, keepdims=True)
        score_grad = (probs * (weight_grad - inner)).astype(BF16)
        key_grad[:length] += tn(score_grad, query)
        query_grad = unstacked(nn(score_grad, keys[:length])) * ATT_SCALE
        pre[rows, :128] = rotate(query_grad, tables[0, rows], -tables[1, rows]).astype(BF16)
    low = lanes(WIDTH) < HEAD_SIZE
    key_sum = key_grad[...] + pltpu.roll(key_grad[...], HEAD_SIZE, 1)
    value_sum = value_grad[...] + pltpu.roll(value_grad[...], HEAD_SIZE, 1)
    kv_grad = jnp.where(low, key_sum * ATT_SCALE, value_sum)
    pre[:, 128:] = rotate(kv_grad, tables[2], -tables[3]).astype(BF16)

    qkv_weight = small[0, :, :, :256].reshape(WIDTH, 256)

    input_sum = TensorScatter(p, partial, *more_sums)

    def give(step, carry):
        b = input_sum.row(step)
        rows = pl.ds(pl.multiple_of(b * QBLOCK, QBLOCK), QBLOCK)
        found = nt(pre[rows], qkv_weight)
        partial[pl.ds(2 * b, 2)] = found.astype(BF16).reshape(2, ROWS, WIDTH)
        input_sum.send_after(step)
        gains[0:1] += jnp.sum(found * normed[rows].astype(F32), axis=0, keepdims=True)
        return carry

    lax.fori_loop(0, WIDTH // QBLOCK, give, 0)
    input_sum.own.start()
    gains[0:1] = gains[0:1] / gains_in[0:1]

    copies = []
    stages = iter((
        [p.core_dev()], [p.z_dev(j) for j in range(1, NZ)], [p.y_dev()],
        [p.x_dev(j) for j in range(1, NX)], [p.tensor_pair()]))

    def gains_send():
        stage = len(copies)
        first = sum(len(group) for group in copies)
        gain_buf[9 + stage] = gains[...]
        copies.append([
            push(gain_buf.at[9 + stage], gain_buf.at[first + k], (gs, gr), first + k, device)
            for k, device in enumerate(next(stages))])

    def gains_add():
        first = sum(len(group) for group in copies[:-1])
        for k, copy in enumerate(copies[-1]):
            copy.wait_recv()
            gains[...] += gain_buf[first + k]

    gains_send()
    moe_sum.exchange()
    input_sum.relay()

    def weigh(i, carry):
        columns = pl.ds(pl.multiple_of(i * 256, 256), 256)
        of_qkv = tn(normed[:, columns], pre[...]).astype(BF16)
        of_out = tn(branch_full[:, :, columns].reshape(WIDTH, 256), attended[...]).astype(BF16)
        for r in range(4):
            z = (i % 2) * 2 + r // 2
            piece = slice(r * PART, r * PART + PART)
            small_grads[0, i // 2, z, r % 2, :, :256] = of_qkv[piece]
            small_grads[0, i // 2, z, r % 2, :, 256:384] = of_out[piece]
            small_grads[0, i // 2, z, r % 2, :, 384:] = jnp.zeros((PART, 128), BF16)
        return carry

    lax.fori_loop(0, 4, weigh, 0)
    smalls = PartScatter(p, *part)
    gains_add()
    gains_send()
    moe_sum.arrive()

    def give_block(i, carry):
        rows = pl.ds(pl.multiple_of(i * 32, 32), 32)
        block_out[rows] = (hidden[rows] + RES_SCALE * moe_sum.rows(rows)).astype(BF16)
        return carry

    lax.fori_loop(0, ROWS // 32, give_block, 0)
    smalls.along()
    gains_add()
    gains_send()
    smalls.relay()
    input_sum.exchange()
    gains_add()
    gains_send()
    smalls.pair()
    gains_add()
    gains_send()
    input_sum.arrive()

    def last(i, carry):
        rows = pl.ds(pl.multiple_of(i * 32, 32), 32)
        pulled, _ = norm_pull(x[rows].astype(F32), gains_in[0:1], input_sum.rows(rows))
        input_grad[rows] = (state_grad[rows] + pulled).astype(BF16)
        return carry

    lax.fori_loop(0, ROWS // 32, last, 0)
    gains_add()
    smalls.finish(((small_out, 0),))
    moe_sum.finish()
    input_sum.finish()
    for group in copies:
        for copy in group:
            copy.wait_send()


def backward(*args):
    rows = shape((ROWS, WIDTH))
    return pl.pallas_call(
        backward_kernel,
        out_shape=(rows, rows, shape((1, PART, UNITS), F32), shape((8, WIDTH), F32)),
        in_specs=[VMEM] * 7 + [ANY] + [VMEM] * 4 + [ANY], out_specs=(VMEM,) * 4,
        scratch_shapes=[
            pltpu.VMEM((WIDTH, WIDTH), BF16), pltpu.VMEM((4, WIDTH, 128), F32), DMA((2,)),
            pltpu.VMEM((WIDTH, 128), BF16), pltpu.VMEM((WIDTH, 128), BF16),
            pltpu.VMEM((WIDTH, 128), F32), pltpu.VMEM((WIDTH, 128), F32), pltpu.VMEM((WIDTH, 256), BF16),
            pltpu.VMEM((8, ROWS, WIDTH), BF16), pltpu.VMEM((14, 8, WIDTH), F32)]
        + TensorScatter.scratch() * 2 + PartScatter.scratch(1) + sems(9),
        compiler_params=params(3, 56), name="backward",
    )(*args)


def rotary_tables(length):
    half_width = HEAD_SIZE // 2
    positions = np.arange(length).astype(np.float32)
    frequencies = np.power(
        np.float32(ROPE_BASE), -(np.arange(half_width).astype(np.float32) * np.float32(2.0 / HEAD_SIZE)))
    angles = positions[:, None] * frequencies[None, :]
    cosine, sine = np.cos(angles), np.sin(angles)
    cosine = np.concatenate([cosine, cosine], axis=1)
    sine = np.concatenate([-sine, sine], axis=1)
    return np.stack([
        np.concatenate([cosine, cosine], axis=1), np.concatenate([sine, sine], axis=1),
        np.concatenate([cosine, np.ones_like(cosine)], axis=1),
        np.concatenate([sine, np.zeros_like(sine)], axis=1)]).astype(np.float32)


def local(
    inputs, first_gain, query_weight, key_matrix, value_matrix, output_weight, second_gain,
    gate_weight, up_weight, down_weight, expert_ids, gate_values, out_grad,
):
    rank = lax.axis_index("tensor")
    rows = inputs.shape[0] * lax.axis_size("tensor")
    experts = gate_weight.shape[0]
    qw = query_weight.shape[1]
    kw = key_matrix.shape[1]
    tables = jnp.asarray(rotary_tables(rows))

    small = jnp.concatenate(
        [query_weight, key_matrix, value_matrix, output_weight.T, first_gain[:, None], second_gain[:, None],
         jnp.zeros((PART, 126), BF16)], axis=1)
    (hidden, normed_two, out_grad_full, gate_full, up_full, down_full, normed, qkv, attended, log_total, small,
     gains) = forward(inputs, small[None], gate_weight, up_weight, jnp.swapaxes(down_weight, 1, 2), out_grad, tables)
    normed_two = normed_two.reshape(rows, WIDTH)
    out_grad_full = out_grad_full.reshape(rows, WIDTH)
    gate_full = gate_full.reshape(experts, WIDTH, UNITS)
    up_full = up_full.reshape(experts, WIDTH, UNITS)
    down_full = down_full.reshape(experts, WIDTH, UNITS)

    expert_index = rank * experts + jnp.arange(experts, dtype=jnp.int32)
    combined = jnp.sum(
        jnp.where(expert_ids[:, :, None] == expert_index, gate_values[:, :, None], 0.0), axis=1)
    moe_partial, branch_full, state_grad, gain_part, gate_grad, up_grad, down_grad = run_experts(
        normed_two, out_grad_full, gate_full, up_full, down_full, combined, hidden, gains, out_grad)
    block_output, input_grad, small_grad, gains = backward(
        moe_partial, branch_full, state_grad, gain_part, hidden, gains, inputs, normed, qkv, attended, log_total,
        small, tables)
    small_grad = small_grad[0]
    gains = lax.dynamic_slice_in_dim(gains, lax.axis_index("dp") * PART, PART, 1)
    return (
        block_output,
        input_grad,
        gains[0],
        small_grad[:, :qw],
        small_grad[:, qw : qw + kw],
        small_grad[:, qw + kw : qw + 2 * kw],
        small_grad[:, qw + 2 * kw : 2 * qw + 2 * kw].T,
        gains[1],
        gate_grad,
        up_grad,
        jnp.swapaxes(down_grad, 1, 2),
    )


def solution(mesh):
    in_specs = (
        P(("dp", "tensor"), None),
        P("dp"),
        P("dp", "tensor"),
        P("dp", "tensor"),
        P("dp", "tensor"),
        P("tensor", "dp"),
        P("dp"),
        P("tensor", "dp", None),
        P("tensor", "dp", None),
        P("tensor", None, "dp"),
        P("dp", None),
        P("dp", None),
        P(("dp", "tensor"), None),
    )
    out_specs = (
        P(("dp", "tensor"), None),
        P(("dp", "tensor"), None),
        P("dp"),
        P("dp", "tensor"),
        P("dp", "tensor"),
        P("dp", "tensor"),
        P("tensor", "dp"),
        P("dp"),
        P("tensor", "dp", None),
        P("tensor", "dp", None),
        P("tensor", None, "dp"),
    )
    return jax.shard_map(local, mesh=mesh, in_specs=in_specs, out_specs=out_specs, check_vma=False)
```

```python
import functools

import jax
import jax.numpy as jnp
import numpy as np
from jax import lax
from jax.experimental import pallas as pl
from jax.experimental.pallas import tpu as pltpu
from jax.sharding import PartitionSpec as P

HEAD_SIZE = 64
NORM_EPSILON = 1e-06
ATT_SCALE = 0.015625
RES_SCALE = 0.22
ROPE_BASE = 10000.0
NEG_FILL = -1e30
F32 = jnp.float32
BF16 = jnp.bfloat16
MESH = pl.DeviceIdType.MESH
NX, NY, NZ, NCORE = 4, 2, 4, 2
ROWS, WIDTH, PART, UNITS = 128, 1024, 64, 512
QBLOCK = 256
ANY = pl.BlockSpec(memory_space=pl.ANY)
VMEM = pl.BlockSpec(memory_space=pltpu.VMEM)
DMA = pltpu.SemaphoreType.DMA


class Place:
    def __init__(self):
        d, t = lax.axis_index("dp"), lax.axis_index("tensor")
        self.d, self.t = d, t
        self.tx, self.ty = t // NY, t % NY
        self.dy, self.dz, self.dc = d // (NZ * NCORE), (d // NCORE) % NZ, d % NCORE
        self.pair = self.tx * NY + (1 - self.ty)
        self.d_pair = self.dp(1 - self.dy, self.dz, self.dc)

    def dp(self, y, z, core):
        return (y * NZ + z) * NCORE + core

    def tensor_pair(self):
        return (self.d, self.pair)

    def x(self, j):
        return (self.tx + j) % NX

    def x_dev(self, j):
        return (self.d, self.x(j) * NY + self.ty)

    def z(self, j):
        return (self.dz + j) % NZ

    def z_dev(self, j):
        return (self.dp(self.dy, self.z(j), self.dc), self.t)

    def y_dev(self):
        return (self.d_pair, self.t)

    def core_dev(self):
        return (self.dp(self.dy, self.dz, 1 - self.dc), self.t)


def meet(p):
    barrier = pltpu.get_barrier_semaphore()
    others = [p.tensor_pair(), p.y_dev(), p.core_dev()]
    others += [p.x_dev(j) for j in range(1, NX)] + [p.z_dev(j) for j in range(1, NZ)]
    for other in others:
        pl.semaphore_signal(barrier, inc=1, device_id=other, device_id_type=MESH)
    pl.semaphore_wait(barrier, len(others))


def push(src, dst, sems, number, device):
    copy = pltpu.make_async_remote_copy(
        src_ref=src, dst_ref=dst, send_sem=sems[0].at[number], recv_sem=sems[1].at[number],
        device_id=device, device_id_type=MESH)
    copy.start()
    return copy


def sems(number):
    return [DMA((number,)), DMA((number,))]


class TensorGather:
    SEMS = 9

    def __init__(self, p, src, out, sem, local_sem):
        self.p, self.out, self.sem = p, out, sem
        self.copies = [push(src, out.at[p.t], sem, 0, p.tensor_pair())]
        self.copies += [push(src, out.at[p.t], sem, 1 + k, p.x_dev(j)) for k, j in enumerate((1, 3))]
        self.own = pltpu.make_async_copy(src, out.at[p.t], local_sem)
        self.own.start()

    def resend(self, block, number, j):
        self.copies.append(push(block, block, self.sem, number, self.p.x_dev(j)))

    def forward(self):
        self.copies[0].wait_recv()
        for k, j in enumerate((1, 3)):
            self.resend(self.out.at[self.p.pair], 3 + k, j)

    def relay(self):
        p = self.p
        for k, (back, on) in enumerate(((3, 1), (1, 3))):
            for c, first in ((p.ty, 1), (1 - p.ty, 3)):
                self.copies[first + k].wait_recv()
                half = self.out.at[p.x(back) * NY + c, pl.ds(k * (ROWS // 2), ROWS // 2)]
                self.resend(half, 4 + first + k, on)

    def arrive(self):
        for copy in self.copies[5:]:
            copy.wait_recv()

    def sent(self):
        for copy in self.copies:
            copy.wait_send()

    def finish(self):
        self.arrive()
        self.sent()
        self.own.wait()


class TensorScatter:
    STEPS = (2, 1, 3)

    @staticmethod
    def scratch():
        half = pltpu.VMEM((2, NY, ROWS // 2, WIDTH), BF16)
        return [pltpu.VMEM((3, NY, ROWS, WIDTH), BF16), half, half, pltpu.VMEM((2, ROWS, WIDTH), BF16)] + sems(13) + [
            DMA((1,))]

    def __init__(self, p, partial, got, via, merged, pair_buf, send, recv, local):
        self.p, self.partial, self.got, self.pair_buf = p, partial, got, pair_buf
        self.via, self.merged = via, merged
        self.sem = (send, recv)
        self.own = pltpu.make_async_copy(partial.at[pl.ds(p.tx * NY, NY)], got.at[2], local.at[0])

    def half(self, k):
        return pl.ds(k * (ROWS // 2), ROWS // 2)

    def copy(self, kind, k, order):
        p = self.p
        c = p.ty if order else 1 - p.ty
        number = kind * 4 + order * 2 + k
        j = (1, 3)[k]
        if kind == 0:
            src, dst = self.partial.at[p.x(2) * NY + c, self.half(k)], self.via.at[k, c]
        elif kind == 1:
            src, dst = self.partial.at[p.x(j) * NY + c, self.half(1 - k)], self.got.at[k, c, self.half(1 - k)]
        else:
            src, dst = self.merged.at[k, c], self.got.at[k, c, self.half(k)]
        return pltpu.make_async_remote_copy(
            src_ref=src, dst_ref=dst, send_sem=self.sem[0].at[number], recv_sem=self.sem[1].at[number],
            device_id=p.x_dev(j), device_id_type=MESH)

    def send(self, j):
        for order in range(2):
            if j == 2:
                self.copy(0, 0, order).start()
                self.copy(0, 1, order).start()
            else:
                self.copy(1, (1, 3).index(j), order).start()

    def row(self, step):
        return self.p.x((2 + 3 * step + 3 * (step // 2) + 2 * (step // 3)) % NX)

    def send_after(self, step):
        for number, j in enumerate(self.STEPS):
            pl.when(step == number)(functools.partial(self.send, j))

    def send_all(self):
        for j in self.STEPS:
            self.send(j)
        self.own.start()

    def relay(self):
        p = self.p
        for order in range(2):
            c = p.ty if order else 1 - p.ty
            for k in range(2):
                self.copy(0, k, order).wait_recv()
                block = p.x((1, 3)[k]) * NY + c

                def step(i, carry):
                    rows = pl.ds(pl.multiple_of(i * 32, 32), 32)
                    mine = self.partial[block, pl.ds(pl.multiple_of(k * (ROWS // 2) + i * 32, 32), 32)]
                    self.merged[k, c, rows] = (mine.astype(F32) + self.via[k, c, rows].astype(F32)).astype(BF16)
                    return carry

                lax.fori_loop(0, ROWS // 64, step, 0)
                self.copy(2, k, order).start()

    def total(self, c, rows):
        value = self.got[0, c, rows].astype(F32)
        for k in range(1, 3):
            value = value + self.got[k, c, rows].astype(F32)
        return value

    def wait_near(self, order):
        for k in range(2):
            self.copy(1, k, order).wait_recv()
            self.copy(2, k, order).wait_recv()

    def exchange(self):
        p = self.p
        self.own.wait()
        self.wait_near(0)

        def step(i, carry):
            rows = pl.ds(pl.multiple_of(i * 32, 32), 32)
            self.pair_buf[0, rows] = self.total(1 - p.ty, rows).astype(BF16)
            return carry

        lax.fori_loop(0, ROWS // 32, step, 0)
        self.pair = push(self.pair_buf.at[0], self.pair_buf.at[1], self.sem, 12, p.tensor_pair())

    def arrive(self):
        self.wait_near(1)
        self.pair.wait_recv()

    def rows(self, rows):
        return self.total(self.p.ty, rows) + self.pair_buf[1, rows].astype(F32)

    def finish(self):
        for kind in range(3):
            for order in range(2):
                for k in range(2):
                    self.copy(kind, k, order).wait_send()
        self.pair.wait_send()


class PartGather:
    SEMS = 17

    def __init__(self, p, shard, out, sem, local_sem):
        self.p, self.out, self.sem = p, out, sem
        mine = out.at[:, p.d]
        self.copies = [push(shard, mine, sem, 0, p.y_dev())]
        self.copies += [push(shard, mine, sem, 1 + k, p.z_dev(j)) for k, j in enumerate((1, 3))]
        self.core = [push(shard, mine, sem, 3, p.core_dev())]
        self.halves = []
        self.own = pltpu.make_async_copy(shard, mine, local_sem)
        self.own.start()

    def resend(self, block, number, device):
        return push(block, block, self.sem, number, device)

    def forward(self):
        p = self.p
        self.copies[0].wait_recv()
        block = self.out.at[:, p.d_pair]
        self.copies += [self.resend(block, 4 + k, p.z_dev(j)) for k, j in enumerate((1, 3))]
        self.core.append(self.resend(block, 6, p.core_dev()))

    def index(self, j, pair):
        p = self.p
        return p.dp(1 - p.dy if pair else p.dy, p.z(j), p.dc)

    def spread(self):
        p = self.p
        for pair in range(2):
            for k, (back, on) in enumerate(((3, 1), (1, 3))):
                self.copies[1 + 2 * pair + k].wait_recv()
                index = self.index(back, pair)
                half = self.out.at[:, index, pl.ds(k * (PART // 2), PART // 2)]
                self.halves.append(self.resend(half, 7 + 2 * pair + k, p.z_dev(on)))
                self.core.append(self.resend(self.out.at[:, index], 11 + 2 * pair + k, p.core_dev()))

    def far(self):
        p = self.p
        for copy in self.halves:
            copy.wait_recv()
        self.core += [
            self.resend(self.out.at[:, self.index(2, pair)], 15 + pair, p.core_dev()) for pair in range(2)]

    def finish(self):
        for copy in self.core:
            copy.wait_recv()
        for copy in self.copies + self.halves + self.core:
            copy.wait_send()
        self.own.wait()


class PartScatter:
    @staticmethod
    def scratch(n):
        return [
            pltpu.VMEM((n, 2, NZ, 2, PART, UNITS), BF16),
            pltpu.VMEM((n, 2, NZ, PART, UNITS), BF16),
            pltpu.VMEM((2, n, 2, PART, UNITS), BF16),
            pltpu.VMEM((2, n, 2, PART // 2, UNITS), BF16),
            pltpu.VMEM((2, n, PART, UNITS), BF16),
        ] + sems(8)

    def __init__(self, p, grads, core_buf, z_buf, via, y_buf, send, recv):
        self.p, self.n = p, grads.shape[0]
        self.grads, self.core_buf, self.z_buf, self.via, self.y_buf = grads, core_buf, z_buf, via, y_buf
        self.sem = (send, recv)
        self.core = push(grads.at[:, :, :, 1 - p.dc], core_buf, self.sem, 0, p.core_dev())

    def half(self, k):
        return pl.ds(k * (PART // 2), PART // 2)

    def copy(self, kind, k):
        p = self.p
        j = (1, 3)[k]
        if kind == 0:
            src, dst = self.grads.at[:, :, p.z(2), p.dc, self.half(k)], self.via.at[k]
        else:
            half = self.half(1 - k if kind == 1 else k)
            src, dst = self.grads.at[:, :, p.z(j), p.dc, half], self.z_buf.at[k, :, :, half]
        number = 1 + kind * 2 + k
        return pltpu.make_async_remote_copy(
            src_ref=src, dst_ref=dst, send_sem=self.sem[0].at[number], recv_sem=self.sem[1].at[number],
            device_id=p.z_dev(j), device_id_type=MESH)

    def along(self):
        p = self.p
        self.core.wait_recv()

        def step(i, carry):
            for y in range(2):
                for z in range(NZ):
                    total = self.grads[i, y, z, p.dc].astype(F32) + self.core_buf[i, y, z].astype(F32)
                    self.grads[i, y, z, p.dc] = total.astype(BF16)
            return carry

        lax.fori_loop(0, self.n, step, 0)
        for kind in range(2):
            for k in range(2):
                self.copy(kind, k).start()

    def relay(self):
        p = self.p
        for k, j in enumerate((1, 3)):
            self.copy(0, k).wait_recv()
            z = p.z(j)

            def step(i, carry):
                for y in range(2):
                    total = self.grads[i, y, z, p.dc, self.half(k)].astype(F32) + self.via[k, i, y].astype(F32)
                    self.grads[i, y, z, p.dc, self.half(k)] = total.astype(BF16)
                return carry

            lax.fori_loop(0, self.n, step, 0)
            self.copy(2, k).start()

    def total(self, i, y):
        value = self.grads[i, y, self.p.dz, self.p.dc].astype(F32)
        for k in range(2):
            value = value + self.z_buf[k, i, y].astype(F32)
        return value

    def pair(self):
        p = self.p
        for kind in (1, 2):
            for k in range(2):
                self.copy(kind, k).wait_recv()

        def step(i, carry):
            self.y_buf[0, i] = self.total(i, 1 - p.dy).astype(BF16)
            return carry

        lax.fori_loop(0, self.n, step, 0)
        self.y_copy = push(self.y_buf.at[0], self.y_buf.at[1], self.sem, 7, p.y_dev())

    def finish(self, outs):
        p = self.p
        self.y_copy.wait_recv()
        for i, (out, slot) in enumerate(outs):
            out[slot] = self.total(i, p.dy) + self.y_buf[1, i].astype(F32)
        for copy in [self.core, self.y_copy] + [self.copy(kind, k) for kind in range(3) for k in range(2)]:
            copy.wait_send()


def params(number, megabytes):
    return pltpu.CompilerParams(
        collective_id=number, has_side_effects=True, vmem_limit_bytes=megabytes << 20)


def shape(dims, dtype=BF16):
    return jax.ShapeDtypeStruct(dims, dtype)


def nn(a, b):
    return lax.dot_general(a, b, (((1,), (0,)), ((), ())), preferred_element_type=F32)


def nt(a, b):
    return lax.dot_general(a, b, (((1,), (1,)), ((), ())), preferred_element_type=F32)


def tn(a, b):
    return lax.dot_general(a, b, (((0,), (0,)), ((), ())), preferred_element_type=F32)


def lanes(rows):
    return lax.broadcasted_iota(jnp.int32, (rows, 2 * HEAD_SIZE), 1)


def rotate(pair, cosine, sine):
    first = lanes(pair.shape[0]) % HEAD_SIZE < HEAD_SIZE // 2
    other = jnp.where(first, pltpu.roll(pair, 3 * HEAD_SIZE // 2, 1), pltpu.roll(pair, HEAD_SIZE // 2, 1))
    return pair * cosine + other * sine


def stacked(pair):
    low = lanes(pair.shape[0]) < HEAD_SIZE
    zero = jnp.zeros_like(pair)
    return jnp.concatenate([jnp.where(low, pair, zero), jnp.where(low, zero, pair)], axis=0)


def unstacked(both):
    rows = both.shape[0] // 2
    return jnp.where(lanes(rows) < HEAD_SIZE, both[:rows], both[rows:])


def masked(scores, first_row):
    rows = lax.broadcasted_iota(jnp.int32, scores.shape, 0) % QBLOCK + first_row
    columns = lax.broadcasted_iota(jnp.int32, scores.shape, 1)
    return jnp.where(columns <= rows, scores, NEG_FILL)


def doubled(kv, keys, values):
    low = lanes(kv.shape[0]) < HEAD_SIZE
    kv = kv.astype(F32)
    swapped = pltpu.roll(kv, HEAD_SIZE, 1)
    keys[...] = jnp.where(low, kv, swapped).astype(BF16)
    values[...] = jnp.where(low, swapped, kv).astype(BF16)


def forward_kernel(
    x, query, key, value, output, gain_pair, gate, up, down, out_grad, tables,
    hidden, normed_out, grad_out, gate_out, up_out, down_out, normed_hbm, qkv_hbm, attended_hbm, log_total, small_out,
    gains,
    small, normed, qkv, attended, keep_sem, x_buf, keys, values, partial, normed_two, *scratch,
):
    p = Place()
    small[0, :, :128] = query[...]
    small[0, :, 128:256] = jnp.concatenate([key[...], value[...]], axis=1)
    small[0, :, 256:384] = output[...]
    row = lax.broadcasted_iota(jnp.int32, (PART, PART), 0)
    same = row == lax.broadcasted_iota(jnp.int32, (PART, PART), 1)
    gain_lanes = jnp.zeros((PART, 128), F32)
    for k in range(2):
        column = jnp.sum(jnp.where(same, gain_pair[k : k + 1].astype(F32), 0.0), axis=1, keepdims=True)
        gain_lanes = jnp.where(lanes(PART) == k, column, gain_lanes)
    small[0, :, 384:] = gain_lanes.astype(BF16)
    meet(p)
    branch_scratch, scratch = scratch[:7], scratch[7:]
    pairs = [scratch[2 * i : 2 * i + 2] for i in range(7)]
    local = scratch[14]
    smalls = PartGather(p, small, small_out, pairs[0], local.at[0])
    rows_in = TensorGather(p, x, x_buf, pairs[1], local.at[1])
    smalls.forward()
    rows_in.forward()
    gates = PartGather(p, gate, gate_out, pairs[2], local.at[2])
    smalls.spread()
    smalls.far()
    ups = PartGather(p, up, up_out, pairs[3], local.at[3])
    downs = PartGather(p, down, down_out, pairs[5], local.at[5])
    smalls.finish()
    pick = (lax.broadcasted_iota(jnp.int32, (8, 128), 0) == lax.broadcasted_iota(jnp.int32, (8, 128), 1))
    gains[...] = nt(pick.astype(F32).astype(BF16), small_out[0, :, :, 384:].reshape(WIDTH, 128))
    qkv_weight = small_out[0, :, :, :256].reshape(WIDTH, 256)

    def project(i, carry):
        rows = pl.ds(pl.multiple_of(i * ROWS, ROWS), ROWS)
        state = x_buf[i].astype(F32)
        scale = lax.rsqrt(jnp.mean(state * state, axis=-1, keepdims=True) + NORM_EPSILON)
        normed_rows = (state * scale * gains[0:1]).astype(BF16)
        normed[rows] = normed_rows
        pre = nn(normed_rows, qkv_weight)
        qkv[rows, :128] = rotate(pre[:, :128], tables[0, rows], tables[1, rows]).astype(BF16)
        qkv[rows, 128:] = rotate(pre[:, 128:], tables[2, rows], tables[3, rows]).astype(BF16)
        return carry

    rows_in.own.wait()
    lax.fori_loop(p.tx * NY, p.tx * NY + NY, project, 0)
    rows_in.relay()
    grads = TensorGather(p, out_grad, grad_out, pairs[4], local.at[4])
    for j in (1, 3, 2):
        if j == 2:
            gates.forward()
            rows_in.arrive()
        start = p.x(j) * NY
        lax.fori_loop(start, start + NY, project, 0)
    grads.forward()
    ups.forward()
    doubled(qkv[:, 128:], keys, values)
    out_weight = small_out[0, :, :, 256:384].reshape(WIDTH, 128)
    branch = TensorScatter(p, partial, *branch_scratch)
    for b in range(WIDTH // QBLOCK):
        length = (b + 1) * QBLOCK
        rows = pl.ds(b * QBLOCK, QBLOCK)
        scores = masked(nt(stacked(qkv[rows, :128]), keys[:length]) * ATT_SCALE, b * QBLOCK)
        peak = jnp.max(scores, axis=-1, keepdims=True)
        terms = jnp.exp(scores - peak)
        total = jnp.sum(terms, axis=-1, keepdims=True)
        log_total[b] = peak + jnp.log(total)
        out = unstacked(nn((terms / total).astype(BF16), values[:length])).astype(BF16)
        attended[rows] = out
        partial[2 * b : 2 * b + 2] = nt(out, out_weight).astype(BF16).reshape(2, ROWS, WIDTH)
        for j in range(1, NX):
            pl.when(p.x(j) == b)(functools.partial(branch.send, j))
        if b == 0:
            downs.forward()
        if b == 2:
            grads.relay()
    branch.own.start()
    keep = [
        pltpu.make_async_copy(src, dst, keep_sem.at[k])
        for k, (src, dst) in enumerate(((normed, normed_hbm), (qkv, qkv_hbm), (attended, attended_hbm)))]
    for copy in keep:
        copy.start()
    branch.relay()
    gates.spread()
    ups.spread()
    branch.exchange()
    downs.spread()
    branch.arrive()

    def step(i, carry):
        rows = pl.ds(pl.multiple_of(i * 32, 32), 32)
        state = x[rows].astype(F32) + RES_SCALE * branch.rows(rows)
        hidden[rows] = state
        scale = lax.rsqrt(jnp.mean(state * state, axis=-1, keepdims=True) + NORM_EPSILON)
        normed_two[rows] = (state * scale * gains[1:2]).astype(BF16)
        return carry

    lax.fori_loop(0, ROWS // 32, step, 0)
    gather = TensorGather(p, normed_two, normed_out, pairs[6], local.at[6])
    gates.far()
    gather.forward()
    ups.far()
    downs.far()
    gather.relay()
    branch.finish()
    gather.finish()
    rows_in.sent()
    for copy in keep:
        copy.wait()
    grads.finish()
    gates.finish()
    ups.finish()
    downs.finish()


def forward(*args):
    full = shape((4, 16, PART, UNITS))
    rows = shape((8, ROWS, WIDTH))
    return pl.pallas_call(
        forward_kernel,
        out_shape=(
            shape((ROWS, WIDTH), F32), rows, rows, full, full, full, shape((WIDTH, WIDTH)), shape((WIDTH, 256)),
            shape((WIDTH, 128)), shape((WIDTH // QBLOCK, 2 * QBLOCK, 1), F32), shape((1, 16, PART, UNITS)),
            shape((8, WIDTH), F32)),
        in_specs=[VMEM] * 6 + [ANY] * 4 + [VMEM],
        out_specs=(VMEM,) + (ANY,) * 8 + (VMEM,) * 3,
        scratch_shapes=[
            pltpu.VMEM((1, PART, UNITS), BF16), pltpu.VMEM((WIDTH, WIDTH), BF16), pltpu.VMEM((WIDTH, 256), BF16),
            pltpu.VMEM((WIDTH, 128), BF16), DMA((3,)),
            pltpu.VMEM((8, ROWS, WIDTH), BF16), pltpu.VMEM((WIDTH, 128), BF16), pltpu.VMEM((WIDTH, 128), BF16),
            pltpu.VMEM((8, ROWS, WIDTH), BF16), pltpu.VMEM((ROWS, WIDTH), BF16)]
        + TensorScatter.scratch() + sems(17) + sems(9) + sems(17) + sems(17) + sems(9) + sems(17) + sems(9)
        + [DMA((7,))],
        compiler_params=params(1, 56), name="forward",
    )(*args)


def norm_pull(state, gain, grad):
    r = lax.rsqrt(jnp.mean(state * state, axis=-1, keepdims=True) + NORM_EPSILON)
    u = state * r
    w = gain * grad
    return r * (w - u * jnp.mean(w * u, axis=-1, keepdims=True)), jnp.sum(grad * u, axis=0, keepdims=True)


def experts_kernel(
    x_in, out_grad_in, gate, up, down, combined, hidden, gains_in, out_grad,
    moe_out, branch_out, state_grad, gain_part, gate_out, up_out, down_out,
    x, out_grad_full, gate_buf, up_buf, down_buf, moe, rows_acc, units, gate_pre, up_pre, rows_out, branch, *scratch,
):
    p = Place()
    load_sem, scratch = scratch[0], scratch[1:]
    sums, scratch = scratch[:7], scratch[7:]
    parts = [scratch[7 * e : 7 * e + 7] for e in range(4)]
    ts, tr, local = scratch[28:]

    def load(e):
        slot = e % 2
        return [
            pltpu.make_async_copy(ref.at[e], buf.at[slot], load_sem.at[slot, k])
            for k, (ref, buf) in enumerate(((gate, gate_buf), (up, up_buf), (down, down_buf)))]

    loads = load(0) + [
        pltpu.make_async_copy(x_in, x, load_sem.at[2, 0]), pltpu.make_async_copy(out_grad_in, out_grad_full, load_sem.at[2, 1])]
    for copy in loads:
        copy.start()
    meet(p)
    gain_part[...] = jnp.zeros_like(gain_part)
    scatters = []
    rows_sum = TensorScatter(p, rows_out, *sums)

    def weigh_expert(e):
        grads = parts[e][0]

        def weigh(i, carry):
            columns = pl.ds(pl.multiple_of(i * 256, 256), 256)
            tokens = x[:, columns]
            found = (
                tn(tokens, gate_pre[...]), tn(tokens, up_pre[...]),
                tn(out_grad_full[:, columns], units[...]) * RES_SCALE)
            for k in range(3):
                for r in range(4):
                    z = (i % 2) * 2 + r // 2
                    grads[k, i // 2, z, r % 2] = found[k][r * PART : r * PART + PART].astype(BF16)
            return carry

        lax.fori_loop(0, 4, weigh, 0)
        scatters.append(PartScatter(p, *parts[e]))

    for e in range(4):
        slot = e % 2
        for copy in loads:
            copy.wait()
        if e < 3:
            loads = load(e + 1)
            for copy in loads:
                copy.start()

        size = QBLOCK if e == 3 else 2 * QBLOCK

        def block(step, carry):
            i = rows_sum.row(step) if e == 3 else step
            rows = pl.ds(pl.multiple_of(i * size, size), size)
            tokens = x[rows]
            gate_part = nn(tokens, gate_buf[slot])
            up_part = nn(tokens, up_buf[slot])
            sig = 0.5 * jnp.tanh(0.5 * gate_part) + 0.5
            act = gate_part * sig
            scale = combined[rows, e : e + 1]
            unit = (scale * (act * up_part)).astype(BF16)
            grad = nn(out_grad_full[rows], down_buf[slot]) * (RES_SCALE * scale)
            to_gate = (grad * up_part * (sig + act * (1.0 - sig))).astype(BF16)
            to_up = (grad * act).astype(BF16)
            units[rows] = unit
            gate_pre[rows] = to_gate
            up_pre[rows] = to_up
            moe_part = nt(unit, down_buf[slot])
            rows_part = nt(to_gate, gate_buf[slot]) + nt(to_up, up_buf[slot])
            if e == 0:
                moe[rows] = moe_part
                rows_acc[rows] = rows_part
            elif e < 3:
                moe[rows] += moe_part
                rows_acc[rows] += rows_part
            else:
                blocks = pl.ds(2 * i, 2)
                moe_out[blocks] = (moe[rows] + moe_part).astype(BF16).reshape(2, ROWS, WIDTH)
                rows_out[blocks] = (rows_acc[rows] + rows_part).astype(BF16).reshape(2, ROWS, WIDTH)
                rows_sum.send_after(step)
            return carry

        lax.fori_loop(0, WIDTH // size, block, 0)
        if e == 3:
            rows_sum.own.start()
            rows_sum.relay()
        if e >= 1:
            scatters[e - 1].along()
        if e == 3:
            scatters[1].pair()
        weigh_expert(e)
        if e == 1 or e == 2:
            scatters[e - 1].relay()
        if e == 2:
            scatters[0].pair()

    scatters[2].relay()
    scatters[3].along()
    rows_sum.exchange()
    scatters[0].finish(((gate_out, 0), (up_out, 0), (down_out, 0)))
    rows_sum.arrive()

    def step(i, carry):
        rows = pl.ds(pl.multiple_of(i * 32, 32), 32)
        pulled, part = norm_pull(hidden[rows], gains_in[1:2], rows_sum.rows(rows))
        gain_part[1:2] += part
        state = out_grad[rows].astype(F32) + pulled
        state_grad[rows] = state
        branch[rows] = (RES_SCALE * state).astype(BF16)
        return carry

    lax.fori_loop(0, ROWS // 32, step, 0)
    gather = TensorGather(p, branch, branch_out, (ts, tr), local.at[0])
    scatters[3].relay()
    gather.forward()
    scatters[2].pair()
    gather.relay()
    scatters[1].finish(((gate_out, 1), (up_out, 1), (down_out, 1)))
    scatters[3].pair()
    scatters[2].finish(((gate_out, 2), (up_out, 2), (down_out, 2)))
    scatters[3].finish(((gate_out, 3), (up_out, 3), (down_out, 3)))
    rows_sum.finish()
    gather.finish()


def run_experts(*args):
    weight = shape((4, PART, UNITS), F32)
    rows = shape((8, ROWS, WIDTH))
    return pl.pallas_call(
        experts_kernel,
        out_shape=(rows, rows, shape((ROWS, WIDTH), F32), shape((8, WIDTH), F32), weight, weight, weight),
        in_specs=[ANY] * 5 + [VMEM] * 4, out_specs=(VMEM, ANY) + (VMEM,) * 5,
        scratch_shapes=[pltpu.VMEM((WIDTH, WIDTH), BF16)] * 2 + [pltpu.VMEM((2, WIDTH, UNITS), BF16)] * 3 + [pltpu.VMEM((WIDTH, WIDTH), F32)] * 2
        + [pltpu.VMEM((WIDTH, UNITS), BF16)] * 3
        + [pltpu.VMEM((8, ROWS, WIDTH), BF16), pltpu.VMEM((ROWS, WIDTH), BF16), DMA((3, 3))]
        + TensorScatter.scratch() + PartScatter.scratch(3) * 4 + sems(9) + [DMA((1,))],
        compiler_params=params(2, 63), name="experts",
    )(*args)


def backward_kernel(
    moe_partial, branch_full, state_grad, gain_part, hidden, gains_in, x, normed_in, qkv, attended, log_total, small,
    tables_in,
    block_out, input_grad, small_out, gains, normed, tables, load_sem,
    keys, values, key_grad, value_grad, pre, partial, gain_buf, *scratch,
):
    p = Place()
    loads = [
        pltpu.make_async_copy(tables_in, tables, load_sem.at[0]), pltpu.make_async_copy(normed_in, normed, load_sem.at[1])]
    for copy in loads:
        copy.start()
    meet(p)
    sums, scratch = scratch[:7], scratch[7:]
    more_sums, scratch = scratch[:7], scratch[7:]
    part = scratch[:7]
    small_grads = part[0]
    gs, gr = scratch[7:]
    moe_sum = TensorScatter(p, moe_partial, *sums)
    moe_sum.send_all()
    doubled(qkv[:, 128:], keys, values)
    key_grad[...] = jnp.zeros_like(key_grad)
    value_grad[...] = jnp.zeros_like(value_grad)
    gains[...] = gain_part[...]

    out_weight = small[0, :, :, 256:384].reshape(WIDTH, 128)
    for copy in loads:
        copy.wait()
    for b in range(WIDTH // QBLOCK):
        if b == 2:
            moe_sum.relay()
        length = (b + 1) * QBLOCK
        rows = pl.ds(b * QBLOCK, QBLOCK)
        grad = stacked(nn(branch_full[2 * b : 2 * b + 2].reshape(QBLOCK, WIDTH), out_weight).astype(BF16))
        query = stacked(qkv[rows, :128])
        scores = masked(nt(query, keys[:length]) * ATT_SCALE, b * QBLOCK)
        probs = jnp.exp(scores - log_total[b])
        value_grad[:length] += tn(probs.astype(BF16), grad)
        weight_grad = nt(grad, values[:length])
        inner = jnp.sum(weight_grad * probs, axis=-1, keepdims=True)
        score_grad = (probs * (weight_grad - inner)).astype(BF16)
        key_grad[:length] += tn(score_grad, query)
        query_grad = unstacked(nn(score_grad, keys[:length])) * ATT_SCALE
        pre[rows, :128] = rotate(query_grad, tables[0, rows], -tables[1, rows]).astype(BF16)
    low = lanes(WIDTH) < HEAD_SIZE
    key_sum = key_grad[...] + pltpu.roll(key_grad[...], HEAD_SIZE, 1)
    value_sum = value_grad[...] + pltpu.roll(value_grad[...], HEAD_SIZE, 1)
    kv_grad = jnp.where(low, key_sum * ATT_SCALE, value_sum)
    pre[:, 128:] = rotate(kv_grad, tables[2], -tables[3]).astype(BF16)

    qkv_weight = small[0, :, :, :256].reshape(WIDTH, 256)

    input_sum = TensorScatter(p, partial, *more_sums)

    def give(step, carry):
        b = input_sum.row(step)
        rows = pl.ds(pl.multiple_of(b * QBLOCK, QBLOCK), QBLOCK)
        found = nt(pre[rows], qkv_weight)
        partial[pl.ds(2 * b, 2)] = found.astype(BF16).reshape(2, ROWS, WIDTH)
        input_sum.send_after(step)
        gains[0:1] += jnp.sum(found * normed[rows].astype(F32), axis=0, keepdims=True)
        return carry

    lax.fori_loop(0, WIDTH // QBLOCK, give, 0)
    input_sum.own.start()
    gains[0:1] = gains[0:1] / gains_in[0:1]

    copies = []
    stages = iter((
        [p.core_dev()], [p.z_dev(j) for j in range(1, NZ)], [p.y_dev()],
        [p.x_dev(j) for j in range(1, NX)], [p.tensor_pair()]))

    def gains_send():
        stage = len(copies)
        first = sum(len(group) for group in copies)
        gain_buf[9 + stage] = gains[...]
        copies.append([
            push(gain_buf.at[9 + stage], gain_buf.at[first + k], (gs, gr), first + k, device)
            for k, device in enumerate(next(stages))])

    def gains_add():
        first = sum(len(group) for group in copies[:-1])
        for k, copy in enumerate(copies[-1]):
            copy.wait_recv()
            gains[...] += gain_buf[first + k]

    gains_send()
    moe_sum.exchange()
    input_sum.relay()

    def weigh(i, carry):
        columns = pl.ds(pl.multiple_of(i * 256, 256), 256)
        of_qkv = tn(normed[:, columns], pre[...]).astype(BF16)
        of_out = tn(branch_full[:, :, columns].reshape(WIDTH, 256), attended[...]).astype(BF16)
        for r in range(4):
            z = (i % 2) * 2 + r // 2
            piece = slice(r * PART, r * PART + PART)
            small_grads[0, i // 2, z, r % 2, :, :256] = of_qkv[piece]
            small_grads[0, i // 2, z, r % 2, :, 256:384] = of_out[piece]
            small_grads[0, i // 2, z, r % 2, :, 384:] = jnp.zeros((PART, 128), BF16)
        return carry

    lax.fori_loop(0, 4, weigh, 0)
    smalls = PartScatter(p, *part)
    gains_add()
    gains_send()
    moe_sum.arrive()

    def give_block(i, carry):
        rows = pl.ds(pl.multiple_of(i * 32, 32), 32)
        block_out[rows] = (hidden[rows] + RES_SCALE * moe_sum.rows(rows)).astype(BF16)
        return carry

    lax.fori_loop(0, ROWS // 32, give_block, 0)
    smalls.along()
    gains_add()
    gains_send()
    smalls.relay()
    input_sum.exchange()
    gains_add()
    gains_send()
    smalls.pair()
    gains_add()
    gains_send()
    input_sum.arrive()

    def last(i, carry):
        rows = pl.ds(pl.multiple_of(i * 32, 32), 32)
        pulled, _ = norm_pull(x[rows].astype(F32), gains_in[0:1], input_sum.rows(rows))
        input_grad[rows] = (state_grad[rows] + pulled).astype(BF16)
        return carry

    lax.fori_loop(0, ROWS // 32, last, 0)
    gains_add()
    smalls.finish(((small_out, 0),))
    moe_sum.finish()
    input_sum.finish()
    for group in copies:
        for copy in group:
            copy.wait_send()


def backward(*args):
    rows = shape((ROWS, WIDTH))
    return pl.pallas_call(
        backward_kernel,
        out_shape=(rows, rows, shape((1, PART, UNITS), F32), shape((8, WIDTH), F32)),
        in_specs=[VMEM] * 7 + [ANY] + [VMEM] * 4 + [ANY], out_specs=(VMEM,) * 4,
        scratch_shapes=[
            pltpu.VMEM((WIDTH, WIDTH), BF16), pltpu.VMEM((4, WIDTH, 128), F32), DMA((2,)),
            pltpu.VMEM((WIDTH, 128), BF16), pltpu.VMEM((WIDTH, 128), BF16),
            pltpu.VMEM((WIDTH, 128), F32), pltpu.VMEM((WIDTH, 128), F32), pltpu.VMEM((WIDTH, 256), BF16),
            pltpu.VMEM((8, ROWS, WIDTH), BF16), pltpu.VMEM((14, 8, WIDTH), F32)]
        + TensorScatter.scratch() * 2 + PartScatter.scratch(1) + sems(9),
        compiler_params=params(3, 56), name="backward",
    )(*args)


def rotary_tables(length):
    half_width = HEAD_SIZE // 2
    positions = np.arange(length).astype(np.float32)
    frequencies = np.power(
        np.float32(ROPE_BASE), -(np.arange(half_width).astype(np.float32) * np.float32(2.0 / HEAD_SIZE)))
    angles = positions[:, None] * frequencies[None, :]
    cosine, sine = np.cos(angles), np.sin(angles)
    cosine = np.concatenate([cosine, cosine], axis=1)
    sine = np.concatenate([-sine, sine], axis=1)
    return np.stack([
        np.concatenate([cosine, cosine], axis=1), np.concatenate([sine, sine], axis=1),
        np.concatenate([cosine, np.ones_like(cosine)], axis=1),
        np.concatenate([sine, np.zeros_like(sine)], axis=1)]).astype(np.float32)


def local(
    inputs, first_gain, query_weight, key_matrix, value_matrix, output_weight, second_gain,
    gate_weight, up_weight, down_weight, expert_ids, gate_values, out_grad,
):
    rank = lax.axis_index("tensor")
    rows = inputs.shape[0] * lax.axis_size("tensor")
    experts = gate_weight.shape[0]
    qw = query_weight.shape[1]
    kw = key_matrix.shape[1]
    tables = jnp.asarray(rotary_tables(rows))

    (hidden, normed_two, out_grad_full, gate_full, up_full, down_full, normed, qkv, attended, log_total, small,
     gains) = forward(
        inputs, query_weight, key_matrix, value_matrix, output_weight.T, jnp.stack([first_gain, second_gain]),
        gate_weight, up_weight, jnp.swapaxes(down_weight, 1, 2), out_grad, tables)
    normed_two = normed_two.reshape(rows, WIDTH)
    out_grad_full = out_grad_full.reshape(rows, WIDTH)
    gate_full = gate_full.reshape(experts, WIDTH, UNITS)
    up_full = up_full.reshape(experts, WIDTH, UNITS)
    down_full = down_full.reshape(experts, WIDTH, UNITS)

    expert_index = rank * experts + jnp.arange(experts, dtype=jnp.int32)
    combined = jnp.sum(
        jnp.where(expert_ids[:, :, None] == expert_index, gate_values[:, :, None], 0.0), axis=1)
    moe_partial, branch_full, state_grad, gain_part, gate_grad, up_grad, down_grad = run_experts(
        normed_two, out_grad_full, gate_full, up_full, down_full, combined, hidden, gains, out_grad)
    block_output, input_grad, small_grad, gains = backward(
        moe_partial, branch_full, state_grad, gain_part, hidden, gains, inputs, normed, qkv, attended, log_total,
        small, tables)
    small_grad = small_grad[0]
    gains = lax.dynamic_slice_in_dim(gains, lax.axis_index("dp") * PART, PART, 1)
    return (
        block_output,
        input_grad,
        gains[0],
        small_grad[:, :qw],
        small_grad[:, qw : qw + kw],
        small_grad[:, qw + kw : qw + 2 * kw],
        small_grad[:, qw + 2 * kw : 2 * qw + 2 * kw].T,
        gains[1],
        gate_grad,
        up_grad,
        jnp.swapaxes(down_grad, 1, 2),
    )


def solution(mesh):
    in_specs = (
        P(("dp", "tensor"), None),
        P("dp"),
        P("dp", "tensor"),
        P("dp", "tensor"),
        P("dp", "tensor"),
        P("tensor", "dp"),
        P("dp"),
        P("tensor", "dp", None),
        P("tensor", "dp", None),
        P("tensor", None, "dp"),
        P("dp", None),
        P("dp", None),
        P(("dp", "tensor"), None),
    )
    out_specs = (
        P(("dp", "tensor"), None),
        P(("dp", "tensor"), None),
        P("dp"),
        P("dp", "tensor"),
        P("dp", "tensor"),
        P("dp", "tensor"),
        P("tensor", "dp"),
        P("dp"),
        P("tensor", "dp", None),
        P("tensor", "dp", None),
        P("tensor", None, "dp"),
    )
    return jax.shard_map(local, mesh=mesh, in_specs=in_specs, out_specs=out_specs, check_vma=False)
```
